32 devices in a mesh: dp: 8 (over y, x, core), fsdp: 4 (over z).
Axes of the slice: x: 2, y: 2, z: 4, core: 2. Of those that a mesh axis runs over, the one named last changes fastest.
Arguments:
- tokens: bfloat16 [32768, 1024], P(('dp', 'fsdp')), may hold values from -6 to 6
- out_grad: bfloat16 [32768, 1024], P(('dp', 'fsdp')), may hold values from -6 to 6
- domain_ids: int32 [32768], P(('dp', 'fsdp')), may hold values from 0 to 15
- domain_scale: float32 [16], replicated, may hold values from 0.5 to 2
- attn_in: float32 [1024, 1536], P(('dp', 'fsdp')), may hold values from -0.1875 to 0.1875
- latent_expand_weight: float32 [512, 1024], P(('dp', 'fsdp')), may hold values from -0.375 to 0.375
- attn_out: float32 [1024, 1024], P(('dp', 'fsdp')), may hold values from -1.5 to 1.5
- gate_up: float32 [1024, 5632], P(('dp', 'fsdp')), may hold values from -0.1875 to 0.1875
- down_proj: float32 [2816, 1024], P(('dp', 'fsdp')), may hold values from -0.109375 to 0.109375
- norm_gains: float32 [2, 1024], P(None, ('dp', 'fsdp')), may hold values from 0.4 to 3.5
- attn_in_first: float32 [1024, 1536], P(('dp', 'fsdp')), may hold values from -0.00018310547 to 0.00018310547
- attn_in_second: float32 [1024, 1536], P(('dp', 'fsdp')), may hold values from 4.492086e-09 to 1.779883e-08
- latent_up_first: float32 [512, 1024], P(('dp', 'fsdp')), may hold values from -0.00018310547 to 0.00018310547
- latent_up_second: float32 [512, 1024], P(('dp', 'fsdp')), may hold values from 4.492086e-09 to 1.779883e-08
- attn_out_first: float32 [1024, 1024], P(('dp', 'fsdp')), may hold values from -6.1035156e-05 to 6.1035156e-05
- attn_out_second: float32 [1024, 1024], P(('dp', 'fsdp')), may hold values from 2.54269e-10 to 1.017076e-09
- gate_up_first: float32 [1024, 5632], P(('dp', 'fsdp')), may hold values from -0.00018310547 to 0.00018310547
- gate_up_second: float32 [1024, 5632], P(('dp', 'fsdp')), may hold values from 4.492086e-09 to 1.779883e-08
- down_proj_first: float32 [2816, 1024], P(('dp', 'fsdp')), may hold values from -0.00018310547 to 0.00018310547
- down_proj_second: float32 [2816, 1024], P(('dp', 'fsdp')), may hold values from 4.492086e-09 to 1.779883e-08
- gains_first: float32 [2, 1024], P(None, ('dp', 'fsdp')), may hold values from -0.00048828125 to 0.00048828125
- gains_second: float32 [2, 1024], P(None, ('dp', 'fsdp')), may hold values from 2.5426901e-08 to 1.01707606e-07
Outputs:
- mixed: bfloat16 [32768, 1024], P(('dp', 'fsdp'))
- input_grad: bfloat16 [32768, 1024], P(('dp', 'fsdp'))
- grad_norm: float32 [], replicated
- attn_in_new: float32 [1024, 1536], P(('dp', 'fsdp'))
- attn_in_first_new: float32 [1024, 1536], P(('dp', 'fsdp'))
- attn_in_second_new: float32 [1024, 1536], P(('dp', 'fsdp'))
- latent_up_new: float32 [512, 1024], P(('dp', 'fsdp'))
- latent_up_first_new: float32 [512, 1024], P(('dp', 'fsdp'))
- latent_up_second_new: float32 [512, 1024], P(('dp', 'fsdp'))
- attn_out_new: float32 [1024, 1024], P(('dp', 'fsdp'))
- attn_out_first_new: float32 [1024, 1024], P(('dp', 'fsdp'))
- attn_out_second_new: float32 [1024, 1024], P(('dp', 'fsdp'))
- gate_up_new: float32 [1024, 5632], P(('dp', 'fsdp'))
- gate_up_first_new: float32 [1024, 5632], P(('dp', 'fsdp'))
- gate_up_second_new: float32 [1024, 5632], P(('dp', 'fsdp'))
- down_proj_new: float32 [2816, 1024], P(('dp', 'fsdp'))
- down_proj_first_new: float32 [2816, 1024], P(('dp', 'fsdp'))
- down_proj_second_new: float32 [2816, 1024], P(('dp', 'fsdp'))
- norm_gains_new: float32 [2, 1024], P(None, ('dp', 'fsdp'))
- gains_first_new: float32 [2, 1024], P(None, ('dp', 'fsdp'))
- gains_second_new: float32 [2, 1024], P(None, ('dp', 'fsdp'))
The draws below stay inside these ranges and needn't reach their ends.
All inputs are finite; a program needn't handle non-finite values.
Results may differ from the reference program's by a relative error of at most 0.017.
The reference program's roundings to bfloat16 on the way count: a program that leaves them out, or rounds other values in their place, can miss the bound.
Values may be sent and summed in bfloat16 or wider, within the bound.
No kernel may reach another device: no remote copies, remote signals or barrier semaphores. Data moves between devices by JAX's collectives and lax.ppermute only.
A program may use at most 320 MiB of HBM per device.

```python
import math
import jax
import jax.numpy as jnp
from jax import lax

D = 1024
HQ = 16
HD = 64
LATENT_HEADS = 2
LATENT_WIDTH = 256
FF = 2816
TOK_DEV = 1024
NDOM = 16
STEP = 10
ROPE = 32
SHARDS = 32
INNER = 4
TOKENS = 32768
PARAMS = 11798528


def draw_norm_gains(key, part):
    key = jax.random.fold_in(key, 7)
    index = jnp.arange(D)
    shard = index // (D // SHARDS)
    outer = (shard // INNER).astype(jnp.float32) / max(SHARDS // INNER - 1, 1)
    inner = (shard % INNER).astype(jnp.float32) / max(INNER - 1, 1)
    rise = 1.73
    noise = jax.random.uniform(key, (2, D), jnp.float32, -0.15, 0.15)
    base = 0.6 * rise ** outer * rise ** inner
    return (base[None, :] * (1.0 + noise)).astype(jnp.float32)


def place_ends(array, key, low, high):
    extent = array.shape
    spot = [jax.random.randint(jax.random.fold_in(key, axis), (), 0, extent[axis]) for axis in range(len(extent))]
    array = array.at[tuple(spot)].set(low)
    longest = extent.index(max(extent))
    spot[longest] = (spot[longest] + 1) % extent[longest]
    return array.at[tuple(spot)].set(high)


def block_levels(stream_key, dims, split, smallest, largest):
    def one(dim, parts):
        steps = jax.random.uniform(jax.random.fold_in(jax.random.fold_in(stream_key, 6), dim), (parts,), jnp.float32, smallest / len(split), largest / len(split))
        return jnp.repeat(jnp.exp(steps), dims[dim] // parts).reshape((-1,) + (1,) * (len(dims) - dim - 1))

    level = one(*split[0])
    for cut in split[1:]:
        level = level * one(*cut)
    return level


def centred(own_key, shape, deviation, limit, pieces=(), kind=jnp.bfloat16):
    entries = jax.random.normal(own_key, shape, jnp.float32) * deviation
    if len(pieces) > 0:
        entries = block_levels(own_key, shape, pieces, -0.22, 0.18) * entries
    return jnp.clip(entries, min=-limit, max=limit).astype(kind)


def setup_inputs(seed: int = 0) -> dict:
    key_list = jax.random.split(jax.random.key(seed), 23)
    return {
        "tokens": centred(key_list[0], (TOKENS, D), 1.0, 6.0, ((0, 32),)),
        "out_grad": centred(key_list[1], (TOKENS, D), 1.0, 6.0, ((0, 32),)),
        "domain_ids": place_ends(jax.random.randint(key_list[2], (TOKENS,), 0, NDOM), jax.random.fold_in(key_list[2], 1), 0, NDOM - 1).astype(jnp.int32),
        "domain_scale": jnp.clip(jnp.exp(jax.random.uniform(key_list[3], (NDOM,), jnp.float32, math.log(0.5), math.log(2.0))), 0.5, 2.0),
        "attn_in": centred(key_list[4], (D, HQ * HD + LATENT_HEADS * LATENT_WIDTH), D ** -0.5, 0.1875, ((0, 32),), jnp.float32),
        "latent_expand_weight": centred(key_list[5], (LATENT_HEADS * LATENT_WIDTH, 2 * HQ * HD // LATENT_HEADS), LATENT_WIDTH ** -0.5, 0.375, ((0, 32),), jnp.float32),
        "attn_out": centred(key_list[6], (HQ * HD, D), (HQ * HD // 64) ** -0.5, 1.5, ((0, 32),), jnp.float32),
        "gate_up": centred(key_list[7], (D, 2 * FF), D ** -0.5, 0.1875, ((0, 32),), jnp.float32),
        "down_proj": centred(key_list[8], (FF, D), FF ** -0.5, 0.109375, ((0, 32),), jnp.float32),
        "norm_gains": draw_norm_gains(jax.random.fold_in(key_list[22], 71), 0),
        "attn_in_first": centred(key_list[10], (D, HQ * HD + LATENT_HEADS * LATENT_WIDTH), (0.11 / PARAMS ** 0.5), 0.00018310547, ((0, 32),), jnp.float32),
        "attn_in_second": jnp.clip(jnp.exp(math.log(1.779883085362144e-08) - 1.37681563 * jax.random.uniform(key_list[11], (D, HQ * HD + LATENT_HEADS * LATENT_WIDTH), jnp.float32) ** block_levels(key_list[11], (D, HQ * HD + LATENT_HEADS * LATENT_WIDTH), ((0, 32),), -0.2, 0.2)), 4.492085814433722e-09, 1.779883085362144e-08),
        "latent_up_first": centred(key_list[12], (LATENT_HEADS * LATENT_WIDTH, 2 * HQ * HD // LATENT_HEADS), (0.11 / PARAMS ** 0.5), 0.00018310547, ((0, 32),), jnp.float32),
        "latent_up_second": jnp.clip(jnp.exp(math.log(1.779883085362144e-08) - 1.37681563 * jax.random.uniform(key_list[13], (LATENT_HEADS * LATENT_WIDTH, 2 * HQ * HD // LATENT_HEADS), jnp.float32) ** block_levels(key_list[13], (LATENT_HEADS * LATENT_WIDTH, 2 * HQ * HD // LATENT_HEADS), ((0, 32),), -0.2, 0.2)), 4.492085814433722e-09, 1.779883085362144e-08),
        "attn_out_first": centred(key_list[14], (HQ * HD, D), (0.035 / PARAMS ** 0.5), 6.103515625e-05, ((0, 32),), jnp.float32),
        "attn_out_second": jnp.clip(jnp.exp(math.log(1.0170759789929207e-09) - 1.3862944 * jax.random.uniform(key_list[15], (HQ * HD, D), jnp.float32) ** block_levels(key_list[15], (HQ * HD, D), ((0, 32),), -0.2, 0.2)), 2.5426899474823017e-10, 1.0170759789929207e-09),
        "gate_up_first": centred(key_list[16], (D, 2 * FF), (0.11 / PARAMS ** 0.5), 0.00018310547, ((0, 32),), jnp.float32),
        "gate_up_second": jnp.clip(jnp.exp(math.log(1.779883085362144e-08) - 1.37681563 * jax.random.uniform(key_list[17], (D, 2 * FF), jnp.float32) ** block_levels(key_list[17], (D, 2 * FF), ((0, 32),), -0.2, 0.2)), 4.492085814433722e-09, 1.779883085362144e-08),
        "down_proj_first": centred(key_list[18], (FF, D), (0.11 / PARAMS ** 0.5), 0.00018310547, ((0, 32),), jnp.float32),
        "down_proj_second": jnp.clip(jnp.exp(math.log(1.779883085362144e-08) - 1.37681563 * jax.random.uniform(key_list[19], (FF, D), jnp.float32) ** block_levels(key_list[19], (FF, D), ((0, 32),), -0.2, 0.2)), 4.492085814433722e-09, 1.779883085362144e-08),
        "gains_first": centred(key_list[20], (2, D), (0.3 / PARAMS ** 0.5), 0.00048828125, ((1, 32),), jnp.float32),
        "gains_second": jnp.clip(jnp.exp(math.log(1.0170760589289785e-07) - 1.3862944 * jax.random.uniform(key_list[21], (2, D), jnp.float32) ** block_levels(key_list[21], (2, D), ((1, 32),), -0.2, 0.2)), 2.542690147322446e-08, 1.0170760589289785e-07),
    }


MAX_NORM = 1.0
BETA_ONE = 0.9
BETA_TWO = 0.95
RATE_MATRIX = 0.02
RATE_OUTPUT = 0.2
RATE_GAIN = 1.0
DECAY_MATRIX = 0.1
EPSILON_ADAM = 1e-08
EPSILON_NORM = 1e-06
ROPE_BASE = 10000.0
HIGHER_PRECISION = lax.Precision.HIGHEST

@jax.custom_vjp
def low(v):
    return lax.optimization_barrier(v.astype(jnp.bfloat16)).astype(jnp.float32)

@jax.custom_vjp
def low_back(v):
    return v

def low_keep(v):
    return (low(v), None)

def low_pass(kept, grad):
    return (grad,)

def back_keep(v):
    return (v, None)

def back_low(kept, grad):
    return (low(grad),)
low.defvjp(low_keep, low_pass)
low_back.defvjp(back_keep, back_low)

def product(left, right):
    return jnp.dot(left, right, precision=HIGHER_PRECISION, preferred_element_type=jnp.float32)

def normed(values, gain):
    return values * lax.rsqrt(lax.optimization_barrier(jnp.mean(values * values, axis=-1, keepdims=True)) + EPSILON_NORM) * gain

def angles(length):
    half = ROPE // 2
    freqs = ROPE_BASE ** (-jnp.arange(half).astype(jnp.float32) / half)
    theta = jnp.arange(length).astype(jnp.float32)[:, None] * freqs[None, :]
    return (jnp.cos(theta)[:, None, :], jnp.sin(theta)[:, None, :])

def rotate(values, cosine, sine):
    half = ROPE // 2
    first = values[..., :half]
    second = values[..., half:ROPE]
    return jnp.concatenate([first * cosine - second * sine, first * sine + second * cosine, values[..., ROPE:]], axis=-1)

def layer(inputs, weights):
    attn_in, latent_expand_weight, attn_out, gate_up, down_proj, norm_gains = [low(w) for w in weights]
    length = inputs.shape[0]
    query_group_width = HQ // LATENT_HEADS * HD
    query_width = HQ * HD
    first_act = low(normed(inputs, norm_gains[0]))
    joined = low_back(product(first_act, attn_in))
    query_pre = joined[:, :query_width].reshape(length, HQ, HD)
    latent_state = low(joined[:, query_width:]).reshape(length, LATENT_HEADS, LATENT_WIDTH)
    key_value_rows = low_back(jnp.einsum('nph,phy->npy', latent_state, latent_expand_weight.reshape(LATENT_HEADS, LATENT_WIDTH, 2 * query_group_width), precision=HIGHER_PRECISION))
    key_pre = key_value_rows[..., :query_group_width].reshape(length, HQ, HD)
    values = low(key_value_rows[..., query_group_width:].reshape(length, HQ, HD))
    cosine, sine = angles(length)
    query = low(rotate(query_pre, cosine, sine))
    keys = low(rotate(key_pre, cosine, sine))
    scores = low_back(jnp.einsum('qhd,khd->hqk', query, keys, precision=HIGHER_PRECISION)) * HD ** (-0.5)
    where = jnp.arange(length)
    allowed = where[:, None] >= where[None, :]
    scores = jnp.where(allowed[None], scores, -1e+30)
    probs = low(jax.nn.softmax(scores, axis=-1))
    attended = low(low_back(jnp.einsum('hqk,khd->qhd', probs, values, precision=HIGHER_PRECISION))).reshape(length, query_width)
    hidden_state = inputs + low_back(product(attended, attn_out))
    second_act = low(normed(hidden_state, norm_gains[1]))
    gate_both = low_back(product(second_act, gate_up))
    hidden = low(jax.nn.silu(gate_both[:, :FF]) * gate_both[:, FF:])
    return hidden_state + low_back(product(hidden, down_proj))

def adamw(master, grad, first, second, rate, decay):
    first_new = BETA_ONE * first + (1.0 - BETA_ONE) * grad
    second_new = BETA_TWO * second + (1.0 - BETA_TWO) * grad * grad
    first_hat = first_new / (1.0 - BETA_ONE ** STEP)
    second_hat = second_new / (1.0 - BETA_TWO ** STEP)
    master_new = master - rate * (first_hat / (jnp.sqrt(second_hat) + EPSILON_ADAM) + decay * master)
    return (master_new, first_new, second_new)

def reference(tokens, out_grad, domain_ids, domain_scale, attn_in, latent_expand_weight, attn_out, gate_up, down_proj, norm_gains, attn_in_first, attn_in_second, latent_up_first, latent_up_second, attn_out_first, attn_out_second, gate_up_first, gate_up_second, down_proj_first, down_proj_second, gains_first, gains_second):
    masters = (attn_in, latent_expand_weight, attn_out, gate_up, down_proj, norm_gains)
    firsts = (attn_in_first, latent_up_first, attn_out_first, gate_up_first, down_proj_first, gains_first)
    seconds = (attn_in_second, latent_up_second, attn_out_second, gate_up_second, down_proj_second, gains_second)
    inputs = tokens.astype(jnp.float32).reshape(-1, TOK_DEV, D)

    def forward(stack, *weights):
        step_fn = jax.checkpoint(lambda one_seq: layer(one_seq, weights))
        return lax.map(step_fn, stack)
    mixed, pull = jax.vjp(forward, inputs, *masters)
    factor = domain_scale[domain_ids]
    cotangent = (out_grad.astype(jnp.float32) * factor[:, None]).reshape(inputs.shape)
    grads = pull(cotangent)
    input_grad = grads[0].reshape(-1, D).astype(jnp.bfloat16)
    weight_grads = grads[1:]
    squares = jnp.float32(0.0)
    for grad in weight_grads:
        squares = squares + jnp.sum(grad * grad)
    grad_norm = jnp.sqrt(squares)
    clip = jnp.minimum(1.0, MAX_NORM / (grad_norm + 1e-06))
    results = []
    for index in range(6):
        if index == 5:
            rate, decay = (RATE_GAIN, 0.0)
        elif index == 2:
            rate, decay = (RATE_OUTPUT, DECAY_MATRIX)
        else:
            rate, decay = (RATE_MATRIX, DECAY_MATRIX)
        results.extend(adamw(masters[index], clip * weight_grads[index], firsts[index], seconds[index], rate, decay))
    return (mixed.reshape(-1, D).astype(jnp.bfloat16), input_grad, grad_norm, results[0], results[1], results[2], results[3], results[4], results[5], results[6], results[7], results[8], results[9], results[10], results[11], results[12], results[13], results[14], results[15], results[16], results[17])
```

```python
import jax
import jax.numpy as jnp
from jax import lax
from jax.experimental import pallas as pl
from jax.experimental.pallas import tpu as pltpu
from jax.sharding import PartitionSpec as P

HQ = 16
HD = 64
LATENT_HEADS = 2
LATENT_WIDTH = 256
FF = 2816
NDOM = 16
STEP = 10
ROPE = 32
QUERY_WIDTH = HQ * HD
GROUP_WIDTH = QUERY_WIDTH // LATENT_HEADS
LANES = 128
PAIRS = QUERY_WIDTH // LANES
PAIRS_PER_LATENT = PAIRS // LATENT_HEADS

MAX_NORM = 1.0
BETA_ONE = 0.9
BETA_TWO = 0.95
RATE_MATRIX = 0.02
RATE_OUTPUT = 0.2
RATE_GAIN = 1.0
DECAY_MATRIX = 0.1
EPSILON_ADAM = 1e-08
EPSILON_NORM = 1e-06
ROPE_BASE = 10000.0

AXES = ("dp", "fsdp")
BF = jnp.bfloat16
F32 = jnp.float32
LOG2E = 1.4426950408889634
SCALE = HD**-0.5
NN = (((1,), (0,)), ((), ()))
NT = (((1,), (1,)), ((), ()))
TN = (((0,), (0,)), ((), ()))
MIB = 1 << 20


def dot(left, right, dims):
    return lax.dot_general(left, right, dims, preferred_element_type=F32)


def resident(*shape):
    return pl.BlockSpec(shape, lambda *step: (0,) * len(shape), pipeline_mode=pl.Buffered(1))


def rotation_tables(length):
    half = ROPE // 2
    freqs = ROPE_BASE ** (-jnp.arange(half).astype(F32) / half)
    theta = jnp.arange(length).astype(F32)[:, None] * freqs[None, :]
    cosine, sine = jnp.cos(theta), jnp.sin(theta)
    zero = jnp.zeros((length, half), F32)
    rest = jnp.zeros((length, HD - ROPE), F32)
    own = jnp.concatenate([cosine, cosine, rest + 1.0], axis=1)
    ahead = jnp.concatenate([-sine, zero, rest], axis=1)
    behind = jnp.concatenate([zero, sine, rest], axis=1)
    return tuple(jnp.concatenate([t, t], axis=1) for t in (own, ahead, behind))


def rotate(values, own, ahead, behind):
    half = ROPE // 2
    return (
        values * own
        + pltpu.roll(values, LANES - half, 1) * ahead
        + pltpu.roll(values, half, 1) * behind
    )


def unrotate(values, own, ahead, behind):
    half = ROPE // 2
    return (
        values * own
        - pltpu.roll(values, LANES - half, 1) * ahead
        - pltpu.roll(values, half, 1) * behind
    )


def project_kernel(x_ref, gain_ref, win_ref, wup_ref, own_ref, ahead_ref, behind_ref,
                   a1_ref, q_ref, k_ref, v_ref, c_ref):
    tables = (own_ref[...], ahead_ref[...], behind_ref[...])
    x = x_ref[...].astype(F32)
    inverse = lax.rsqrt(jnp.mean(x * x, axis=1, keepdims=True) + EPSILON_NORM)
    a1 = (x * inverse * gain_ref[...].astype(F32)).astype(BF)
    a1_ref[...] = a1
    joined = dot(a1, win_ref[...], NN)
    for pair in range(PAIRS):
        lanes = slice(pair * LANES, (pair + 1) * LANES)
        q_ref[:, lanes] = rotate(joined[:, lanes], *tables).astype(BF)
    c = joined[:, QUERY_WIDTH:].astype(BF)
    c_ref[...] = c
    for head in range(LATENT_HEADS):
        latent = slice(head * LATENT_WIDTH, (head + 1) * LATENT_WIDTH)
        both = dot(c[:, latent], wup_ref[latent, :], NN)
        for pair in range(PAIRS_PER_LATENT):
            lanes = slice(pair * LANES, (pair + 1) * LANES)
            out = slice(head * GROUP_WIDTH + pair * LANES, head * GROUP_WIDTH + (pair + 1) * LANES)
            k_ref[:, out] = rotate(both[:, lanes], *tables).astype(BF)
        out = slice(head * GROUP_WIDTH, (head + 1) * GROUP_WIDTH)
        v_ref[:, out] = both[:, GROUP_WIDTH:].astype(BF)


def project(x, gain, w_in, w_up, tables):
    length, width = x.shape
    tile = min(256, length)
    latents = LATENT_HEADS * LATENT_WIDTH
    rows = lambda columns: pl.BlockSpec((tile, columns), lambda i: (i, 0))
    shape = lambda columns: jax.ShapeDtypeStruct((length, columns), BF)
    return pl.pallas_call(
        project_kernel,
        grid=(length // tile,),
        in_specs=[rows(width), resident(1, width), resident(*w_in.shape), resident(*w_up.shape)]
        + [rows(LANES)] * 3,
        out_specs=[rows(width), rows(QUERY_WIDTH), rows(QUERY_WIDTH), rows(QUERY_WIDTH), rows(latents)],
        out_shape=[shape(width), shape(QUERY_WIDTH), shape(QUERY_WIDTH), shape(QUERY_WIDTH), shape(latents)],
        compiler_params=pltpu.CompilerParams(vmem_limit_bytes=48 * MIB),
        cost_estimate=pl.CostEstimate(
            flops=2 * length * (w_in.size + w_up.size), bytes_accessed=16 * MIB, transcendentals=0
        ),
        name="project",
    )(x, gain, w_in, w_up, *tables)


def halves(pair, axis):
    first = lax.broadcasted_iota(jnp.int32, pair.shape, axis) < HD
    zero = jnp.zeros_like(pair)
    return (jnp.where(first, pair, zero), jnp.where(first, zero, pair))


def not_after(block):
    keys = lax.broadcasted_iota(jnp.int32, (block, block), 0)
    queries = lax.broadcasted_iota(jnp.int32, (block, block), 1)
    return keys <= queries


def attention_kernel(q_ref, k_ref, v_ref, o_ref, log_ref):
    length = q_ref.shape[0]
    block = min(256, length)
    values = halves(v_ref[...].T, 0)
    for start in range(0, length, block):
        stop = start + block
        queries = halves(q_ref[start:stop, :], 1)
        probs = []
        for head in range(2):
            scores = dot(k_ref[:stop, :], queries[head], NT) * (SCALE * LOG2E)
            last = jnp.where(not_after(block), scores[start:, :], -1e30)
            scores = jnp.concatenate([scores[:start, :], last], axis=0) if start else last
            peak = jnp.max(scores, axis=0, keepdims=True)
            expo = jnp.exp2(scores - peak)
            total = jnp.sum(expo, axis=0, keepdims=True)
            log_ref[0, head : head + 1, start:stop] = peak + jnp.log2(total)
            probs.append((expo * (1.0 / total)).astype(BF))
        mixed = dot(values[0][:, :stop], probs[0], NN) + dot(values[1][:, :stop], probs[1], NN)
        o_ref[start:stop, :] = mixed.T.astype(BF)


def attention(q, k, v):
    length, width = q.shape
    spec = pl.BlockSpec((length, LANES), lambda i: (0, i))
    logs = pl.BlockSpec((1, 2, length), lambda i: (i, 0, 0))
    return pl.pallas_call(
        attention_kernel,
        grid=(PAIRS,),
        in_specs=[spec] * 3,
        out_specs=[spec, logs],
        out_shape=[
            jax.ShapeDtypeStruct((length, width), BF),
            jax.ShapeDtypeStruct((PAIRS, 2, length), F32),
        ],
        compiler_params=pltpu.CompilerParams(vmem_limit_bytes=48 * MIB),
        cost_estimate=pl.CostEstimate(
            flops=PAIRS * 8 * LANES * length * length,
            bytes_accessed=8 * length * width,
            transcendentals=PAIRS * length * length,
        ),
        name="attention",
    )(q, k, v)


def attention_back_kernel(q_ref, k_ref, v_ref, o_ref, do_ref, log_ref, own_ref, ahead_ref, behind_ref,
                          dq_ref, dk_ref, dv_ref, total_ref):
    length = q_ref.shape[0]
    block = min(256, length)
    tables = lambda rows: (own_ref[rows, :], ahead_ref[rows, :], behind_ref[rows, :])
    product = (do_ref[...].astype(F32) * o_ref[...].astype(F32)).T
    deltas = (
        jnp.sum(product[:HD], axis=0, keepdims=True),
        jnp.sum(product[HD:], axis=0, keepdims=True),
    )
    keys = halves(k_ref[...].T, 0)
    for start in range(0, length, block):
        stop = start + block
        queries = halves(q_ref[start:, :], 1)
        grads = halves(do_ref[start:, :], 1)
        dk = dv = dq = None
        for head in range(2):
            scores = dot(k_ref[start:stop, :], queries[head], NT) * (SCALE * LOG2E)
            probs = jnp.exp2(scores - log_ref[0, head : head + 1, start:])
            first = jnp.where(not_after(block), probs[:, :block], 0.0)
            probs = jnp.concatenate([first, probs[:, block:]], axis=1) if stop < length else first
            dprobs = dot(v_ref[start:stop, :], grads[head], NT)
            dscores = (probs * (dprobs - deltas[head][:, start:])).astype(BF)
            parts = (
                dot(probs.astype(BF), grads[head], NN),
                dot(dscores, queries[head], NN),
                dot(keys[head][:, start:stop], dscores, NN),
            )
            dv = parts[0] if dv is None else dv + parts[0]
            dk = parts[1] if dk is None else dk + parts[1]
            dq = parts[2] if dq is None else dq + parts[2]
        dv_ref[start:stop, :] = dv.astype(BF)
        dk_ref[start:stop, :] = unrotate(dk * SCALE, *tables(slice(start, stop))).astype(BF)
        if start == 0:
            total_ref[...] = dq
        else:
            total_ref[:, start:] += dq
    dq_ref[...] = unrotate(total_ref[...].T * SCALE, *tables(slice(None))).astype(BF)


def attention_back(q, k, v, o, do, logs, tables):
    length, width = q.shape
    spec = pl.BlockSpec((length, LANES), lambda i: (0, i))
    return pl.pallas_call(
        attention_back_kernel,
        grid=(PAIRS,),
        in_specs=[spec] * 5 + [pl.BlockSpec((1, 2, length), lambda i: (i, 0, 0))] + [resident(length, LANES)] * 3,
        out_specs=[spec] * 3,
        out_shape=[jax.ShapeDtypeStruct((length, width), BF)] * 3,
        scratch_shapes=[pltpu.VMEM((LANES, length), F32)],
        compiler_params=pltpu.CompilerParams(vmem_limit_bytes=48 * MIB),
        cost_estimate=pl.CostEstimate(
            flops=PAIRS * 20 * LANES * length * length,
            bytes_accessed=16 * length * width,
            transcendentals=PAIRS * length * length,
        ),
        name="attention_back",
    )(q, k, v, o, do, logs, *tables)


def feed_forward_kernel(x_ref, o_ref, og_ref, factor_ref, gain_ref, wout_ref, wg_ref, wu_ref, wd_ref,
                        mixed_ref, dh_ref, do_ref, gout_ref, gg_ref, gu_ref, gd_ref, dgain_ref,
                        h_ref, acc_ref, da2_ref, a2_ref, a2t_ref, dyb_ref, hid_ref, dgu_ref):
    step = pl.program_id(0)
    last = pl.num_programs(0) - 1
    length, width = x_ref.shape
    chunk = wg_ref.shape[1]
    tile = min(256, length)
    gain = gain_ref[...].astype(F32)

    @pl.when(step == 0)
    def _():
        for m in range(0, length, tile):
            rows = pl.ds(m, tile)
            h = x_ref[rows, :].astype(F32) + dot(o_ref[rows, :], wout_ref[...], NN)
            h_ref[rows, :] = h
            acc_ref[rows, :] = h
            inverse = lax.rsqrt(jnp.mean(h * h, axis=1, keepdims=True) + EPSILON_NORM)
            a2 = (h * inverse * gain).astype(BF)
            a2_ref[rows, :] = a2
            a2t_ref[:, rows] = a2.T
            dyb_ref[rows, :] = (og_ref[rows, :].astype(F32) * factor_ref[rows, :]).astype(BF)
            da2_ref[rows, :] = jnp.zeros((tile, width), F32)

    for m in range(0, length, tile):
        rows = pl.ds(m, tile)
        gate = dot(a2_ref[rows, :], wg_ref[...], NN)
        up = dot(a2_ref[rows, :], wu_ref[...], NN)
        dhid = dot(dyb_ref[rows, :], wd_ref[...], NT)
        sig = 1.0 / (1.0 + jnp.exp2(gate * -LOG2E))
        act = gate * sig
        hid_ref[rows, :] = (act * up).astype(BF)
        dgu_ref[rows, :chunk] = (dhid * up * (sig + act * (1.0 - sig))).astype(BF)
        dgu_ref[rows, chunk:] = (dhid * act).astype(BF)
    for m in range(0, length, tile):
        rows = pl.ds(m, tile)
        acc_ref[rows, :] += dot(hid_ref[rows, :], wd_ref[...], NN)
        da2_ref[rows, :] += dot(dgu_ref[rows, :chunk], wg_ref[...], NT) + dot(
            dgu_ref[rows, chunk:], wu_ref[...], NT
        )
    gd_ref[...] = dot(hid_ref[...], dyb_ref[...], TN).astype(BF)
    gg_ref[...] = dot(a2t_ref[...], dgu_ref[:, :chunk], NN).astype(BF)
    gu_ref[...] = dot(a2t_ref[...], dgu_ref[:, chunk:], NN).astype(BF)

    @pl.when(step == last)
    def _():
        total = jnp.zeros((1, width), F32)
        for m in range(0, length, tile):
            rows = pl.ds(m, tile)
            mixed_ref[rows, :] = acc_ref[rows, :].astype(BF)
            h = h_ref[rows, :]
            inverse = lax.rsqrt(jnp.mean(h * h, axis=1, keepdims=True) + EPSILON_NORM)
            hat = h * inverse
            da2 = da2_ref[rows, :]
            total = total + jnp.sum(da2 * hat, axis=0, keepdims=True)
            scaled = da2 * gain
            dy = og_ref[rows, :].astype(F32) * factor_ref[rows, :]
            dh = dy + inverse * (scaled - hat * jnp.mean(scaled * hat, axis=1, keepdims=True))
            dh_ref[rows, :] = dh
            low = dh.astype(BF)
            dyb_ref[rows, :] = low
            do_ref[rows, :] = dot(low, wout_ref[...], NT).astype(BF)
        dgain_ref[...] = total
        gout_ref[...] = dot(o_ref[...], dyb_ref[...], TN).astype(BF)


def feed_forward(x, o, out_grad, factor, gain, w_out, w_gate, w_down):
    length, width = x.shape
    chunk = 256
    steps = FF // chunk
    grid = lambda block, index: pl.BlockSpec(block, index)
    columns = lambda shift: pl.BlockSpec((width, chunk), lambda i: (0, i + shift))
    rows = pl.BlockSpec((chunk, width), lambda i: (i, 0))
    shape = jax.ShapeDtypeStruct
    return pl.pallas_call(
        feed_forward_kernel,
        grid=(steps,),
        in_specs=[
            resident(length, width),
            resident(length, QUERY_WIDTH),
            resident(length, width),
            resident(length, 1),
            resident(1, width),
            resident(QUERY_WIDTH, width),
            columns(0),
            columns(steps),
            rows,
        ],
        out_specs=[
            resident(length, width),
            resident(length, width),
            resident(length, QUERY_WIDTH),
            resident(QUERY_WIDTH, width),
            columns(0),
            columns(0),
            rows,
            resident(1, width),
        ],
        out_shape=[
            shape((length, width), BF),
            shape((length, width), F32),
            shape((length, QUERY_WIDTH), BF),
            shape((QUERY_WIDTH, width), BF),
            shape((width, FF), BF),
            shape((width, FF), BF),
            shape((FF, width), BF),
            shape((1, width), F32),
        ],
        scratch_shapes=[
            pltpu.VMEM((length, width), F32),
            pltpu.VMEM((length, width), F32),
            pltpu.VMEM((length, width), F32),
            pltpu.VMEM((length, width), BF),
            pltpu.VMEM((width, length), BF),
            pltpu.VMEM((length, width), BF),
            pltpu.VMEM((length, chunk), BF),
            pltpu.VMEM((length, 2 * chunk), BF),
        ],
        compiler_params=pltpu.CompilerParams(vmem_limit_bytes=58 * MIB),
        cost_estimate=pl.CostEstimate(
            flops=2 * length * width * (9 * FF + 3 * QUERY_WIDTH),
            bytes_accessed=60 * MIB,
            transcendentals=length * FF,
        ),
        name="feed_forward",
    )(x, o, out_grad, factor, gain, w_out, w_gate, w_gate, w_down)


def unproject_kernel(a1_ref, c_ref, dq_ref, dk_ref, dv_ref, wup_ref, dc_ref, ginq_ref, ginc_ref, gup_ref, a1t_ref):
    head = pl.program_id(0)

    @pl.when(head == 0)
    def _():
        a1t_ref[...] = a1_ref[...].T

    dc = (
        dot(dk_ref[...], wup_ref[:, :GROUP_WIDTH], NT) + dot(dv_ref[...], wup_ref[:, GROUP_WIDTH:], NT)
    ).astype(BF)
    dc_ref[...] = dc
    latent = c_ref[...].T
    gup_ref[:, :GROUP_WIDTH] = dot(latent, dk_ref[...], NN).astype(BF)
    gup_ref[:, GROUP_WIDTH:] = dot(latent, dv_ref[...], NN).astype(BF)
    ginc_ref[...] = dot(a1t_ref[...], dc, NN).astype(BF)
    ginq_ref[...] = dot(a1t_ref[...], dq_ref[...], NN).astype(BF)


def unproject(a1, c, dq, dk, dv, w_up):
    length, width = a1.shape
    group = pl.BlockSpec((length, GROUP_WIDTH), lambda g: (0, g))
    latent = pl.BlockSpec((length, LATENT_WIDTH), lambda g: (0, g))
    up = pl.BlockSpec((LATENT_WIDTH, 2 * GROUP_WIDTH), lambda g: (g, 0))
    shape = jax.ShapeDtypeStruct
    latents = LATENT_HEADS * LATENT_WIDTH
    return pl.pallas_call(
        unproject_kernel,
        grid=(LATENT_HEADS,),
        in_specs=[resident(length, width), latent, group, group, group, up],
        out_specs=[
            latent,
            pl.BlockSpec((width, GROUP_WIDTH), lambda g: (0, g)),
            pl.BlockSpec((width, LATENT_WIDTH), lambda g: (0, g)),
            up,
        ],
        out_shape=[
            shape((length, latents), BF),
            shape((width, QUERY_WIDTH), BF),
            shape((width, latents), BF),
            shape((latents, 2 * GROUP_WIDTH), BF),
        ],
        scratch_shapes=[pltpu.VMEM((width, length), BF)],
        compiler_params=pltpu.CompilerParams(vmem_limit_bytes=56 * MIB),
        cost_estimate=pl.CostEstimate(
            flops=2 * length * (width * (QUERY_WIDTH + latents) + 4 * latents * GROUP_WIDTH),
            bytes_accessed=16 * MIB,
            transcendentals=0,
        ),
        name="unproject",
    )(a1, c, dq, dk, dv, w_up)


def input_grad_kernel(x_ref, dh_ref, dq_ref, dc_ref, gain_ref, win_ref, out_ref, dgain_ref):
    x = x_ref[...].astype(F32)
    inverse = lax.rsqrt(jnp.mean(x * x, axis=1, keepdims=True) + EPSILON_NORM)
    hat = x * inverse
    da1 = dot(dq_ref[...], win_ref[:, :QUERY_WIDTH], NT) + dot(dc_ref[...], win_ref[:, QUERY_WIDTH:], NT)
    part = jnp.sum(da1 * hat, axis=0, keepdims=True)
    scaled = da1 * gain_ref[...].astype(F32)
    out_ref[...] = (
        dh_ref[...] + inverse * (scaled - hat * jnp.mean(scaled * hat, axis=1, keepdims=True))
    ).astype(BF)

    @pl.when(pl.program_id(0) == 0)
    def _():
        dgain_ref[...] = part

    @pl.when(pl.program_id(0) > 0)
    def _():
        dgain_ref[...] += part


def input_grad(x, dh, dq, dc, gain, w_in):
    length, width = x.shape
    tile = min(256, length)
    rows = lambda columns: pl.BlockSpec((tile, columns), lambda i: (i, 0))
    return pl.pallas_call(
        input_grad_kernel,
        grid=(length // tile,),
        in_specs=[rows(width), rows(width), rows(QUERY_WIDTH), rows(dc.shape[1]), resident(1, width), resident(*w_in.shape)],
        out_specs=[rows(width), resident(1, width)],
        out_shape=[jax.ShapeDtypeStruct((length, width), BF), jax.ShapeDtypeStruct((1, width), F32)],
        compiler_params=pltpu.CompilerParams(vmem_limit_bytes=48 * MIB),
        cost_estimate=pl.CostEstimate(flops=2 * length * w_in.size, bytes_accessed=16 * MIB, transcendentals=0),
        name="input_grad",
    )(x, dh, dq, dc, gain, w_in)


class Ring:
    def __init__(self, data, line):
        self.cores = 2 if data % 2 == 0 else 1
        self.plane, self.line = data // self.cores, line
        place = lax.axis_index("dp")
        self.core, self.at, self.z = place % self.cores, place // self.cores, lax.axis_index("fsdp")

    def partner(self, index, shift, count):
        if count & (count - 1) == 0:
            return index ^ shift
        return (index + shift) % count

    def send_core(self, value):
        swap = [(i, i ^ 1) for i in range(self.plane * 2)]
        return lax.ppermute(value, "dp", swap)

    def send_plane(self, value, shift):
        pairs = [
            (p * self.cores + c, self.partner(p, shift, self.plane) * self.cores + c)
            for p in range(self.plane)
            for c in range(self.cores)
        ]
        return lax.ppermute(value, "dp", pairs)

    def send_line(self, value, shift):
        return lax.ppermute(value, "fsdp", [(i, (i + shift) % self.line) for i in range(self.line)])


def take(array, index, axis):
    return lax.dynamic_index_in_dim(array, index, axis, keepdims=False)


def sum_core(ring, grad):
    columns = grad.shape[1]
    rows = grad.shape[0] // (ring.plane * ring.cores * ring.line)
    grad = grad.reshape(ring.plane, ring.cores, ring.line, rows, columns)
    if ring.cores == 1:
        return grad[:, 0]
    received = ring.send_core(take(grad, 1 - ring.core, 1))
    return (take(grad, ring.core, 1).astype(F32) + received.astype(F32)).astype(BF)


def sum_plane(ring, grad):
    total = take(grad, ring.at, 0).astype(F32)
    for shift in range(1, ring.plane):
        total += ring.send_plane(take(grad, ring.partner(ring.at, shift, ring.plane), 0), shift).astype(F32)
    return total


def sum_line(ring, grad, axis):
    total = take(grad, ring.z, axis).astype(F32)
    for shift in range(1, ring.line):
        total += ring.send_line(take(grad, (ring.z + shift) % ring.line, axis), shift).astype(F32)
    return total


def plane_first(ring, grad):
    return sum_line(ring, sum_plane(ring, sum_core(ring, grad)).astype(BF), 0)


def line_first(ring, grad):
    return sum_plane(ring, sum_line(ring, sum_core(ring, grad), 1).astype(BF))


def sum_all(ring, value):
    if ring.cores == 2:
        value = value + ring.send_core(value)
    for count, send in ((ring.plane, ring.send_plane), (ring.line, None)):
        if count & (count - 1):
            return lax.psum(value, AXES)
    shift = 1
    while shift < ring.plane:
        value = value + ring.send_plane(value, shift)
        shift *= 2
    shift = 1
    while shift < ring.line:
        swap = [(i, i ^ shift) for i in range(ring.line)]
        value = value + lax.ppermute(value, "fsdp", swap)
        shift *= 2
    return value


def adamw(master, grad, first, second, rate, decay):
    first_new = BETA_ONE * first + (1.0 - BETA_ONE) * grad
    second_new = BETA_TWO * second + (1.0 - BETA_TWO) * grad * grad
    first_hat = first_new / (1.0 - BETA_ONE**STEP)
    second_hat = second_new / (1.0 - BETA_TWO**STEP)
    master_new = master - rate * (
        first_hat / (jnp.sqrt(second_hat) + EPSILON_ADAM) + decay * master
    )
    return (master_new, first_new, second_new)


def gather(piece, axis=0):
    return lax.all_gather(piece, AXES, axis=axis, tiled=True)


def shards(data, line, tokens, out_grad, domain_ids, domain_scale, *state):
    masters, moments = state[:6], state[6:]
    firsts, seconds = moments[0::2], moments[1::2]
    ring = Ring(data, line)
    length, width = tokens.shape
    lowered = tuple(w.astype(BF) for w in masters)
    w_in = gather(lowered[0])
    gains = gather(lowered[5], 1)
    w_up = gather(lowered[1])
    w_out = gather(lowered[2])
    w_gate = gather(lowered[3])
    w_down = gather(lowered[4])
    tables = rotation_tables(length)
    factor = jnp.sum(
        jnp.where(domain_ids[:, None] == jnp.arange(NDOM)[None, :], domain_scale[None, :], 0.0),
        axis=1,
        keepdims=True,
    )
    a1, q, k, v, c = project(tokens, gains[:1], w_in, w_up, tables)
    o, logs = attention(q, k, v)
    mixed, dh, do, g_out, g_gate, g_upper, g_down, dgain_two = feed_forward(
        tokens, o, out_grad, factor, gains[1:], w_out, w_gate, w_down
    )
    sum_down = line_first(ring, g_down)
    sum_gate = plane_first(ring, g_gate)
    sum_upper = plane_first(ring, g_upper)
    sum_out = line_first(ring, g_out)
    dq, dk, dv = attention_back(q, k, v, o, do, logs, tables)
    dc, g_query, g_latent_in, g_up = unproject(a1, c, dq, dk, dv, w_up)
    sum_query = plane_first(ring, g_query)
    sum_latent_in = plane_first(ring, g_latent_in)
    sum_up = line_first(ring, g_up)
    given, dgain_one = input_grad(tokens, dh, dq, dc, gains[:1], w_in)
    owned = [
        jnp.concatenate([sum_query, sum_latent_in], axis=1),
        sum_up,
        sum_out,
        jnp.concatenate([sum_gate, sum_upper], axis=1),
        sum_down,
    ]
    squares = sum(jnp.sum(grad * grad) for grad in owned)
    dgains = jnp.concatenate([dgain_one, dgain_two], axis=0)
    message = jnp.concatenate(
        [dgains.reshape(-1, LANES), jnp.full((8, LANES), squares, F32)], axis=0
    )
    message = sum_all(ring, message)
    dgains = message[:-8].reshape(2, width)
    grad_norm = jnp.sqrt(message[-1, 0] + jnp.sum(dgains * dgains))
    clip = jnp.minimum(1.0, MAX_NORM / (grad_norm + 1e-06))
    share = masters[5].shape[1]
    place = lax.axis_index("dp") * line + lax.axis_index("fsdp")
    owned.append(lax.dynamic_slice_in_dim(dgains, place * share, share, 1))
    results = []
    for index in range(6):
        if index == 5:
            rate, decay = (RATE_GAIN, 0.0)
        elif index == 2:
            rate, decay = (RATE_OUTPUT, DECAY_MATRIX)
        else:
            rate, decay = (RATE_MATRIX, DECAY_MATRIX)
        results.extend(
            adamw(masters[index], clip * owned[index], firsts[index], seconds[index], rate, decay)
        )
    return (mixed, given, grad_norm, *results)


def solution(mesh):
    data, line = mesh.shape["dp"], mesh.shape["fsdp"]
    rows, flat, columns = P(AXES, None), P(AXES), P(None, AXES)

    def run(*arrays):
        return shards(data, line, *arrays)

    return jax.shard_map(
        run,
        mesh=mesh,
        in_specs=(rows, rows, flat, P()) + (rows,) * 5 + (columns,) + (rows,) * 10 + (columns,) * 2,
        out_specs=(rows, rows, P()) + (rows,) * 15 + (columns,) * 3,
        check_vma=False,
    )
```

```python
import functools

import jax
import jax.numpy as jnp
from jax import lax
from jax.experimental import pallas as pl
from jax.experimental.pallas import tpu as pltpu
from jax.sharding import PartitionSpec as P

HQ = 16
HD = 64
LATENT_HEADS = 2
LATENT_WIDTH = 256
FF = 2816
NDOM = 16
STEP = 10
ROPE = 32
QUERY_WIDTH = HQ * HD
GROUP_WIDTH = QUERY_WIDTH // LATENT_HEADS
LANES = 128
PAIRS = QUERY_WIDTH // LANES
PAIRS_PER_LATENT = PAIRS // LATENT_HEADS

MAX_NORM = 1.0
BETA_ONE = 0.9
BETA_TWO = 0.95
RATE_MATRIX = 0.02
RATE_OUTPUT = 0.2
RATE_GAIN = 1.0
DECAY_MATRIX = 0.1
EPSILON_ADAM = 1e-08
EPSILON_NORM = 1e-06
ROPE_BASE = 10000.0

AXES = ("dp", "fsdp")
BF = jnp.bfloat16
F32 = jnp.float32
LOG2E = 1.4426950408889634
SCALE = HD**-0.5
NN = (((1,), (0,)), ((), ()))
NT = (((1,), (1,)), ((), ()))
TN = (((0,), (0,)), ((), ()))
MIB = 1 << 20
CHUNK = 256
TILE = 2 * CHUNK


def dot(left, right, dims):
    return lax.dot_general(left, right, dims, preferred_element_type=F32)


def resident(*shape):
    return pl.BlockSpec(shape, lambda *step: (0,) * len(shape), pipeline_mode=pl.Buffered(1))


def rotation_tables(length):
    half = ROPE // 2
    freqs = ROPE_BASE ** (-jnp.arange(half).astype(F32) / half)
    theta = jnp.arange(length).astype(F32)[:, None] * freqs[None, :]
    cosine, sine = jnp.cos(theta), jnp.sin(theta)
    zero = jnp.zeros((length, half), F32)
    rest = jnp.zeros((length, HD - ROPE), F32)
    own = jnp.concatenate([cosine, cosine, rest + 1.0], axis=1)
    ahead = jnp.concatenate([-sine, zero, rest], axis=1)
    behind = jnp.concatenate([zero, sine, rest], axis=1)
    return tuple(jnp.concatenate([t, t], axis=1) for t in (own, ahead, behind))


def rotate(values, own, ahead, behind):
    half = ROPE // 2
    return (
        values * own
        + pltpu.roll(values, LANES - half, 1) * ahead
        + pltpu.roll(values, half, 1) * behind
    )


def unrotate(values, own, ahead, behind):
    half = ROPE // 2
    return (
        values * own
        - pltpu.roll(values, LANES - half, 1) * ahead
        - pltpu.roll(values, half, 1) * behind
    )


def project_kernel(x_ref, gain_ref, win_ref, wup_ref, own_ref, ahead_ref, behind_ref,
                   a1_ref, q_ref, k_ref, v_ref, c_ref):
    tables = (own_ref[...], ahead_ref[...], behind_ref[...])
    x = x_ref[...].astype(F32)
    inverse = lax.rsqrt(jnp.mean(x * x, axis=1, keepdims=True) + EPSILON_NORM)
    a1 = (x * inverse * gain_ref[...].astype(F32)).astype(BF)
    a1_ref[...] = a1
    joined = dot(a1, win_ref[...], NN)
    for pair in range(PAIRS):
        lanes = slice(pair * LANES, (pair + 1) * LANES)
        q_ref[:, lanes] = rotate(joined[:, lanes], *tables).astype(BF)
    c = joined[:, QUERY_WIDTH:].astype(BF)
    c_ref[...] = c
    for head in range(LATENT_HEADS):
        latent = slice(head * LATENT_WIDTH, (head + 1) * LATENT_WIDTH)
        both = dot(c[:, latent], wup_ref[latent, :], NN)
        for pair in range(PAIRS_PER_LATENT):
            lanes = slice(pair * LANES, (pair + 1) * LANES)
            out = slice(head * GROUP_WIDTH + pair * LANES, head * GROUP_WIDTH + (pair + 1) * LANES)
            k_ref[:, out] = rotate(both[:, lanes], *tables).astype(BF)
        out = slice(head * GROUP_WIDTH, (head + 1) * GROUP_WIDTH)
        v_ref[:, out] = both[:, GROUP_WIDTH:].astype(BF)


def project(x, gain, w_in, w_up, tables):
    length, width = x.shape
    tile = min(256, length)
    latents = LATENT_HEADS * LATENT_WIDTH
    rows = lambda columns: pl.BlockSpec((tile, columns), lambda i: (i, 0))
    shape = lambda columns: jax.ShapeDtypeStruct((length, columns), BF)
    return pl.pallas_call(
        project_kernel,
        grid=(length // tile,),
        in_specs=[rows(width), resident(1, width), resident(*w_in.shape), resident(*w_up.shape)]
        + [rows(LANES)] * 3,
        out_specs=[rows(width), rows(QUERY_WIDTH), rows(QUERY_WIDTH), rows(QUERY_WIDTH), rows(latents)],
        out_shape=[shape(width), shape(QUERY_WIDTH), shape(QUERY_WIDTH), shape(QUERY_WIDTH), shape(latents)],
        compiler_params=pltpu.CompilerParams(vmem_limit_bytes=48 * MIB),
        cost_estimate=pl.CostEstimate(
            flops=2 * length * (w_in.size + w_up.size), bytes_accessed=16 * MIB, transcendentals=0
        ),
        name="project",
    )(x, gain, w_in, w_up, *tables)


def halves(pair, axis):
    first = lax.broadcasted_iota(jnp.int32, pair.shape, axis) < HD
    zero = jnp.zeros_like(pair)
    return (jnp.where(first, pair, zero), jnp.where(first, zero, pair))


def not_after(block):
    keys = lax.broadcasted_iota(jnp.int32, (block, block), 0)
    queries = lax.broadcasted_iota(jnp.int32, (block, block), 1)
    return keys <= queries


def attention_kernel(q_ref, k_ref, v_ref, o_ref, log_ref):
    length = q_ref.shape[0]
    block = min(256, length)
    values = halves(v_ref[...].T, 0)
    for start in range(0, length, block):
        stop = start + block
        queries = halves(q_ref[start:stop, :], 1)
        probs = []
        for head in range(2):
            scores = dot(k_ref[:stop, :], queries[head], NT) * (SCALE * LOG2E)
            last = jnp.where(not_after(block), scores[start:, :], -1e30)
            scores = jnp.concatenate([scores[:start, :], last], axis=0) if start else last
            peak = jnp.max(scores, axis=0, keepdims=True)
            expo = jnp.exp2(scores - peak)
            total = jnp.sum(expo, axis=0, keepdims=True)
            log_ref[0, head : head + 1, start:stop] = peak + jnp.log2(total)
            probs.append((expo * (1.0 / total)).astype(BF))
        mixed = dot(values[0][:, :stop], probs[0], NN) + dot(values[1][:, :stop], probs[1], NN)
        o_ref[start:stop, :] = mixed.T.astype(BF)


def attention(q, k, v):
    length, width = q.shape
    spec = pl.BlockSpec((length, LANES), lambda i: (0, i))
    logs = pl.BlockSpec((1, 2, length), lambda i: (i, 0, 0))
    return pl.pallas_call(
        attention_kernel,
        grid=(PAIRS,),
        in_specs=[spec] * 3,
        out_specs=[spec, logs],
        out_shape=[
            jax.ShapeDtypeStruct((length, width), BF),
            jax.ShapeDtypeStruct((PAIRS, 2, length), F32),
        ],
        compiler_params=pltpu.CompilerParams(vmem_limit_bytes=48 * MIB),
        cost_estimate=pl.CostEstimate(
            flops=PAIRS * 8 * LANES * length * length,
            bytes_accessed=8 * length * width,
            transcendentals=PAIRS * length * length,
        ),
        name="attention",
    )(q, k, v)


def attention_back_kernel(q_ref, k_ref, v_ref, o_ref, do_ref, log_ref, own_ref, ahead_ref, behind_ref,
                          dq_ref, dk_ref, dv_ref, total_ref):
    length = q_ref.shape[0]
    block = min(256, length)
    tables = lambda rows: (own_ref[rows, :], ahead_ref[rows, :], behind_ref[rows, :])
    product = (do_ref[...].astype(F32) * o_ref[...].astype(F32)).T
    deltas = (
        jnp.sum(product[:HD], axis=0, keepdims=True),
        jnp.sum(product[HD:], axis=0, keepdims=True),
    )
    keys = halves(k_ref[...].T, 0)
    for start in range(0, length, block):
        stop = start + block
        queries = halves(q_ref[start:, :], 1)
        grads = halves(do_ref[start:, :], 1)
        dk = dv = dq = None
        for head in range(2):
            scores = dot(k_ref[start:stop, :], queries[head], NT) * (SCALE * LOG2E)
            probs = jnp.exp2(scores - log_ref[0, head : head + 1, start:])
            first = jnp.where(not_after(block), probs[:, :block], 0.0)
            probs = jnp.concatenate([first, probs[:, block:]], axis=1) if stop < length else first
            dprobs = dot(v_ref[start:stop, :], grads[head], NT)
            dscores = (probs * (dprobs - deltas[head][:, start:])).astype(BF)
            parts = (
                dot(probs.astype(BF), grads[head], NN),
                dot(dscores, queries[head], NN),
                dot(keys[head][:, start:stop], dscores, NN),
            )
            dv = parts[0] if dv is None else dv + parts[0]
            dk = parts[1] if dk is None else dk + parts[1]
            dq = parts[2] if dq is None else dq + parts[2]
        dv_ref[start:stop, :] = dv.astype(BF)
        dk_ref[start:stop, :] = unrotate(dk * SCALE, *tables(slice(start, stop))).astype(BF)
        if start == 0:
            total_ref[...] = dq
        else:
            total_ref[:, start:] += dq
    dq_ref[...] = unrotate(total_ref[...].T * SCALE, *tables(slice(None))).astype(BF)


def attention_back(start, count, q, k, v, o, do, logs, tables):
    length = q.shape[0]
    spec = pl.BlockSpec((length, LANES), lambda i: (0, i + start))
    out = pl.BlockSpec((length, LANES), lambda i: (0, i))
    log = pl.BlockSpec((1, 2, length), lambda i: (i + start, 0, 0))
    return pl.pallas_call(
        attention_back_kernel,
        grid=(count,),
        in_specs=[spec] * 5 + [log] + [resident(length, LANES)] * 3,
        out_specs=[out] * 3,
        out_shape=[jax.ShapeDtypeStruct((length, count * LANES), BF)] * 3,
        scratch_shapes=[pltpu.VMEM((LANES, length), F32)],
        compiler_params=pltpu.CompilerParams(vmem_limit_bytes=48 * MIB),
        cost_estimate=pl.CostEstimate(
            flops=count * 20 * LANES * length * length,
            bytes_accessed=16 * length * count * LANES,
            transcendentals=count * length * length,
        ),
        name="attention_back",
    )(q, k, v, o, do, logs, *tables)


def place_rows(target_ref, columns, values, order_ref):
    blocks = order_ref.shape[0]
    size = values.shape[1] // blocks
    for block in range(blocks):
        start = pl.multiple_of(order_ref[block] * size, size)
        target_ref[pl.ds(start, size), columns] = values[:, block * size : (block + 1) * size].T


def feed_forward_kernel(first, last, order_ref, *refs):
    x_ref, o_ref, og_ref, factor_ref, gain_ref, out_low_ref, out_high_ref, wgu_ref, wd_ref = refs[:9]
    refs = refs[9:]
    if first:
        (h_ref, acc_ref, da2_ref, own_ref, send_ref, gd_ref, a2_ref, a2t_ref, dyb_ref, hid_ref, dgu_ref) = refs
    else:
        h_ref, acc_in_ref, da2_in_ref = refs[:3]
        (mixed_ref, dh_ref, do_ref, own_ref, send_ref, gd_ref, dgain_ref) = refs[4:11]
        (acc_ref, da2_ref, a2_ref, a2t_ref, dyb_ref, hid_ref, dgu_ref) = refs[11:]
    step = pl.program_id(0)
    length, width = x_ref.shape
    chunk = wd_ref.shape[0]
    side = width // 2
    tile = min(256, length)
    gain = gain_ref[...].astype(F32)
    matrix = lambda ref: ref[...].reshape(-1, ref.shape[-1])

    @pl.when(step == 0)
    def _():
        for m in range(0, length, tile):
            rows = pl.ds(m, tile)
            if first:
                o = o_ref[rows, :]
                added = [dot(o, matrix(ref), NN) for ref in (out_low_ref, out_high_ref)]
                h = x_ref[rows, :].astype(F32) + jnp.concatenate(added, axis=1)
                h_ref[rows, :] = h
                acc_ref[rows, :] = h
                da2_ref[rows, :] = jnp.zeros((tile, width), F32)
            else:
                h = h_ref[rows, :]
                acc_ref[rows, :] = acc_in_ref[rows, :]
                da2_ref[rows, :] = da2_in_ref[rows, :]
            inverse = lax.rsqrt(jnp.mean(h * h, axis=1, keepdims=True) + EPSILON_NORM)
            a2 = (h * inverse * gain).astype(BF)
            a2_ref[rows, :] = a2
            place_rows(a2t_ref, rows, a2, order_ref)
            dyb_ref[rows, :] = (og_ref[rows, :].astype(F32) * factor_ref[rows, :]).astype(BF)

    def one_chunk():
        weights = matrix(wgu_ref)
        for m in range(0, length, tile):
            rows = pl.ds(m, tile)
            gate = dot(a2_ref[rows, :], weights[:, :chunk], NN)
            up = dot(a2_ref[rows, :], weights[:, chunk:], NN)
            dhid = dot(dyb_ref[rows, :], wd_ref[...], NT)
            sig = 1.0 / (1.0 + jnp.exp2(gate * -LOG2E))
            act = gate * sig
            hid_ref[rows, :] = (act * up).astype(BF)
            dgu_ref[rows, :chunk] = (dhid * up * (sig + act * (1.0 - sig))).astype(BF)
            dgu_ref[rows, chunk:] = (dhid * act).astype(BF)
        for m in range(0, length, tile):
            rows = pl.ds(m, tile)
            acc_ref[rows, :] += dot(hid_ref[rows, :], wd_ref[...], NN)
            da2_ref[rows, :] += dot(dgu_ref[rows, :], weights, NT)
        gd_ref[...] = dot(hid_ref[...], dyb_ref[...], TN).astype(BF)
        own_ref[...] = dot(a2t_ref[:side, :], dgu_ref[...], NN).astype(BF)
        send_ref[...] = dot(a2t_ref[side:, :], dgu_ref[...], NN).astype(BF)

    if first:
        one_chunk()
        return
    tail = pl.num_programs(0) - 2
    pl.when(step < tail)(one_chunk)

    @pl.when(step == tail)
    def _():
        total = jnp.zeros((1, width), F32)
        for m in range(0, length, tile):
            rows = pl.ds(m, tile)
            mixed_ref[rows, :] = acc_ref[rows, :].astype(BF)
            h = h_ref[rows, :]
            inverse = lax.rsqrt(jnp.mean(h * h, axis=1, keepdims=True) + EPSILON_NORM)
            hat = h * inverse
            da2 = da2_ref[rows, :]
            total = total + jnp.sum(da2 * hat, axis=0, keepdims=True)
            scaled = da2 * gain
            dy = og_ref[rows, :].astype(F32) * factor_ref[rows, :]
            dh = dy + inverse * (scaled - hat * jnp.mean(scaled * hat, axis=1, keepdims=True))
            dh_ref[rows, :] = dh
            low = dh.astype(BF)
            dyb_ref[rows, :] = low
            half = width // 2
            do_ref[rows, :] = (
                dot(low[:, :half], matrix(out_low_ref), NT) + dot(low[:, half:], matrix(out_high_ref), NT)
            ).astype(BF)
            place_rows(a2t_ref, rows, o_ref[rows, :], order_ref)
        dgain_ref[...] = total

    for tile_number in range(2):

        @pl.when(step == tail + tile_number)
        def _():
            half = width // 2
            grads = dyb_ref[:, tile_number * half : (tile_number + 1) * half]
            own_ref[...] = dot(a2t_ref[:side, :], grads, NN).astype(BF)
            send_ref[...] = dot(a2t_ref[side:, :], grads, NN).astype(BF)


def feed_forward(order, start, count, state, x, o, out_grad, factor, gain, weights, w_down):
    length, width = x.shape
    chunk = CHUNK
    first = state is None
    chunks = FF // chunk
    steps = count if first else count + 2
    parts, per, tile = weights.shape[0], width // weights.shape[0], weights.shape[2]
    within = lambda i: start + jnp.minimum(i, count - 1)
    weight = lambda index: pl.BlockSpec((parts, per, tile), lambda i, order: (0, index(i), 0))
    kept = lambda index: pl.BlockSpec(
        (parts, per, tile), lambda i, order: (0, index, 0), pipeline_mode=pl.Buffered(1)
    )
    rows = pl.BlockSpec((chunk, width), lambda i, order: (within(i), 0))
    columns = pl.BlockSpec((width // 2, tile), lambda i, order: (0, i))
    shape = jax.ShapeDtypeStruct
    scratch = [
        pltpu.VMEM((length, width), BF),
        pltpu.VMEM((width, length), BF),
        pltpu.VMEM((length, width), BF),
        pltpu.VMEM((length, chunk), BF),
        pltpu.VMEM((length, 2 * chunk), BF),
    ]
    big = resident(length, width)
    in_specs = [big, big, big, resident(length, 1), resident(1, width), kept(chunks), kept(chunks + 1), weight(within), rows]
    operands = [x, o, out_grad, factor, gain, weights, weights, weights, w_down]
    halves_out = [shape((width // 2, steps * tile), BF)] * 2
    aliases = {}
    if first:
        out_specs = [big, big, big, columns, columns, rows]
        out_shape = [shape((length, width), F32)] * 3 + halves_out + [shape((FF, width), BF)]
    else:
        in_specs += [big] * 3 + [pl.BlockSpec(memory_space=pl.ANY)]
        operands += list(state)
        out_specs = [big, big, big, columns, columns, rows, resident(1, width)]
        out_shape = [shape((length, width), BF), shape((length, width), F32), shape((length, width), BF)]
        out_shape += halves_out + [shape((FF, width), BF), shape((1, width), F32)]
        scratch = [pltpu.VMEM((length, width), F32)] * 2 + scratch
        aliases = {len(operands): 5}
    return pl.pallas_call(
        functools.partial(feed_forward_kernel, first, not first),
        grid_spec=pltpu.PrefetchScalarGridSpec(
            num_scalar_prefetch=1, grid=(steps,), in_specs=in_specs, out_specs=out_specs, scratch_shapes=scratch
        ),
        out_shape=out_shape,
        input_output_aliases=aliases,
        compiler_params=pltpu.CompilerParams(vmem_limit_bytes=60 * MIB),
        cost_estimate=pl.CostEstimate(
            flops=2 * length * width * (9 * chunk * count + 2 * QUERY_WIDTH),
            bytes_accessed=40 * MIB,
            transcendentals=length * chunk * count,
        ),
        name="feed_forward",
    )(order, *operands)


def unproject_kernel(a1_ref, c_ref, dq0_ref, dk0_ref, dv0_ref, dq1_ref, dk1_ref, dv1_ref, wup_ref, dql_ref, gin_ref, gup_ref):
    a1t = a1_ref[...].T
    for head, (dq_ref, dk_ref, dv_ref) in enumerate(((dq0_ref, dk0_ref, dv0_ref), (dq1_ref, dk1_ref, dv1_ref))):
        latent = slice(head * LATENT_WIDTH, (head + 1) * LATENT_WIDTH)
        dc = (
            dot(dk_ref[...], wup_ref[latent, :GROUP_WIDTH], NT) + dot(dv_ref[...], wup_ref[latent, GROUP_WIDTH:], NT)
        ).astype(BF)
        mine = slice(QUERY_WIDTH + head * LATENT_WIDTH, QUERY_WIDTH + (head + 1) * LATENT_WIDTH)
        group = slice(head * GROUP_WIDTH, (head + 1) * GROUP_WIDTH)
        dql_ref[:, mine] = dc
        dql_ref[:, group] = dq_ref[...]
        gin_ref[:, mine] = dot(a1t, dc, NN).astype(BF)
        gin_ref[:, group] = dot(a1t, dq_ref[...], NN).astype(BF)
        turned = c_ref[:, latent].T
        gup_ref[latent, :GROUP_WIDTH] = dot(turned, dk_ref[...], NN).astype(BF)
        gup_ref[latent, GROUP_WIDTH:] = dot(turned, dv_ref[...], NN).astype(BF)


def unproject(a1, c, one, two, w_up):
    length, width = a1.shape
    shape = jax.ShapeDtypeStruct
    latents = LATENT_HEADS * LATENT_WIDTH
    operands = (a1, c, *one, *two, w_up)
    outs = ((length, QUERY_WIDTH + latents), (width, QUERY_WIDTH + latents), (latents, 2 * GROUP_WIDTH))
    return pl.pallas_call(
        unproject_kernel,
        grid=(1,),
        in_specs=[resident(*a.shape) for a in operands],
        out_specs=[resident(*s) for s in outs],
        out_shape=[shape(s, BF) for s in outs],
        compiler_params=pltpu.CompilerParams(vmem_limit_bytes=56 * MIB),
        cost_estimate=pl.CostEstimate(
            flops=2 * length * (width * (QUERY_WIDTH + latents) + 4 * latents * GROUP_WIDTH),
            bytes_accessed=16 * MIB,
            transcendentals=0,
        ),
        name="unproject",
    )(*operands)


def input_grad_kernel(x_ref, dh_ref, dql_ref, gain_ref, win_ref, out_ref, dgain_ref):
    x = x_ref[...].astype(F32)
    inverse = lax.rsqrt(jnp.mean(x * x, axis=1, keepdims=True) + EPSILON_NORM)
    hat = x * inverse
    da1 = dot(dql_ref[...], win_ref[...], NT)
    part = jnp.sum(da1 * hat, axis=0, keepdims=True)
    scaled = da1 * gain_ref[...].astype(F32)
    out_ref[...] = (
        dh_ref[...] + inverse * (scaled - hat * jnp.mean(scaled * hat, axis=1, keepdims=True))
    ).astype(BF)

    @pl.when(pl.program_id(0) == 0)
    def _():
        dgain_ref[...] = part

    @pl.when(pl.program_id(0) > 0)
    def _():
        dgain_ref[...] += part


def input_grad(x, dh, dql, gain, w_in):
    length, width = x.shape
    tile = min(256, length)
    rows = lambda columns: pl.BlockSpec((tile, columns), lambda i: (i, 0))
    return pl.pallas_call(
        input_grad_kernel,
        grid=(length // tile,),
        in_specs=[rows(width), rows(width), rows(dql.shape[1]), resident(1, width), resident(*w_in.shape)],
        out_specs=[rows(width), resident(1, width)],
        out_shape=[jax.ShapeDtypeStruct((length, width), BF), jax.ShapeDtypeStruct((1, width), F32)],
        compiler_params=pltpu.CompilerParams(vmem_limit_bytes=48 * MIB),
        cost_estimate=pl.CostEstimate(flops=2 * length * w_in.size, bytes_accessed=16 * MIB, transcendentals=0),
        name="input_grad",
    )(x, dh, dql, gain, w_in)


class Ring:
    def __init__(self, data, line):
        self.cores = 2 if data % 2 == 0 else 1
        self.plane, self.line = data // self.cores, line
        place = lax.axis_index("dp")
        self.core, self.at, self.z = place % self.cores, place // self.cores, lax.axis_index("fsdp")

    def partner(self, index, shift, count):
        if count & (count - 1) == 0:
            return index ^ shift
        return (index + shift) % count

    def send_core(self, value):
        swap = [(i, i ^ 1) for i in range(self.plane * 2)]
        return lax.ppermute(value, "dp", swap)

    def send_plane(self, value, shift):
        pairs = [
            (p * self.cores + c, self.partner(p, shift, self.plane) * self.cores + c)
            for p in range(self.plane)
            for c in range(self.cores)
        ]
        return lax.ppermute(value, "dp", pairs)

    def send_line(self, value, shift):
        return lax.ppermute(value, "fsdp", [(i, (i + shift) % self.line) for i in range(self.line)])


def take(array, index, axis):
    return lax.dynamic_index_in_dim(array, index, axis, keepdims=False)


def split_core(ring, grad):
    rows = grad.shape[0] // (ring.plane * ring.cores * ring.line)
    grad = grad.reshape(ring.plane, ring.cores, ring.line, rows, grad.shape[1])
    if ring.cores == 1:
        return grad[:, 0], None
    return take(grad, ring.core, 1), take(grad, 1 - ring.core, 1)


def sum_core(ring, own, other):
    if ring.cores == 1:
        return own.astype(F32)
    return own.astype(F32) + ring.send_core(other).astype(F32)


def sum_plane(ring, grad, relative):
    block = lambda shift: grad[shift] if relative else take(grad, ring.partner(ring.at, shift, ring.plane), 0)
    received = [ring.send_plane(block(shift).astype(BF), shift) for shift in range(1, ring.plane)]
    return sum((r.astype(F32) for r in received), block(0).astype(F32))


def sum_line(ring, grad, axis):
    received = [
        ring.send_line(take(grad, (ring.z + shift) % ring.line, axis).astype(BF), shift)
        for shift in range(1, ring.line)
    ]
    return sum((r.astype(F32) for r in received), take(grad, ring.z, axis).astype(F32))


def halves_order(ring):
    blocks = jnp.arange(ring.plane * ring.cores)
    plane, core = blocks // ring.cores, blocks % ring.cores
    if ring.plane & (ring.plane - 1) == 0:
        shift = plane ^ ring.at
    else:
        shift = (plane - ring.at) % ring.plane
    return (((core - ring.core) % ring.cores) * ring.plane + shift).astype(jnp.int32)


def gather_first(ring, piece):
    pieces = [piece] + [ring.send_line(piece, shift) for shift in range(1, ring.line)]
    around = jnp.stack(pieces[:0:-1] + [piece] + pieces[:0:-1])
    line = lax.dynamic_slice_in_dim(around, ring.line - 1 - ring.z, ring.line, 0)
    blocks = [line] + [ring.send_plane(line, shift) for shift in range(1, ring.plane)]
    if ring.plane & (ring.plane - 1) == 0:
        shifts = [ring.at ^ at for at in range(ring.plane)]
    else:
        shifts = [(ring.at - at) % ring.plane for at in range(ring.plane)]
    plane = jnp.stack([choose(shift, blocks) for shift in shifts])
    if ring.cores == 1:
        return plane
    other = ring.send_core(plane)
    low = jnp.where(ring.core == 0, plane, other)
    high = jnp.where(ring.core == 0, other, plane)
    both = jnp.stack([low, high], axis=1)
    return both.reshape(ring.plane * 2, *both.shape[2:])


def choose(index, options):
    result = options[0]
    for number, option in enumerate(options[1:], 1):
        result = jnp.where(index == number, option, result)
    return result


def sum_all(ring, value):
    if ring.cores == 2:
        value = value + ring.send_core(value)
    for count, send in ((ring.plane, ring.send_plane), (ring.line, None)):
        if count & (count - 1):
            return lax.psum(value, AXES)
    shift = 1
    while shift < ring.plane:
        value = value + ring.send_plane(value, shift)
        shift *= 2
    shift = 1
    while shift < ring.line:
        swap = [(i, i ^ shift) for i in range(ring.line)]
        value = value + lax.ppermute(value, "fsdp", swap)
        shift *= 2
    return value


def adamw(master, grad, first, second, rate, decay):
    first_new = BETA_ONE * first + (1.0 - BETA_ONE) * grad
    second_new = BETA_TWO * second + (1.0 - BETA_TWO) * grad * grad
    first_hat = first_new / (1.0 - BETA_ONE**STEP)
    second_hat = second_new / (1.0 - BETA_TWO**STEP)
    master_new = master - rate * (
        first_hat / (jnp.sqrt(second_hat) + EPSILON_ADAM) + decay * master
    )
    return (master_new, first_new, second_new)


def after(values, *done):
    return lax.optimization_barrier((values, done))[0]


def shards(data, line, tokens, out_grad, domain_ids, domain_scale, *state):
    masters, moments = state[:6], state[6:]
    firsts, seconds = moments[0::2], moments[1::2]
    ring = Ring(data, line)
    devices = data * line
    length, width = tokens.shape
    p_in, p_up, p_out, p_gate, p_down, p_gains = (w.astype(BF) for w in masters)
    latents = LATENT_HEADS * LATENT_WIDTH
    rows = width // devices
    chunks = FF // CHUNK
    columns = lambda a: a.reshape(a.shape[0], -1, TILE).transpose(1, 0, 2).reshape(-1, TILE)

    gate_tiles = p_gate.reshape(rows, 2, chunks, CHUNK).transpose(2, 0, 1, 3).reshape(-1, TILE)
    bundle = jnp.concatenate([gate_tiles, columns(p_out), columns(p_down)], axis=0)
    bundle = lax.all_gather(bundle, AXES, axis=0, tiled=True).reshape(devices, -1, TILE)

    first = jnp.concatenate([p_in, columns(p_up).reshape(rows, -1), lane_pad(p_gains, rows)], axis=1)
    first = gather_first(ring, first).reshape(devices, rows, -1)
    w_in = first[:, :, : p_in.shape[1]].reshape(width, -1)
    w_up = first[:, :, p_in.shape[1] : p_in.shape[1] + p_up.size // rows]
    w_up = w_up.reshape(devices, 2 * GROUP_WIDTH // TILE, p_up.shape[0], TILE).transpose(0, 2, 1, 3).reshape(latents, -1)
    gains = first[:, :2, -LANES:][:, :, : p_gains.shape[1]].transpose(1, 0, 2).reshape(2, width)

    tables = rotation_tables(length)
    factor = jnp.sum(
        jnp.where(domain_ids[:, None] == jnp.arange(NDOM)[None, :], domain_scale[None, :], 0.0),
        axis=1,
        keepdims=True,
    )
    a1, q, k, v, c = project(tokens, gains[:1], w_in, w_up, tables)
    o, logs = attention(q, k, v)

    split = rows * (chunks + width // TILE)
    w_down = bundle[:, split:].reshape(devices, -1, p_down.shape[0], TILE).transpose(0, 2, 1, 3).reshape(FF, width)
    if rows % 16:
        bundle = bundle[:, :split].reshape(devices, -1, rows, TILE).transpose(1, 0, 2, 3).reshape(1, -1, TILE)
    order = halves_order(ring)
    half = chunks // 2 + 1
    common = (tokens, o, out_grad, factor, gains[1:], bundle, w_down)
    h, acc, da2, own_a, send_a, g_down = feed_forward(order, 0, half, None, *common)
    blocks = lambda a: a.reshape(ring.plane, ring.line, rows, -1)
    sum_a = sum_core(ring, blocks(own_a), blocks(send_a)).astype(BF)
    mixed, dh, do, own_b, send_b, g_down, dgain_two = feed_forward(
        order, half, chunks - half, (h, acc, da2, g_down), *common
    )
    do = after(do, sum_a)
    part_a = sum_plane(ring, sum_a, True).astype(BF)
    sum_b = sum_core(ring, blocks(own_b), blocks(send_b)).astype(BF)
    sum_d = sum_core(ring, *split_core(ring, g_down)).astype(BF)
    one = attention_back(0, PAIRS_PER_LATENT, q, k, v, o, do, logs, tables)
    do = after(do, sum_b, sum_d, one)
    part_d = sum_line(ring, sum_d, 1).astype(BF)
    part_b = sum_plane(ring, sum_b, True).astype(BF)
    two = attention_back(PAIRS_PER_LATENT, PAIRS_PER_LATENT, q, k, v, o, do, logs, tables)
    two = after(two, part_a)
    total_a = sum_line(ring, part_a, 0)
    dql, g_in, g_up = unproject(a1, c, one, two, w_up)
    g_up = g_up.reshape(devices, -1, 2 * GROUP_WIDTH // TILE, TILE).transpose(0, 2, 1, 3).reshape(width, -1)
    sum_c = sum_core(ring, *split_core(ring, jnp.concatenate([g_in, g_up], axis=1))).astype(BF)
    part_c = sum_plane(ring, sum_c, False).astype(BF)
    given, dgain_one = input_grad(tokens, dh, after(dql, sum_c), gains[:1], w_in)
    total_b = sum_line(ring, part_b, 0)
    total_d = sum_plane(ring, part_d, False)
    total_c = sum_line(ring, part_c, 0)

    gated = jnp.concatenate([total_a, total_b[:, : (chunks - half) * TILE]], axis=1)
    gated = gated.reshape(rows, chunks, 2, CHUNK).transpose(0, 2, 1, 3).reshape(rows, -1)
    owned = [
        total_c[:, : p_in.shape[1]],
        total_c[:, p_in.shape[1] :].reshape(-1, *p_up.shape[:1], TILE).transpose(1, 0, 2).reshape(p_up.shape),
        total_b[:, (chunks - half) * TILE :],
        gated,
        total_d,
    ]
    squares = sum(jnp.sum(grad * grad) for grad in (total_a, total_b, total_c, total_d))
    dgains = jnp.concatenate([dgain_one, dgain_two], axis=0)
    message = jnp.concatenate(
        [dgains.reshape(-1, LANES), jnp.full((8, LANES), squares, F32)], axis=0
    )
    message = sum_all(ring, message)
    dgains = message[:-8].reshape(2, width)
    grad_norm = jnp.sqrt(message[-1, 0] + jnp.sum(dgains * dgains))
    clip = jnp.minimum(1.0, MAX_NORM / (grad_norm + 1e-06))
    share = masters[5].shape[1]
    place = lax.axis_index("dp") * line + lax.axis_index("fsdp")
    owned.append(lax.dynamic_slice_in_dim(dgains, place * share, share, 1))
    results = []
    for index in range(6):
        if index == 5:
            rate, decay = (RATE_GAIN, 0.0)
        elif index == 2:
            rate, decay = (RATE_OUTPUT, DECAY_MATRIX)
        else:
            rate, decay = (RATE_MATRIX, DECAY_MATRIX)
        results.extend(
            adamw(masters[index], clip * owned[index], firsts[index], seconds[index], rate, decay)
        )
    return (mixed, given, grad_norm, *results)


def lane_pad(gains, rows):
    return jnp.pad(gains, ((0, rows - gains.shape[0]), (0, LANES - gains.shape[1])))


def solution(mesh):
    data, line = mesh.shape["dp"], mesh.shape["fsdp"]
    rows, flat, columns = P(AXES, None), P(AXES), P(None, AXES)

    def run(*arrays):
        return shards(data, line, *arrays)

    return jax.shard_map(
        run,
        mesh=mesh,
        in_specs=(rows, rows, flat, P()) + (rows,) * 5 + (columns,) + (rows,) * 10 + (columns,) * 2,
        out_specs=(rows, rows, P()) + (rows,) * 15 + (columns,) * 3,
        check_vma=False,
    )
```

```python
import functools
import math

import jax
import jax.numpy as jnp
from jax import lax
from jax.experimental import pallas as pl
from jax.experimental.pallas import tpu as pltpu
from jax.sharding import PartitionSpec as P

HQ = 16
HD = 64
LATENT_HEADS = 2
LATENT_WIDTH = 256
FF = 2816
NDOM = 16
STEP = 10
ROPE = 32
QUERY_WIDTH = HQ * HD
GROUP_WIDTH = QUERY_WIDTH // LATENT_HEADS
LANES = 128
PAIRS = QUERY_WIDTH // LANES
PAIRS_PER_LATENT = PAIRS // LATENT_HEADS

MAX_NORM = 1.0
BETA_ONE = 0.9
BETA_TWO = 0.95
RATE_MATRIX = 0.02
RATE_OUTPUT = 0.2
RATE_GAIN = 1.0
DECAY_MATRIX = 0.1
EPSILON_ADAM = 1e-08
EPSILON_NORM = 1e-06
ROPE_BASE = 10000.0

AXES = ("dp", "fsdp")
BF = jnp.bfloat16
F32 = jnp.float32
LOG2E = 1.4426950408889634
SCALE = HD**-0.5
NN = (((1,), (0,)), ((), ()))
NT = (((1,), (1,)), ((), ()))
TN = (((0,), (0,)), ((), ()))
MIB = 1 << 20
CHUNK = 256
TILE = 2 * CHUNK
FIRST_CHUNKS = 7


def dot(left, right, dims):
    return lax.dot_general(left, right, dims, preferred_element_type=F32)


def cost(microseconds):
    return pl.CostEstimate(flops=int(microseconds * 1e9), bytes_accessed=1 << 20, transcendentals=0)


def resident(*shape):
    return pl.BlockSpec(shape, lambda *step: (0,) * len(shape), pipeline_mode=pl.Buffered(1))


def rotation_tables(length):
    half = ROPE // 2
    lane = jnp.arange(LANES) % HD
    freqs = jnp.where(lane < ROPE, ROPE_BASE ** (-(lane % half).astype(F32) / half), 0.0)
    theta = jnp.arange(length).astype(F32)[:, None] * freqs[None, :]
    sine = jnp.sin(theta)
    ahead = jnp.where(lane < half, -sine, 0.0)
    behind = jnp.where((lane >= half) & (lane < ROPE), sine, 0.0)
    return jnp.cos(theta), ahead, behind


def rotate(values, own, ahead, behind):
    half = ROPE // 2
    return (
        values * own
        + pltpu.roll(values, LANES - half, 1) * ahead
        + pltpu.roll(values, half, 1) * behind
    )


def unrotate(values, own, ahead, behind):
    half = ROPE // 2
    return (
        values * own
        - pltpu.roll(values, LANES - half, 1) * ahead
        - pltpu.roll(values, half, 1) * behind
    )


def lay_out(devices, inverse_ref, mine_ref, other_ref, win_ref, wup_ref, gains_ref):
    plane, size = mine_ref.shape[:2]
    width, side = win_ref.shape
    rows, ups, pieces = width // devices, wup_ref.shape[0] // devices, wup_ref.shape[1] // TILE
    line = size // rows
    gains = [jnp.zeros((1, width), F32)] * 2
    source = lambda rows, columns: lax.broadcasted_iota(jnp.int32, (rows, columns), 0)
    target = lambda rows, columns: lax.broadcasted_iota(jnp.int32, (rows, columns), 1)
    share = width // devices
    spread = (source(LANES, width) == target(LANES, width) % share).astype(BF)
    for place in range(inverse_ref.shape[0]):
        ref = mine_ref if place < plane else other_ref
        block = ref[place % plane]
        index = inverse_ref[place]
        win_ref[pl.ds(pl.multiple_of(index * size, size), size), :] = block[:, :side]
        for z in range(line):
            start = pl.multiple_of((index * line + z) * ups, ups)
            for piece in range(pieces):
                row = z * rows + piece * ups
                columns = slice(piece * TILE, (piece + 1) * TILE)
                wup_ref[pl.ds(start, ups), columns] = block[row : row + ups, side : side + TILE]
        spots = block[:, side + TILE :]
        for which in range(2):
            pick = (target(line, size) == source(line, size) * rows + which).astype(BF)
            found = dot(dot(pick, spots, NN).astype(BF), spread, NN)
            here = target(line, width) // share == source(line, width) + index * line
            gains[which] += jnp.sum(jnp.where(here, found, 0.0), axis=0, keepdims=True)
    gains_ref[...] = jnp.concatenate(gains, axis=0)


def project_kernel(devices, *refs):
    if devices:
        inverse_ref, x_ref, mine_ref, other_ref = refs[:4]
        own_ref, ahead_ref, behind_ref, a1_ref, q_ref, k_ref, v_ref, c_ref, win_ref, wup_ref, gains_ref = refs[4:]

        @pl.when(pl.program_id(0) == 0)
        def _():
            lay_out(devices, inverse_ref, mine_ref, other_ref, win_ref, wup_ref, gains_ref)
    else:
        x_ref, win_ref, wup_ref, gains_ref = refs[1:5]
        own_ref, ahead_ref, behind_ref, a1_ref, q_ref, k_ref, v_ref, c_ref = refs[5:]
    tables = (own_ref[...], ahead_ref[...], behind_ref[...])
    x = x_ref[...].astype(F32)
    inverse = lax.rsqrt(jnp.mean(x * x, axis=1, keepdims=True) + EPSILON_NORM)
    a1 = (x * inverse * gains_ref[:1, :]).astype(BF)
    a1_ref[...] = a1
    joined = dot(a1, win_ref[...], NN)
    for pair in range(PAIRS):
        lanes = slice(pair * LANES, (pair + 1) * LANES)
        q_ref[:, lanes] = rotate(joined[:, lanes], *tables).astype(BF)
    c = joined[:, QUERY_WIDTH:].astype(BF)
    c_ref[...] = c
    for head in range(LATENT_HEADS):
        latent = slice(head * LATENT_WIDTH, (head + 1) * LATENT_WIDTH)
        both = dot(c[:, latent], wup_ref[latent, :], NN)
        for pair in range(PAIRS_PER_LATENT):
            lanes = slice(pair * LANES, (pair + 1) * LANES)
            out = slice(head * GROUP_WIDTH + pair * LANES, head * GROUP_WIDTH + (pair + 1) * LANES)
            k_ref[:, out] = rotate(both[:, lanes], *tables).astype(BF)
        out = slice(head * GROUP_WIDTH, (head + 1) * GROUP_WIDTH)
        v_ref[:, out] = both[:, GROUP_WIDTH:].astype(BF)


def project(devices, inverse, x, tables, *weights):
    length, width = x.shape
    tile = min(256, length)
    latents = LATENT_HEADS * LATENT_WIDTH
    rows = lambda columns: pl.BlockSpec((tile, columns), lambda i, *_: (i, 0))
    shape = lambda columns: jax.ShapeDtypeStruct((length, columns), BF)
    out_specs = [rows(width), rows(QUERY_WIDTH), rows(QUERY_WIDTH), rows(QUERY_WIDTH), rows(latents)]
    out_shape = [shape(width), shape(QUERY_WIDTH), shape(QUERY_WIDTH), shape(QUERY_WIDTH), shape(latents)]
    if devices:
        more = [((width, QUERY_WIDTH + latents), BF), ((latents, 2 * GROUP_WIDTH), BF), ((2, width), F32)]
        out_specs += [resident(*s) for s, _ in more]
        out_shape += [jax.ShapeDtypeStruct(*s) for s in more]
    return pl.pallas_call(
        functools.partial(project_kernel, devices),
        grid_spec=pltpu.PrefetchScalarGridSpec(
            num_scalar_prefetch=1,
            grid=(length // tile,),
            in_specs=[rows(width)] + [resident(*w.shape) for w in weights] + [rows(LANES)] * 3,
            out_specs=out_specs,
        ),
        out_shape=out_shape,
        compiler_params=pltpu.CompilerParams(vmem_limit_bytes=60 * MIB),
        cost_estimate=cost(20),
        name="project",
    )(inverse, x, *weights, *tables)


def halves(pair, axis):
    first = lax.broadcasted_iota(jnp.int32, pair.shape, axis) < HD
    zero = jnp.zeros_like(pair)
    return (jnp.where(first, pair, zero), jnp.where(first, zero, pair))


def not_after(block):
    keys = lax.broadcasted_iota(jnp.int32, (block, block), 0)
    queries = lax.broadcasted_iota(jnp.int32, (block, block), 1)
    return keys <= queries


def attention_kernel(q_ref, k_ref, v_ref, o_ref, log_ref):
    length = q_ref.shape[0]
    block = min(256, length)
    values = halves(v_ref[...].T, 0)
    for start in range(0, length, block):
        stop = start + block
        queries = halves(q_ref[start:stop, :], 1)
        probs = []
        for head in range(2):
            scores = dot(k_ref[:stop, :], queries[head], NT) * (SCALE * LOG2E)
            last = jnp.where(not_after(block), scores[start:, :], -1e30)
            scores = jnp.concatenate([scores[:start, :], last], axis=0) if start else last
            peak = jnp.max(scores, axis=0, keepdims=True)
            expo = jnp.exp2(scores - peak)
            total = jnp.sum(expo, axis=0, keepdims=True)
            log_ref[0, head : head + 1, start:stop] = peak + jnp.log2(total)
            probs.append((expo * (1.0 / total)).astype(BF))
        mixed = dot(values[0][:, :stop], probs[0], NN) + dot(values[1][:, :stop], probs[1], NN)
        o_ref[start:stop, :] = mixed.T.astype(BF)


def attention(q, k, v):
    length, width = q.shape
    spec = pl.BlockSpec((length, LANES), lambda i: (0, i))
    logs = pl.BlockSpec((1, 2, length), lambda i: (i, 0, 0))
    return pl.pallas_call(
        attention_kernel,
        grid=(PAIRS,),
        in_specs=[spec] * 3,
        out_specs=[spec, logs],
        out_shape=[
            jax.ShapeDtypeStruct((length, width), BF),
            jax.ShapeDtypeStruct((PAIRS, 2, length), F32),
        ],
        compiler_params=pltpu.CompilerParams(vmem_limit_bytes=60 * MIB),
        cost_estimate=cost(1),
        name="attention",
    )(q, k, v)


def attention_back_kernel(q_ref, k_ref, v_ref, o_ref, do_ref, log_ref, own_ref, ahead_ref, behind_ref,
                          dq_ref, dk_ref, dv_ref, total_ref):
    length = q_ref.shape[0]
    block = min(256, length)
    tables = lambda rows: (own_ref[rows, :], ahead_ref[rows, :], behind_ref[rows, :])
    product = (do_ref[...].astype(F32) * o_ref[...].astype(F32)).T
    deltas = (
        jnp.sum(product[:HD], axis=0, keepdims=True),
        jnp.sum(product[HD:], axis=0, keepdims=True),
    )
    keys = halves(k_ref[...].T, 0)
    for start in range(0, length, block):
        stop = start + block
        queries = halves(q_ref[start:, :], 1)
        grads = halves(do_ref[start:, :], 1)
        dk = dv = dq = None
        for head in range(2):
            scores = dot(k_ref[start:stop, :], queries[head], NT) * (SCALE * LOG2E)
            probs = jnp.exp2(scores - log_ref[0, head : head + 1, start:])
            first = jnp.where(not_after(block), probs[:, :block], 0.0)
            probs = jnp.concatenate([first, probs[:, block:]], axis=1) if stop < length else first
            dprobs = dot(v_ref[start:stop, :], grads[head], NT)
            dscores = (probs * (dprobs - deltas[head][:, start:])).astype(BF)
            parts = (
                dot(probs.astype(BF), grads[head], NN),
                dot(dscores, queries[head], NN),
                dot(keys[head][:, start:stop], dscores, NN),
            )
            dv = parts[0] if dv is None else dv + parts[0]
            dk = parts[1] if dk is None else dk + parts[1]
            dq = parts[2] if dq is None else dq + parts[2]
        dv_ref[start:stop, :] = dv.astype(BF)
        dk_ref[start:stop, :] = unrotate(dk * SCALE, *tables(slice(start, stop))).astype(BF)
        if start == 0:
            total_ref[...] = dq
        else:
            total_ref[:, start:] += dq
    dq_ref[...] = unrotate(total_ref[...].T * SCALE, *tables(slice(None))).astype(BF)


def attention_back(weight, start, count, q, k, v, o, do, logs, tables):
    length = q.shape[0]
    spec = pl.BlockSpec((length, LANES), lambda i: (0, i + start))
    out = pl.BlockSpec((length, LANES), lambda i: (0, i))
    log = pl.BlockSpec((1, 2, length), lambda i: (i + start, 0, 0))
    return pl.pallas_call(
        attention_back_kernel,
        grid=(count,),
        in_specs=[spec] * 5 + [log] + [resident(length, LANES)] * 3,
        out_specs=[out] * 3,
        out_shape=[jax.ShapeDtypeStruct((length, count * LANES), BF)] * 3,
        scratch_shapes=[pltpu.VMEM((LANES, length), F32)],
        compiler_params=pltpu.CompilerParams(vmem_limit_bytes=60 * MIB),
        cost_estimate=cost(weight),
        name="attention_back",
    )(q, k, v, o, do, logs, *tables)


def place_rows(target_ref, columns, values, order_ref):
    blocks = order_ref.shape[0]
    size = values.shape[1] // blocks
    for block in range(blocks):
        start = pl.multiple_of(order_ref[block] * size, size)
        target_ref[pl.ds(start, size), columns] = values[:, block * size : (block + 1) * size].T


def natural_rows(target_ref, piece_refs, places, inverse_ref):
    size = target_ref.shape[0] // inverse_ref.shape[0]
    for ref, (_, entries) in zip(piece_refs, places):
        for number, (place, row) in enumerate(entries):
            start = pl.multiple_of(inverse_ref[place] * size + row, math.gcd(size, row or size))
            target_ref[pl.ds(start, ref.shape[1]), :] = ref[number]


def natural_copies(target_ref, piece_refs, places, inverse_ref, sems, first, last):
    size = target_ref.shape[0] // inverse_ref.shape[0]
    starts = sorted({column for column, _ in places})
    copy = lambda ref, number, column, block: pltpu.make_async_copy(
        ref.at[number],
        target_ref.at[pl.ds(block * size, size), pl.ds(column, ref.shape[2])],
        sems.at[block, starts.index(column)],
    )

    def start():
        for ref, (column, entries) in zip(piece_refs, places):
            for number, (place, _) in enumerate(entries):
                block = inverse_ref[place]

                @pl.when((block >= first) & (block <= last))
                def _():
                    copy(ref, number, column, block).start()

    def wait(block):
        for column in starts:
            ref = next(ref for ref, (at, _) in zip(piece_refs, places) if at == column)
            copy(ref, 0, column, block).wait()

    return start, wait


def feed_forward_kernel(first, start, count, places, order_ref, inverse_ref, *refs):
    out_places, w_places, d_places = places
    out_refs, refs = refs[: len(out_places)], refs[len(out_places) :]
    w_refs, refs = refs[: len(w_places)], refs[len(w_places) :]
    d_refs, refs = refs[: len(d_places)], refs[len(d_places) :]
    og_ref, factor_ref, gain_ref, o_ref = refs[:4]
    if first:
        x_ref, h_out, acc_ref, da2_ref, own_ref, send_ref, gd_ref, h_ref = refs[4:12]
        refs = refs[12:]
    else:
        h_ref, acc_in, da2_in = refs[4:7]
        mixed_out, dh_out, do_out, own_ref, send_ref, gd_ref, dgain_ref = refs[8:15]
        acc_ref, da2_ref, acc_old_ref, da2_old_ref, mixed_ref, do_ref = refs[15:21]
        refs = refs[21:]
    wout_ref, w_ref, wd_ref, a2_ref, a2t_ref, dyb_ref, hid_ref, dgu_ref, sems, more_sems = refs
    step = pl.program_id(0)
    steps = pl.num_programs(0)
    length, width = og_ref.shape
    chunk = gd_ref.shape[0]
    side = width // 2
    tile, big = min(256, length), min(1024, length)
    gain = gain_ref[...]
    copy = lambda source, target, number: pltpu.make_async_copy(source, target, more_sems.at[number])
    block_size = wd_ref.shape[0] // inverse_ref.shape[0]
    block_first, block_last = start * chunk // block_size, ((start + count) * chunk - 1) // block_size
    fetch, arrived = natural_copies(wd_ref, d_refs, d_places, inverse_ref, sems, block_first, block_last)

    @pl.when(step == 0)
    def _():
        fetch()
        if not first:
            copy(acc_in, acc_old_ref, 0).start()
            copy(da2_in, da2_old_ref, 1).start()
        natural_rows(wout_ref, out_refs, out_places, inverse_ref)
        for m in range(0, length, tile):
            rows = pl.ds(m, tile)
            if first:
                h = x_ref[rows, :].astype(F32) + dot(o_ref[rows, :], wout_ref[...], NN)
                h_ref[rows, :] = h
                acc_ref[rows, :] = h
            else:
                h = h_ref[rows, :]
                acc_ref[rows, :] = jnp.zeros((tile, width), F32)
            da2_ref[rows, :] = jnp.zeros((tile, width), F32)
            inverse = lax.rsqrt(jnp.mean(h * h, axis=1, keepdims=True) + EPSILON_NORM)
            a2 = (h * inverse * gain).astype(BF)
            a2_ref[rows, :] = a2
            place_rows(a2t_ref, rows, a2, order_ref)
            dyb_ref[rows, :] = (og_ref[rows, :].astype(F32) * factor_ref[rows, :]).astype(BF)
        if first:
            copy(h_ref, h_out, 0).start()

    for block in range(block_first, block_last + 1):

        @pl.when(step == max(0, block * block_size // chunk - start))
        def _():
            arrived(block)

    def one_chunk():
        natural_rows(w_ref, w_refs, w_places, inverse_ref)
        down = wd_ref[pl.ds(pl.multiple_of((start + step) * chunk, chunk), chunk), :]
        for m in range(0, length, big):
            rows = pl.ds(m, big)
            gate = dot(a2_ref[rows, :], w_ref[:, :chunk], NN)
            up = dot(a2_ref[rows, :], w_ref[:, chunk:], NN)
            dhid = dot(dyb_ref[rows, :], down, NT)
            sig = 1.0 / (1.0 + jnp.exp2(gate * -LOG2E))
            act = gate * sig
            hid_ref[rows, :] = (act * up).astype(BF)
            dgu_ref[rows, :chunk] = (dhid * up * (sig + act * (1.0 - sig))).astype(BF)
            dgu_ref[rows, chunk:] = (dhid * act).astype(BF)
        for m in range(0, length, big):
            rows = pl.ds(m, big)
            acc_ref[rows, :] += dot(hid_ref[rows, :], down, NN)
            da2_ref[rows, :] += dot(dgu_ref[rows, :], w_ref[...], NT)
        gd_ref[...] = dot(hid_ref[...], dyb_ref[...], TN).astype(BF)
        own_ref[...] = dot(a2t_ref[:side, :], dgu_ref[...], NN).astype(BF)
        send_ref[...] = dot(a2t_ref[side:, :], dgu_ref[...], NN).astype(BF)

    if first:
        one_chunk()

        @pl.when(step == steps - 1)
        def _():
            copy(h_ref, h_out, 0).wait()

        return
    tail = steps - 2
    pl.when(step < tail)(one_chunk)

    @pl.when(step == tail)
    def _():
        copy(acc_in, acc_old_ref, 0).wait()
        copy(da2_in, da2_old_ref, 1).wait()
        total = jnp.zeros((1, width), F32)
        for m in range(0, length, tile):
            rows = pl.ds(m, tile)
            mixed_ref[rows, :] = (acc_old_ref[rows, :] + acc_ref[rows, :]).astype(BF)
            h = h_ref[rows, :]
            inverse = lax.rsqrt(jnp.mean(h * h, axis=1, keepdims=True) + EPSILON_NORM)
            hat = h * inverse
            da2 = da2_old_ref[rows, :] + da2_ref[rows, :]
            total = total + jnp.sum(da2 * hat, axis=0, keepdims=True)
            scaled = da2 * gain
            dy = og_ref[rows, :].astype(F32) * factor_ref[rows, :]
            dh = dy + inverse * (scaled - hat * jnp.mean(scaled * hat, axis=1, keepdims=True))
            acc_ref[rows, :] = dh
            low = dh.astype(BF)
            dyb_ref[rows, :] = low
            do_ref[rows, :] = dot(low, wout_ref[...], NT).astype(BF)
            place_rows(a2t_ref, rows, o_ref[rows, :], order_ref)
        dgain_ref[...] = total
        copy(mixed_ref, mixed_out, 2).start()
        copy(acc_ref, dh_out, 3).start()
        copy(do_ref, do_out, 4).start()

    for tile_number in range(2):

        @pl.when(step == tail + tile_number)
        def _():
            half = width // 2
            grads = dyb_ref[:, tile_number * half : (tile_number + 1) * half]
            own_ref[...] = dot(a2t_ref[:side, :], grads, NN).astype(BF)
            send_ref[...] = dot(a2t_ref[side:, :], grads, NN).astype(BF)

    @pl.when(step == steps - 1)
    def _():
        copy(mixed_ref, mixed_out, 2).wait()
        copy(acc_ref, dh_out, 3).wait()
        copy(do_ref, do_out, 4).wait()


def feed_forward(order, inverse, start, count, skip, state, x, o, out_grad, factor, gain, out_pieces, pieces, down_pieces):
    length, width = out_grad.shape
    chunk = CHUNK
    first = state is None
    steps = count if first else count + 2
    last = count - 1
    rows = pl.BlockSpec((chunk, width), lambda i, *_: (start + jnp.minimum(i, last), 0))
    columns = pl.BlockSpec((width // 2, TILE), lambda i, *_: (0, i))
    whole = lambda *s: pl.BlockSpec(s, lambda i, *_: (0,) * len(s), pipeline_mode=pl.Buffered(1))
    anywhere = pl.BlockSpec(memory_space=pl.ANY)
    shape = jax.ShapeDtypeStruct
    (outs, out_places), (tiles, w_places), (downs, d_places) = out_pieces, pieces, down_pieces
    big = whole(length, width)
    full, low = pltpu.VMEM((length, width), F32), pltpu.VMEM((length, width), BF)
    scratch = [
        pltpu.VMEM((width, width), BF),
        pltpu.VMEM((width, TILE), BF),
        pltpu.VMEM((FF, width), BF),
        low,
        pltpu.VMEM((width, length), BF),
        low,
        pltpu.VMEM((length, chunk), BF),
        pltpu.VMEM((length, TILE), BF),
        pltpu.SemaphoreType.DMA((inverse.shape[0], 2)),
        pltpu.SemaphoreType.DMA((5,)),
    ]
    in_specs = [whole(*piece.shape[:2], width) for piece in outs]
    in_specs += [
        pl.BlockSpec((*piece.shape[:2], TILE), lambda i, *_: (0, 0, skip + jnp.minimum(i, last))) for piece in tiles
    ]
    in_specs += [anywhere] * len(downs)
    in_specs += [big, whole(length, 1), whole(1, width), big]
    operands = [*outs, *tiles, *downs, out_grad, factor, gain, o]
    halves_out = [shape((width // 2, steps * TILE), BF)] * 2
    aliases = {}
    if first:
        in_specs += [big]
        operands += [x]
        out_specs = [anywhere, big, big, columns, columns, rows]
        out_shape = [shape((length, width), F32)] * 3 + halves_out + [shape((FF, width), BF)]
        scratch = [full] + scratch
    else:
        in_specs += [big, anywhere, anywhere, anywhere]
        operands += list(state)
        out_specs = [anywhere, anywhere, anywhere, columns, columns, rows, whole(1, width)]
        out_shape = [shape((length, width), BF), shape((length, width), F32), shape((length, width), BF)]
        out_shape += halves_out + [shape((FF, width), BF), shape((1, width), F32)]
        scratch = [full, full, full, full, low, low] + scratch
        aliases = {len(operands) + 1: 5}
    return pl.pallas_call(
        functools.partial(feed_forward_kernel, first, start, count, (out_places, w_places, d_places)),
        grid_spec=pltpu.PrefetchScalarGridSpec(
            num_scalar_prefetch=2, grid=(steps,), in_specs=in_specs, out_specs=out_specs, scratch_shapes=scratch
        ),
        out_shape=out_shape,
        input_output_aliases=aliases,
        compiler_params=pltpu.CompilerParams(vmem_limit_bytes=63 * MIB),
        cost_estimate=cost(40),
        name="feed_forward",
    )(order, inverse, *operands)


def unproject_kernel(devices, order_ref, a1_ref, c_ref, dq_ref, dk_ref, dv_ref, wup_ref, dql_ref, own_ref, send_ref, *refs):
    gup_ref, a1t_ref, all_ref = refs if devices else (refs[0], refs[1], None)
    length, width = a1_ref.shape
    half = width // 2
    tile = min(256, length)
    for m in range(0, length, tile):
        place_rows(a1t_ref, pl.ds(m, tile), a1_ref[m : m + tile, :], order_ref)
    for head in range(LATENT_HEADS):
        latent = slice(head * LATENT_WIDTH, (head + 1) * LATENT_WIDTH)
        group = slice(head * GROUP_WIDTH, (head + 1) * GROUP_WIDTH)
        dq, dk, dv = dq_ref[:, group], dk_ref[:, group], dv_ref[:, group]
        dc = (dot(dk, wup_ref[latent, :GROUP_WIDTH], NT) + dot(dv, wup_ref[latent, GROUP_WIDTH:], NT)).astype(BF)
        mine = slice(QUERY_WIDTH + head * LATENT_WIDTH, QUERY_WIDTH + (head + 1) * LATENT_WIDTH)
        dql_ref[:, mine] = dc
        dql_ref[:, group] = dq
        for columns, grad in ((mine, dc), (group, dq)):
            own_ref[:, columns] = dot(a1t_ref[:half, :], grad, NN).astype(BF)
            send_ref[:, columns] = dot(a1t_ref[half:, :], grad, NN).astype(BF)
        turned = c_ref[:, latent].T
        gup_ref[latent, :GROUP_WIDTH] = dot(turned, dk, NN).astype(BF)
        gup_ref[latent, GROUP_WIDTH:] = dot(turned, dv, NN).astype(BF)
    if not devices:
        return
    rows, ups = width // devices, gup_ref.shape[0] // devices
    blocks = order_ref.shape[0]
    line = devices // blocks
    for block in range(blocks):
        for z in range(line):
            device = block * line + z
            for piece in range(gup_ref.shape[1] // TILE):
                start = pl.multiple_of(order_ref[block] * (line * rows) + (z * rows + piece * ups), ups)
                value = gup_ref[device * ups : (device + 1) * ups, piece * TILE : (piece + 1) * TILE]
                all_ref[pl.ds(start, ups), :] = value
    side = dql_ref.shape[1]
    own_ref[:, side:] = all_ref[:half, :]
    send_ref[:, side:] = all_ref[half:, :]


def unproject(devices, order, a1, c, dq, dk, dv, w_up):
    length, width = a1.shape
    latents = LATENT_HEADS * LATENT_WIDTH
    side = QUERY_WIDTH + latents
    operands = (a1, c, dq, dk, dv, w_up)
    both = side + TILE if devices else side
    outs = [(length, side), (width // 2, both), (width // 2, both)]
    scratch = [pltpu.VMEM((width, length), BF)]
    if devices:
        scratch = [pltpu.VMEM(w_up.shape, BF)] + scratch + [pltpu.VMEM((width, TILE), BF)]
    else:
        outs.append(w_up.shape)
    return pl.pallas_call(
        functools.partial(unproject_kernel, devices),
        grid_spec=pltpu.PrefetchScalarGridSpec(
            num_scalar_prefetch=1,
            grid=(1,),
            in_specs=[resident(*a.shape) for a in operands],
            out_specs=[resident(*s) for s in outs],
            scratch_shapes=scratch,
        ),
        out_shape=[jax.ShapeDtypeStruct(s, BF) for s in outs],
        compiler_params=pltpu.CompilerParams(vmem_limit_bytes=60 * MIB),
        cost_estimate=cost(20),
        name="unproject",
    )(order, *operands)


def input_grad_kernel(x_ref, dh_ref, dql_ref, gain_ref, win_ref, out_ref, dgain_ref):
    x = x_ref[...].astype(F32)
    inverse = lax.rsqrt(jnp.mean(x * x, axis=1, keepdims=True) + EPSILON_NORM)
    hat = x * inverse
    da1 = dot(dql_ref[...], win_ref[...], NT)
    part = jnp.sum(da1 * hat, axis=0, keepdims=True)
    scaled = da1 * gain_ref[...].astype(F32)
    out_ref[...] = (
        dh_ref[...] + inverse * (scaled - hat * jnp.mean(scaled * hat, axis=1, keepdims=True))
    ).astype(BF)

    @pl.when(pl.program_id(0) == 0)
    def _():
        dgain_ref[...] = part

    @pl.when(pl.program_id(0) > 0)
    def _():
        dgain_ref[...] += part


def input_grad(x, dh, dql, gain, w_in):
    length, width = x.shape
    tile = min(256, length)
    rows = lambda columns: pl.BlockSpec((tile, columns), lambda i: (i, 0))
    return pl.pallas_call(
        input_grad_kernel,
        grid=(length // tile,),
        in_specs=[rows(width), rows(width), rows(dql.shape[1]), resident(1, width), resident(*w_in.shape)],
        out_specs=[rows(width), resident(1, width)],
        out_shape=[jax.ShapeDtypeStruct((length, width), BF), jax.ShapeDtypeStruct((1, width), F32)],
        compiler_params=pltpu.CompilerParams(vmem_limit_bytes=60 * MIB),
        cost_estimate=cost(20),
        name="input_grad",
    )(x, dh, dql, gain, w_in)


class Ring:
    def __init__(self, data, line):
        self.cores = 2 if data % 2 == 0 else 1
        self.plane, self.line = data // self.cores, line
        place = lax.axis_index("dp")
        self.core, self.at, self.z = place % self.cores, place // self.cores, lax.axis_index("fsdp")

    def partner(self, index, shift, count):
        if count & (count - 1) == 0:
            return index ^ shift
        return (index + shift) % count

    def send_core(self, value):
        swap = [(i, i ^ 1) for i in range(self.plane * 2)]
        return lax.ppermute(value, "dp", swap)

    def send_plane(self, value, shift):
        pairs = [
            (p * self.cores + c, self.partner(p, shift, self.plane) * self.cores + c)
            for p in range(self.plane)
            for c in range(self.cores)
        ]
        return lax.ppermute(value, "dp", pairs)

    def send_line(self, value, shift):
        return lax.ppermute(value, "fsdp", [(i, (i + shift) % self.line) for i in range(self.line)])


def take(array, index, axis):
    return lax.dynamic_index_in_dim(array, index, axis, keepdims=False)


def core_blocks(ring, grad, core):
    rows = grad.shape[0] // (ring.plane * ring.cores * ring.line)
    return take(grad.reshape(ring.plane, ring.cores, ring.line, rows, grad.shape[1]), core, 1)


def total(parts):
    return sum(part.astype(F32) for part in parts)


def core_sends(ring, value):
    return [(ring.send_core, value)]


def plane_sends(ring, parts, relative):
    spot = lambda shift: shift if relative else ring.partner(ring.at, shift, ring.plane)
    block = lambda shift: total([take(part, spot(shift), 0) for part in parts]).astype(BF)
    sends = [
        (lambda value, shift=shift: ring.send_plane(value, shift), block(shift)) for shift in range(1, ring.plane)
    ]
    return block(0), sends


def line_sends(ring, grad, bit, axis=0):
    shape = grad.shape
    pairs = grad.reshape(*shape[:axis], shape[axis] // 2, 2, *shape[axis + 1 :])
    side = (ring.z >> bit) & 1
    swap = [(i, i ^ (1 << bit)) for i in range(ring.line)]
    give = take(pairs, 1 - side, axis + 1).astype(BF)
    return take(pairs, side, axis + 1), [(lambda value: lax.ppermute(value, "fsdp", swap), give)]


def beside(sends, kept, kernel=None, *inputs):
    inputs, gives, kept = together(inputs, [give for _, give in sends], kept)
    received = [send(give) for (send, _), give in zip(sends, gives)]
    return together(kernel(*inputs) if kernel else (), received, kept)


def line_rest(ring, grads, done):
    for bit in range(done, ring.line.bit_length() - 1):
        kept, sends = zip(*(line_sends(ring, grad, bit) for grad in grads))
        _, received, kept = beside([send for one in sends for send in one], kept)
        grads = [total(pair) for pair in zip(kept, received)]
    return [grad[0] for grad in grads]


def halves_order(ring):
    blocks = jnp.arange(ring.plane * ring.cores)
    plane, core = blocks // ring.cores, blocks % ring.cores
    if ring.plane & (ring.plane - 1) == 0:
        shift = plane ^ ring.at
    else:
        shift = (plane - ring.at) % ring.plane
    order = (((core - ring.core) % ring.cores) * ring.plane + shift).astype(jnp.int32)
    shift, core = blocks % ring.plane, blocks // ring.plane
    if ring.plane & (ring.plane - 1) == 0:
        plane = shift ^ ring.at
    else:
        plane = (shift + ring.at) % ring.plane
    inverse = (plane * ring.cores + (core + ring.core) % ring.cores).astype(jnp.int32)
    return order, inverse


class Gather:
    def __init__(self, ring, piece, by_columns=False):
        self.ring, self.by_columns = ring, by_columns
        self.block = piece[None]
        self.bits = list(range(ring.line.bit_length() - 1))[::-1]

    def line_sends(self):
        swap = [(i, i ^ (1 << self.bits[0])) for i in range(self.ring.line)]
        return [(lambda value: lax.ppermute(value, "fsdp", swap), self.block)]

    def line_receive(self, values):
        low = ((self.ring.z >> self.bits.pop(0)) & 1) == 0
        pair = [jnp.where(low, self.block, values[0]), jnp.where(low, values[0], self.block)]
        block = jnp.stack(pair, axis=1)
        self.block = block.reshape(-1, *block.shape[2:])
        if not self.bits:
            self.split()

    def split(self):
        line, rows, columns = self.block.shape
        count = self.ring.plane.bit_length() - 1
        if self.by_columns:
            cut = columns // 2
            halves = [self.block[..., :cut].reshape(1, -1, cut), self.block[..., cut:].reshape(1, -1, cut)]
            self.offsets = [(0, 0), (cut, 0)]
        else:
            whole = self.block.reshape(-1, columns)
            cut = whole.shape[0] // 2
            halves = [whole[None, :cut], whole[None, cut:]]
            self.offsets = [(0, 0), (0, cut)]
        self.halves = [([half], [[0]]) for half in halves]
        self.orders = [list(range(count)), list(range(count))[::-1]]

    def plane_sends(self):
        sends = []
        for (arrays, _), order in zip(self.halves, self.orders):
            value = jnp.concatenate(arrays, axis=0) if len(arrays) > 1 else arrays[0]
            sends.append((lambda value, bit=order[0]: self.ring.send_plane(value, 1 << bit), value))
        return sends

    def plane_receive(self, values):
        for (arrays, shifts), order, value in zip(self.halves, self.orders, values):
            bit = order.pop(0)
            shifts.append([shift ^ (1 << bit) for have in shifts for shift in have])
            arrays.append(value)

    def direct_sends(self):
        self.offsets = [(0, 0)]
        block = self.block.reshape(1, -1, self.block.shape[-1])
        self.halves = [([block], [[0]])]
        return [(lambda value, k=k: self.ring.send_plane(value, k), block) for k in range(1, self.ring.plane)]

    def direct_receive(self, values):
        for shift, value in enumerate(values, 1):
            self.halves[0][0].append(value)
            self.halves[0][1].append([shift])

    def arrays(self):
        return [array for arrays, _ in self.halves for array in arrays]

    def hold(self, arrays):
        arrays = list(arrays)
        for mine, _ in self.halves:
            for number in range(len(mine)):
                mine[number] = arrays.pop(0)

    def places(self, core):
        return [
            (column, [(core * self.ring.plane + shift, row) for shift in have])
            for (_, shifts), (column, row) in zip(self.halves, self.offsets)
            for have in shifts
        ]

    def pieces(self, other):
        if self.ring.cores == 1:
            return self.arrays(), self.places(0)
        return self.arrays() + list(other), self.places(0) + self.places(1)

    def stacked(self):
        blocks = [{}, {}]
        for found, (arrays, shifts) in zip(blocks, self.halves):
            for array, have in zip(arrays, shifts):
                found.update(zip(have, array))
        return jnp.stack([jnp.concatenate([found[k] for found in blocks], axis=0) for k in range(self.ring.plane)])


def natural(ring, mine, other):
    if ring.plane & (ring.plane - 1) == 0:
        shifts = [ring.at ^ at for at in range(ring.plane)]
    else:
        shifts = [(ring.at - at) % ring.plane for at in range(ring.plane)]
    blocks = []
    for shift in shifts:
        pair = [choose(shift, list(part)) for part in (mine, other)][: ring.cores]
        blocks += [choose((core - ring.core) % ring.cores, pair) for core in range(ring.cores)]
    return jnp.stack(blocks)


def choose(index, options):
    result = options[0]
    for number, option in enumerate(options[1:], 1):
        result = jnp.where(index == number, option, result)
    return result


def sum_all(ring, value):
    if ring.cores == 2:
        value = value + ring.send_core(value)
    for count, send in ((ring.plane, ring.send_plane), (ring.line, None)):
        if count & (count - 1):
            return lax.psum(value, AXES)
    shift = 1
    while shift < ring.plane:
        value = value + ring.send_plane(value, shift)
        shift *= 2
    shift = 1
    while shift < ring.line:
        swap = [(i, i ^ shift) for i in range(ring.line)]
        value = value + lax.ppermute(value, "fsdp", swap)
        shift *= 2
    return value


def adamw_kernel(message_ref, dgains_ref, a_ref, b_ref, c_ref, d_ref, *refs):
    masters, firsts, seconds, norm_ref, outs = refs[:6], refs[6:12], refs[12:18], refs[18], refs[19:]
    gains = message_ref[:-8, :]
    norm = jnp.sqrt(message_ref[-1:, :1] + jnp.sum(gains * gains, keepdims=True))
    norm_ref[...] = norm
    clip = jnp.minimum(1.0, MAX_NORM / (norm + 1e-06))

    def update(index, place, grad, rate, decay):
        grad = clip * grad
        master = masters[index][place]
        first_new = BETA_ONE * firsts[index][place] + (1.0 - BETA_ONE) * grad
        second_new = BETA_TWO * seconds[index][place] + (1.0 - BETA_TWO) * grad * grad
        first_hat = first_new / (1.0 - BETA_ONE**STEP)
        second_hat = second_new / (1.0 - BETA_TWO**STEP)
        outs[3 * index][place] = master - rate * (
            first_hat / (jnp.sqrt(second_hat) + EPSILON_ADAM) + decay * master
        )
        outs[3 * index + 1][place] = first_new
        outs[3 * index + 2][place] = second_new

    everything = (slice(None), slice(None))
    side = masters[0].shape[1]
    update(0, everything, c_ref[:, :side], RATE_MATRIX, DECAY_MATRIX)
    rows = masters[1].shape[0]
    for tile in range(masters[1].shape[1] // TILE):
        place = (slice(None), slice(tile * TILE, (tile + 1) * TILE))
        update(1, place, c_ref[tile * rows : (tile + 1) * rows, side:], RATE_MATRIX, DECAY_MATRIX)
    second = FF // CHUNK - FIRST_CHUNKS
    update(2, everything, b_ref[:, second * TILE :], RATE_OUTPUT, DECAY_MATRIX)
    for chunk in range(FF // CHUNK):
        ref, at = (a_ref, chunk) if chunk < FIRST_CHUNKS else (b_ref, chunk - FIRST_CHUNKS)
        for which in range(2):
            place = (slice(None), slice(which * FF + chunk * CHUNK, which * FF + (chunk + 1) * CHUNK))
            start = at * TILE + which * CHUNK
            update(3, place, ref[:, start : start + CHUNK], RATE_MATRIX, DECAY_MATRIX)
    update(4, everything, d_ref[...], RATE_MATRIX, DECAY_MATRIX)
    update(5, everything, dgains_ref[...], RATE_GAIN, 0.0)


def adamw(message, dgains, totals, masters, firsts, seconds):
    shape = jax.ShapeDtypeStruct
    outs = [shape((1, 1), F32)] + [shape(w.shape, F32) for w in masters for _ in range(3)]
    return pl.pallas_call(
        adamw_kernel,
        out_shape=outs,
        compiler_params=pltpu.CompilerParams(vmem_limit_bytes=60 * MIB),
        cost_estimate=cost(5),
        name="adamw",
    )(message, dgains, *totals, *masters, *firsts, *seconds)


def together(*values):
    return lax.optimization_barrier(values)


def shards(data, line, tokens, out_grad, domain_ids, domain_scale, *state):
    masters, moments = state[:6], state[6:]
    firsts, seconds = moments[0::2], moments[1::2]
    ring = Ring(data, line)
    devices = data * line
    length, width = tokens.shape
    p_in, p_up, p_out, p_gate, p_down, p_gains = (w.astype(BF) for w in masters)
    latents = LATENT_HEADS * LATENT_WIDTH
    rows = width // devices
    chunks = FF // CHUNK
    columns = lambda a: a.reshape(a.shape[0], -1, TILE).transpose(1, 0, 2).reshape(-1, TILE)

    tiles = p_gate.reshape(rows, 2, chunks, CHUNK).transpose(0, 2, 1, 3).reshape(rows, -1)
    half = FIRST_CHUNKS
    one = Gather(ring, jnp.concatenate([p_in, columns(p_up).reshape(rows, -1), lane_pad(p_gains, rows)], axis=1))
    two = Gather(ring, jnp.concatenate([p_out, tiles[:, : half * TILE]], axis=1))
    down = Gather(ring, p_down, True)
    three = Gather(ring, tiles[:, half * TILE :])
    order, inverse = halves_order(ring)

    def early(domain_ids):
        picked = domain_ids[:, None] == jnp.arange(NDOM)[None, :]
        factor = jnp.sum(jnp.where(picked, domain_scale[None, :], 0.0), axis=1, keepdims=True)
        return rotation_tables(length), factor

    first = True
    while len(one.bits) > 0:
        if first:
            (tables, factor), received, _ = beside(one.line_sends(), (), early, domain_ids)
        else:
            _, received, _ = beside(one.line_sends(), ())
        first = False
        one.line_receive(received)
    number = 0
    while len(down.bits) > 0 or len(one.orders[0]) > 0:
        sends = one.plane_sends() if len(one.orders[0]) > 0 else []
        split = len(sends)
        sends += down.line_sends() if len(down.bits) > 0 else []
        _, received, kept = beside(sends, one.arrays())
        one.hold(kept)
        if split:
            one.plane_receive(received[:split])
        if len(received) > split:
            down.line_receive(received[split:])
    one_block = one.stacked()
    sends = core_sends(ring, one_block) + down.plane_sends() + two.line_sends()
    _, received, (one_block, kept, tokens) = beside(sends, (one_block, down.arrays(), tokens))
    down.hold(kept)
    one_other = received[0]
    down.plane_receive(received[1:-1])
    two.line_receive(received[-1:])
    while len(down.orders[0]) > 0 or len(two.bits) > 0:
        sends = down.plane_sends() if len(down.orders[0]) > 0 else []
        split = len(sends)
        sends += two.line_sends() if len(two.bits) > 0 else []
        _, received, kept = beside(sends, down.arrays())
        down.hold(kept)
        if split:
            down.plane_receive(received[:split])
        if len(received) > split:
            two.line_receive(received[split:])
    aligned = rows % 32 == 0 and p_up.shape[0] % 16 == 0
    if aligned:
        run = lambda tokens: project(devices, inverse, tokens, tables, one_block, one_other)
    else:
        first = natural(ring, one_block, one_other).reshape(devices, rows, -1)
        w_in = first[:, :, : p_in.shape[1]].reshape(width, -1)
        w_up = first[:, :, p_in.shape[1] : p_in.shape[1] + p_up.size // rows]
        w_up = w_up.reshape(devices, 2 * GROUP_WIDTH // TILE, p_up.shape[0], TILE).transpose(0, 2, 1, 3).reshape(latents, -1)
        gains = first[:, :2, -LANES:][:, :, : p_gains.shape[1]].transpose(1, 0, 2).reshape(2, width).astype(F32)
        run = lambda tokens: (*project(0, inverse, tokens, tables, w_in, w_up, gains), w_in, w_up, gains)
    down_mine = down.arrays()
    down_sends = [send for array in down_mine for send in core_sends(ring, array)]
    cut = 2
    sends = two.plane_sends() + three.line_sends() + down_sends[:cut]
    (a1, q, k, v, c, w_in, w_up, gains), received, kept = beside(sends, (two.arrays(), down_mine), run, tokens)
    two.hold(kept[0])
    down.hold(kept[1])
    down_sends = [(send, array) for (send, _), array in zip(down_sends, kept[1])]
    two.plane_receive(received[:2])
    three.line_receive(received[2:3])
    down_other = list(received[3:])
    sends = two.plane_sends() if len(two.orders[0]) > 0 else []
    split = len(sends)
    sends += three.line_sends() if len(three.bits) > 0 else []
    middle = len(sends)
    sends += down_sends[cut : 2 * cut]
    (o, logs), received, kept = beside(sends, (two.arrays(), down.arrays()), attention, q, k, v)
    two.hold(kept[0])
    down.hold(kept[1])
    down_sends = [(send, array) for (send, _), array in zip(down_sends, kept[1])]
    if split:
        two.plane_receive(received[:split])
    if middle > split:
        three.line_receive(received[split:middle])
    down_other += list(received[middle:])
    while len(two.orders[0]) > 0:
        two.plane_receive(beside(two.plane_sends(), ())[1])
    while len(three.bits) > 0:
        three.line_receive(beside(three.line_sends(), ())[1])
    sends = down_sends[2 * cut :] + [send for array in two.arrays() for send in core_sends(ring, array)]
    split = len(down_sends[2 * cut :])
    _, received, (o, kept, kept_down, kept_other) = beside(sends, (o, two.arrays(), down.arrays(), down_other))
    two.hold(kept)
    down.hold(kept_down)
    down_pieces = down.pieces(list(kept_other) + list(received[:split]))
    two_pieces = two.pieces(received[split:])
    common = (tokens, o, out_grad, factor, gains[1:], two_pieces)
    run = lambda o: feed_forward(
        order, inverse, 0, half, width // TILE, None, tokens, o, out_grad, factor, gains[1:], two_pieces, two_pieces, down_pieces
    )
    (h, acc, da2, own_a, send_a, g_down), received, kept = beside(three.direct_sends(), three.arrays(), run, o)
    three.hold(kept)
    three.direct_receive(received)
    blocks = lambda a: a.reshape(ring.plane, ring.line, rows, -1)
    sends = core_sends(ring, blocks(send_a)) + [send for array in three.arrays() for send in core_sends(ring, array)]
    _, received, (h, own_a, kept) = beside(sends, (h, own_a, three.arrays()))
    three.hold(kept)
    three_pieces = three.pieces(received[1:])
    kept_a, sends = plane_sends(ring, [blocks(own_a), received[0]], True)
    state = (acc, da2, g_down)
    run = lambda h: feed_forward(
        order, inverse, half, chunks - half, 0, (h, *state), *common, three_pieces, down_pieces
    )
    out, received, kept_a = beside(sends, kept_a, run, h)
    mixed, dh, do, own_b, send_b, g_down, dgain_two = out

    def run(g_down, kept_a, *came_a):
        kept_a, send_a = line_sends(ring, total([kept_a, *came_a]), 0)
        return core_blocks(ring, g_down, 1 - ring.core), kept_a, send_a[0][1]

    out, came_b, (do, own_b) = beside(core_sends(ring, blocks(send_b)), (do, own_b), run, g_down, kept_a, *received)
    send_d, kept_a, give_a = out
    kept_b, send_b = plane_sends(ring, [blocks(own_b), *came_b], True)
    sends = send_b + core_sends(ring, send_d) + [(line_sends(ring, give_a, 0)[1][0][0], give_a)]
    run = lambda do: attention_back(40, 0, PAIRS, q, k, v, o, do, logs, tables)
    grads, received, (kept_a, kept_b, g_down) = beside(sends, (kept_a, kept_b, g_down), run, do)
    *came_b, came_d, came_a = received
    halves_d = [jnp.split(part, 2, axis=-1) for part in (core_blocks(ring, g_down, ring.core), came_d)]
    kept_d, send_d = plane_sends(ring, [part[0] for part in halves_d], False)
    kept_e, send_e = line_sends(ring, total([part[1] for part in halves_d]), 0, 1)
    kept_a, send_a = line_sends(ring, total([kept_a, came_a]), 1)

    def run(dq, dk, dv):
        dql, own, send, *g_up = unproject(devices if aligned else 0, order, a1, c, dq, dk, dv, w_up)
        if g_up:
            g_up = g_up[0].reshape(devices, -1, 2 * GROUP_WIDTH // TILE, TILE).transpose(0, 2, 1, 3).reshape(width, -1)
            spots = [jnp.stack([take(core_blocks(ring, g_up, core), ring.partner(ring.at, k, ring.plane), 0)
                                for k in range(ring.plane)]).reshape(width // 2, -1) for core in (ring.core, 1 - ring.core)]
            own, send = jnp.concatenate([own, spots[0]], axis=1), jnp.concatenate([send, spots[1]], axis=1)
        return dql, own, send

    kept = (kept_a, kept_b, kept_d, kept_e, came_b)
    out, received, kept = beside(send_d + send_a + send_e, kept, run, *grads)
    kept_a, kept_b, kept_d, kept_e, came_b = kept
    dql, own_c, send_c = out
    *came_d, came_a, came_e = received
    kept_b, send_b = line_sends(ring, total([kept_b, *came_b]), 0)
    kept_e, send_e = line_sends(ring, total([kept_e, came_e]), 1, 1)
    _, received, kept = beside(
        core_sends(ring, blocks(send_c)) + send_b + send_e, (dql, own_c, kept_a, came_a, kept_b, kept_d, came_d, kept_e)
    )
    dql, own_c, kept_a, came_a, kept_b, kept_d, came_d, kept_e = kept
    came_c, came_b, came_e = received
    kept_a = total([kept_a, came_a])
    kept_c, send_c = plane_sends(ring, [blocks(own_c), came_c], True)
    kept_b, send_b = line_sends(ring, total([kept_b, came_b]), 1)
    kept_d, send_d = line_sends(ring, total([kept_d, *came_d]), 0)
    run = lambda dql: input_grad(tokens, dh, dql, gains[:1], w_in)
    kept = (kept_b, kept_c, kept_d, kept_e, came_e)
    (given, dgain_one), received, kept = beside(send_c + send_d + send_b, kept, run, dql)
    kept_b, kept_c, kept_d, kept_e, came_e = kept
    *came_c, came_d, came_b = received
    kept_b = total([kept_b, came_b])
    sum_e = total([kept_e, came_e])
    for bit in range(2, ring.line.bit_length() - 1):
        kept_e, send_e = line_sends(ring, sum_e, bit, 1)
        sum_e = total([kept_e, beside(send_e, ())[1][0]])
    kept_c, send_c = line_sends(ring, total([kept_c, *came_c]), 0)
    kept_d, send_d = line_sends(ring, total([kept_d, came_d]), 1)
    kept_e, send_e = plane_sends(ring, [sum_e], False)
    _, received, (kept_c, kept_d, kept_e) = beside(send_c + send_d + send_e, (kept_c, kept_d, kept_e))
    came_c, came_d, *came_e = received
    sums = [kept_a, kept_b, total([kept_d, came_d])]
    total_a, total_b, total_d = line_rest(ring, sums, 2)
    (total_c,) = line_rest(ring, [total([kept_c, came_c])], 1)
    total_d = jnp.concatenate([total_d, total([kept_e, *came_e])[0]], axis=-1)

    squares = sum(jnp.sum(grad * grad) for grad in (total_a, total_b, total_c, total_d))
    dgains = jnp.concatenate([dgain_one, dgain_two], axis=0)
    message = jnp.concatenate(
        [dgains.reshape(-1, LANES), jnp.full((8, LANES), squares, F32)], axis=0
    )
    message = sum_all(ring, message)
    share = masters[5].shape[1]
    place = lax.axis_index("dp") * line + lax.axis_index("fsdp")
    dgains = lax.dynamic_slice_in_dim(message[:-8].reshape(2, width), place * share, share, 1)
    totals = (total_a, total_b, total_c, total_d)
    grad_norm, *results = adamw(message, dgains, totals, masters, firsts, seconds)
    return (mixed, given, grad_norm[0, 0], *results)


def lane_pad(gains, rows):
    return jnp.pad(gains, ((0, rows - gains.shape[0]), (0, LANES - gains.shape[1])))


def solution(mesh):
    data, line = mesh.shape["dp"], mesh.shape["fsdp"]
    rows, flat, columns = P(AXES, None), P(AXES), P(None, AXES)

    def run(*arrays):
        return shards(data, line, *arrays)

    return jax.shard_map(
        run,
        mesh=mesh,
        in_specs=(rows, rows, flat, P()) + (rows,) * 5 + (columns,) + (rows,) * 10 + (columns,) * 2,
        out_specs=(rows, rows, P()) + (rows,) * 15 + (columns,) * 3,
        check_vma=False,
    )
```

```python
import functools
import math

import jax
import jax.numpy as jnp
from jax import lax
from jax.experimental import pallas as pl
from jax.experimental.pallas import tpu as pltpu
from jax.sharding import PartitionSpec as P

HQ = 16
HD = 64
LATENT_HEADS = 2
LATENT_WIDTH = 256
FF = 2816
NDOM = 16
STEP = 10
ROPE = 32
QUERY_WIDTH = HQ * HD
GROUP_WIDTH = QUERY_WIDTH // LATENT_HEADS
LANES = 128
PAIRS = QUERY_WIDTH // LANES
PAIRS_PER_LATENT = PAIRS // LATENT_HEADS

MAX_NORM = 1.0
BETA_ONE = 0.9
BETA_TWO = 0.95
RATE_MATRIX = 0.02
RATE_OUTPUT = 0.2
RATE_GAIN = 1.0
DECAY_MATRIX = 0.1
EPSILON_ADAM = 1e-08
EPSILON_NORM = 1e-06
ROPE_BASE = 10000.0

AXES = ("dp", "fsdp")
BF = jnp.bfloat16
F32 = jnp.float32
LOG2E = 1.4426950408889634
SCALE = HD**-0.5
NN = (((1,), (0,)), ((), ()))
NT = (((1,), (1,)), ((), ()))
TN = (((0,), (0,)), ((), ()))
MIB = 1 << 20
CHUNK = 256
TILE = 2 * CHUNK
FIRST_CHUNKS = 7


def dot(left, right, dims):
    return lax.dot_general(left, right, dims, preferred_element_type=F32)


def cost(microseconds):
    return pl.CostEstimate(flops=int(microseconds * 1e9), bytes_accessed=1 << 20, transcendentals=0)


def resident(*shape):
    return pl.BlockSpec(shape, lambda *step: (0,) * len(shape), pipeline_mode=pl.Buffered(1))


def rotation_tables(length):
    half = ROPE // 2
    lane = jnp.arange(LANES) % HD
    freqs = jnp.where(lane < ROPE, ROPE_BASE ** (-(lane % half).astype(F32) / half), 0.0)
    theta = jnp.arange(length).astype(F32)[:, None] * freqs[None, :]
    sine = jnp.sin(theta)
    ahead = jnp.where(lane < half, -sine, 0.0)
    behind = jnp.where((lane >= half) & (lane < ROPE), sine, 0.0)
    return jnp.cos(theta), ahead, behind


def rotate(values, own, ahead, behind):
    half = ROPE // 2
    return (
        values * own
        + pltpu.roll(values, LANES - half, 1) * ahead
        + pltpu.roll(values, half, 1) * behind
    )


def unrotate(values, own, ahead, behind):
    half = ROPE // 2
    return (
        values * own
        - pltpu.roll(values, LANES - half, 1) * ahead
        - pltpu.roll(values, half, 1) * behind
    )


def lay_out(devices, inverse_ref, mine_ref, other_ref, win_ref, wup_ref, gains_ref):
    plane, size = mine_ref.shape[:2]
    width, side = win_ref.shape
    rows, ups, pieces = width // devices, wup_ref.shape[0] // devices, wup_ref.shape[1] // TILE
    line = size // rows
    gains = [jnp.zeros((1, width), F32)] * 2
    source = lambda rows, columns: lax.broadcasted_iota(jnp.int32, (rows, columns), 0)
    target = lambda rows, columns: lax.broadcasted_iota(jnp.int32, (rows, columns), 1)
    share = width // devices
    spread = (source(LANES, width) == target(LANES, width) % share).astype(BF)
    for place in range(inverse_ref.shape[0]):
        ref = mine_ref if place < plane else other_ref
        block = ref[place % plane]
        index = inverse_ref[place]
        win_ref[pl.ds(pl.multiple_of(index * size, size), size), :] = block[:, :side]
        for z in range(line):
            start = pl.multiple_of((index * line + z) * ups, ups)
            for piece in range(pieces):
                row = z * rows + piece * ups
                columns = slice(piece * TILE, (piece + 1) * TILE)
                wup_ref[pl.ds(start, ups), columns] = block[row : row + ups, side : side + TILE]
        spots = block[:, side + TILE :]
        for which in range(2):
            pick = (target(line, size) == source(line, size) * rows + which).astype(BF)
            found = dot(dot(pick, spots, NN).astype(BF), spread, NN)
            here = target(line, width) // share == source(line, width) + index * line
            gains[which] += jnp.sum(jnp.where(here, found, 0.0), axis=0, keepdims=True)
    gains_ref[...] = jnp.concatenate(gains, axis=0)


def project_kernel(devices, *refs):
    if devices:
        inverse_ref, x_ref, mine_ref, other_ref = refs[:4]
        own_ref, ahead_ref, behind_ref, a1_ref, q_ref, k_ref, v_ref, c_ref, win_ref, wup_ref, gains_ref = refs[4:]

        @pl.when(pl.program_id(0) == 0)
        def _():
            lay_out(devices, inverse_ref, mine_ref, other_ref, win_ref, wup_ref, gains_ref)
    else:
        x_ref, win_ref, wup_ref, gains_ref = refs[1:5]
        own_ref, ahead_ref, behind_ref, a1_ref, q_ref, k_ref, v_ref, c_ref = refs[5:]
    tables = (own_ref[...], ahead_ref[...], behind_ref[...])
    x = x_ref[...].astype(F32)
    inverse = lax.rsqrt(jnp.mean(x * x, axis=1, keepdims=True) + EPSILON_NORM)
    a1 = (x * inverse * gains_ref[:1, :]).astype(BF)
    a1_ref[...] = a1
    joined = dot(a1, win_ref[...], NN)
    for pair in range(PAIRS):
        lanes = slice(pair * LANES, (pair + 1) * LANES)
        q_ref[:, lanes] = rotate(joined[:, lanes], *tables).astype(BF)
    c = joined[:, QUERY_WIDTH:].astype(BF)
    c_ref[...] = c
    for head in range(LATENT_HEADS):
        latent = slice(head * LATENT_WIDTH, (head + 1) * LATENT_WIDTH)
        both = dot(c[:, latent], wup_ref[latent, :], NN)
        for pair in range(PAIRS_PER_LATENT):
            lanes = slice(pair * LANES, (pair + 1) * LANES)
            out = slice(head * GROUP_WIDTH + pair * LANES, head * GROUP_WIDTH + (pair + 1) * LANES)
            k_ref[:, out] = rotate(both[:, lanes], *tables).astype(BF)
        out = slice(head * GROUP_WIDTH, (head + 1) * GROUP_WIDTH)
        v_ref[:, out] = both[:, GROUP_WIDTH:].astype(BF)


def project(devices, inverse, x, tables, *weights):
    length, width = x.shape
    tile = min(256, length)
    latents = LATENT_HEADS * LATENT_WIDTH
    rows = lambda columns: pl.BlockSpec((tile, columns), lambda i, *_: (i, 0))
    shape = lambda columns: jax.ShapeDtypeStruct((length, columns), BF)
    out_specs = [rows(width), rows(QUERY_WIDTH), rows(QUERY_WIDTH), rows(QUERY_WIDTH), rows(latents)]
    out_shape = [shape(width), shape(QUERY_WIDTH), shape(QUERY_WIDTH), shape(QUERY_WIDTH), shape(latents)]
    if devices:
        more = [((width, QUERY_WIDTH + latents), BF), ((latents, 2 * GROUP_WIDTH), BF), ((2, width), F32)]
        out_specs += [resident(*s) for s, _ in more]
        out_shape += [jax.ShapeDtypeStruct(*s) for s in more]
    return pl.pallas_call(
        functools.partial(project_kernel, devices),
        grid_spec=pltpu.PrefetchScalarGridSpec(
            num_scalar_prefetch=1,
            grid=(length // tile,),
            in_specs=[rows(width)] + [resident(*w.shape) for w in weights] + [rows(LANES)] * 3,
            out_specs=out_specs,
        ),
        out_shape=out_shape,
        compiler_params=pltpu.CompilerParams(vmem_limit_bytes=60 * MIB),
        cost_estimate=cost(20),
        name="project",
    )(inverse, x, *weights, *tables)


def halves(pair, axis):
    first = lax.broadcasted_iota(jnp.int32, pair.shape, axis) < HD
    zero = jnp.zeros_like(pair)
    return (jnp.where(first, pair, zero), jnp.where(first, zero, pair))


def not_after(block):
    keys = lax.broadcasted_iota(jnp.int32, (block, block), 0)
    queries = lax.broadcasted_iota(jnp.int32, (block, block), 1)
    return keys <= queries


def attention_kernel(q_ref, k_ref, v_ref, o_ref, log_ref):
    length = q_ref.shape[0]
    block = min(256, length)
    values = halves(v_ref[...].T, 0)
    for start in range(0, length, block):
        stop = start + block
        queries = halves(q_ref[start:stop, :], 1)
        probs = []
        for head in range(2):
            scores = dot(k_ref[:stop, :], queries[head], NT) * (SCALE * LOG2E)
            last = jnp.where(not_after(block), scores[start:, :], -1e30)
            scores = jnp.concatenate([scores[:start, :], last], axis=0) if start else last
            peak = jnp.max(scores, axis=0, keepdims=True)
            expo = jnp.exp2(scores - peak)
            total = jnp.sum(expo, axis=0, keepdims=True)
            log_ref[0, head : head + 1, start:stop] = peak + jnp.log2(total)
            probs.append((expo * (1.0 / total)).astype(BF))
        mixed = dot(values[0][:, :stop], probs[0], NN) + dot(values[1][:, :stop], probs[1], NN)
        o_ref[start:stop, :] = mixed.T.astype(BF)


def attention(q, k, v):
    length, width = q.shape
    spec = pl.BlockSpec((length, LANES), lambda i: (0, i))
    logs = pl.BlockSpec((1, 2, length), lambda i: (i, 0, 0))
    return pl.pallas_call(
        attention_kernel,
        grid=(PAIRS,),
        in_specs=[spec] * 3,
        out_specs=[spec, logs],
        out_shape=[
            jax.ShapeDtypeStruct((length, width), BF),
            jax.ShapeDtypeStruct((PAIRS, 2, length), F32),
        ],
        compiler_params=pltpu.CompilerParams(vmem_limit_bytes=60 * MIB),
        cost_estimate=cost(1),
        name="attention",
    )(q, k, v)


def attention_back_kernel(q_ref, k_ref, v_ref, o_ref, do_ref, log_ref, own_ref, ahead_ref, behind_ref,
                          dq_ref, dk_ref, dv_ref, total_ref):
    length = q_ref.shape[0]
    block = min(256, length)
    tables = lambda rows: (own_ref[rows, :], ahead_ref[rows, :], behind_ref[rows, :])
    product = (do_ref[...].astype(F32) * o_ref[...].astype(F32)).T
    deltas = (
        jnp.sum(product[:HD], axis=0, keepdims=True),
        jnp.sum(product[HD:], axis=0, keepdims=True),
    )
    keys = halves(k_ref[...].T, 0)
    for start in range(0, length, block):
        stop = start + block
        queries = halves(q_ref[start:, :], 1)
        grads = halves(do_ref[start:, :], 1)
        dk = dv = dq = None
        for head in range(2):
            scores = dot(k_ref[start:stop, :], queries[head], NT) * (SCALE * LOG2E)
            probs = jnp.exp2(scores - log_ref[0, head : head + 1, start:])
            first = jnp.where(not_after(block), probs[:, :block], 0.0)
            probs = jnp.concatenate([first, probs[:, block:]], axis=1) if stop < length else first
            dprobs = dot(v_ref[start:stop, :], grads[head], NT)
            dscores = (probs * (dprobs - deltas[head][:, start:])).astype(BF)
            parts = (
                dot(probs.astype(BF), grads[head], NN),
                dot(dscores, queries[head], NN),
                dot(keys[head][:, start:stop], dscores, NN),
            )
            dv = parts[0] if dv is None else dv + parts[0]
            dk = parts[1] if dk is None else dk + parts[1]
            dq = parts[2] if dq is None else dq + parts[2]
        dv_ref[start:stop, :] = dv.astype(BF)
        dk_ref[start:stop, :] = unrotate(dk * SCALE, *tables(slice(start, stop))).astype(BF)
        if start == 0:
            total_ref[...] = dq
        else:
            total_ref[:, start:] += dq
    dq_ref[...] = unrotate(total_ref[...].T * SCALE, *tables(slice(None))).astype(BF)


def attention_back(weight, start, count, q, k, v, o, do, logs, tables):
    length = q.shape[0]
    spec = pl.BlockSpec((length, LANES), lambda i: (0, i + start))
    out = pl.BlockSpec((length, LANES), lambda i: (0, i))
    log = pl.BlockSpec((1, 2, length), lambda i: (i + start, 0, 0))
    return pl.pallas_call(
        attention_back_kernel,
        grid=(count,),
        in_specs=[spec] * 5 + [log] + [resident(length, LANES)] * 3,
        out_specs=[out] * 3,
        out_shape=[jax.ShapeDtypeStruct((length, count * LANES), BF)] * 3,
        scratch_shapes=[pltpu.VMEM((LANES, length), F32)],
        compiler_params=pltpu.CompilerParams(vmem_limit_bytes=60 * MIB),
        cost_estimate=cost(weight),
        name="attention_back",
    )(q, k, v, o, do, logs, *tables)


def place_rows(target_ref, columns, values, order_ref):
    blocks = order_ref.shape[0]
    size = values.shape[1] // blocks
    for block in range(blocks):
        start = pl.multiple_of(order_ref[block] * size, size)
        target_ref[pl.ds(start, size), columns] = values[:, block * size : (block + 1) * size].T


def natural_rows(target_ref, piece_refs, places, inverse_ref):
    size = target_ref.shape[0] // inverse_ref.shape[0]
    for ref, (_, entries) in zip(piece_refs, places):
        for number, (place, row) in enumerate(entries):
            start = pl.multiple_of(inverse_ref[place] * size + row, math.gcd(size, row or size))
            target_ref[pl.ds(start, ref.shape[1]), :] = ref[number]


def natural_copies(target_ref, piece_refs, places, inverse_ref, sems, first, last):
    size = target_ref.shape[0] // inverse_ref.shape[0]
    starts = sorted({column for column, _ in places})
    copy = lambda ref, number, column, block: pltpu.make_async_copy(
        ref.at[number],
        target_ref.at[pl.ds(block * size, size), pl.ds(column, ref.shape[2])],
        sems.at[block, starts.index(column)],
    )

    def start():
        for ref, (column, entries) in zip(piece_refs, places):
            for number, (place, _) in enumerate(entries):
                block = inverse_ref[place]

                @pl.when((block >= first) & (block <= last))
                def _():
                    copy(ref, number, column, block).start()

    def wait(block):
        for column in starts:
            ref = next(ref for ref, (at, _) in zip(piece_refs, places) if at == column)
            copy(ref, 0, column, block).wait()

    return start, wait


def feed_forward_kernel(first, start, count, places, order_ref, inverse_ref, *refs):
    out_places, w_places, d_places = places
    out_refs, refs = refs[: len(out_places)], refs[len(out_places) :]
    w_refs, refs = refs[: len(w_places)], refs[len(w_places) :]
    d_refs, refs = refs[: len(d_places)], refs[len(d_places) :]
    og_ref, factor_ref, gain_ref, o_ref = refs[:4]
    if first:
        x_ref, h_out, acc_ref, da2_ref, own_ref, send_ref, gd_ref, h_ref = refs[4:12]
        refs = refs[12:]
    else:
        h_ref, acc_in, da2_in = refs[4:7]
        mixed_out, dh_out, do_out, own_ref, send_ref, gd_ref, dgain_ref = refs[8:15]
        acc_ref, da2_ref, acc_old_ref, da2_old_ref, mixed_ref, do_ref = refs[15:21]
        refs = refs[21:]
    wout_ref, w_ref, wd_ref, a2_ref, a2t_ref, dyb_ref, hid_ref, dgu_ref, sems, more_sems = refs
    step = pl.program_id(0)
    steps = pl.num_programs(0)
    length, width = og_ref.shape
    chunk = gd_ref.shape[0]
    side = width // 2
    tile, big = min(256, length), min(1024, length)
    gain = gain_ref[...]
    copy = lambda source, target, number: pltpu.make_async_copy(source, target, more_sems.at[number])
    block_size = wd_ref.shape[0] // inverse_ref.shape[0]
    block_first, block_last = start * chunk // block_size, ((start + count) * chunk - 1) // block_size
    fetch, arrived = natural_copies(wd_ref, d_refs, d_places, inverse_ref, sems, block_first, block_last)

    @pl.when(step == 0)
    def _():
        fetch()
        if not first:
            copy(acc_in, acc_old_ref, 0).start()
            copy(da2_in, da2_old_ref, 1).start()
        natural_rows(wout_ref, out_refs, out_places, inverse_ref)
        for m in range(0, length, tile):
            rows = pl.ds(m, tile)
            if first:
                h = x_ref[rows, :].astype(F32) + dot(o_ref[rows, :], wout_ref[...], NN)
                h_ref[rows, :] = h
                acc_ref[rows, :] = h
            else:
                h = h_ref[rows, :]
                acc_ref[rows, :] = jnp.zeros((tile, width), F32)
            da2_ref[rows, :] = jnp.zeros((tile, width), F32)
            inverse = lax.rsqrt(jnp.mean(h * h, axis=1, keepdims=True) + EPSILON_NORM)
            a2 = (h * inverse * gain).astype(BF)
            a2_ref[rows, :] = a2
            place_rows(a2t_ref, rows, a2, order_ref)
            dyb_ref[rows, :] = (og_ref[rows, :].astype(F32) * factor_ref[rows, :]).astype(BF)
        if first:
            copy(h_ref, h_out, 0).start()

    for block in range(block_first, block_last + 1):

        @pl.when(step == max(0, block * block_size // chunk - start))
        def _():
            arrived(block)

    def one_chunk():
        natural_rows(w_ref, w_refs, w_places, inverse_ref)
        down = wd_ref[pl.ds(pl.multiple_of((start + step) * chunk, chunk), chunk), :]
        for m in range(0, length, big):
            rows = pl.ds(m, big)
            gate = dot(a2_ref[rows, :], w_ref[:, :chunk], NN)
            up = dot(a2_ref[rows, :], w_ref[:, chunk:], NN)
            dhid = dot(dyb_ref[rows, :], down, NT)
            sig = 1.0 / (1.0 + jnp.exp2(gate * -LOG2E))
            act = gate * sig
            hid_ref[rows, :] = (act * up).astype(BF)
            dgu_ref[rows, :chunk] = (dhid * up * (sig + act * (1.0 - sig))).astype(BF)
            dgu_ref[rows, chunk:] = (dhid * act).astype(BF)
        for m in range(0, length, big):
            rows = pl.ds(m, big)
            acc_ref[rows, :] += dot(hid_ref[rows, :], down, NN)
            da2_ref[rows, :] += dot(dgu_ref[rows, :], w_ref[...], NT)
        gd_ref[...] = dot(hid_ref[...], dyb_ref[...], TN).astype(BF)
        own_ref[...] = dot(a2t_ref[:side, :], dgu_ref[...], NN).astype(BF)
        send_ref[...] = dot(a2t_ref[side:, :], dgu_ref[...], NN).astype(BF)

    if first:
        one_chunk()

        @pl.when(step == steps - 1)
        def _():
            copy(h_ref, h_out, 0).wait()

        return
    tail = steps - 2
    pl.when(step < tail)(one_chunk)

    @pl.when(step == tail)
    def _():
        copy(acc_in, acc_old_ref, 0).wait()
        copy(da2_in, da2_old_ref, 1).wait()
        total = jnp.zeros((1, width), F32)
        for m in range(0, length, tile):
            rows = pl.ds(m, tile)
            mixed_ref[rows, :] = (acc_old_ref[rows, :] + acc_ref[rows, :]).astype(BF)
            h = h_ref[rows, :]
            inverse = lax.rsqrt(jnp.mean(h * h, axis=1, keepdims=True) + EPSILON_NORM)
            hat = h * inverse
            da2 = da2_old_ref[rows, :] + da2_ref[rows, :]
            total = total + jnp.sum(da2 * hat, axis=0, keepdims=True)
            scaled = da2 * gain
            dy = og_ref[rows, :].astype(F32) * factor_ref[rows, :]
            dh = dy + inverse * (scaled - hat * jnp.mean(scaled * hat, axis=1, keepdims=True))
            acc_ref[rows, :] = dh
            low = dh.astype(BF)
            dyb_ref[rows, :] = low
            do_ref[rows, :] = dot(low, wout_ref[...], NT).astype(BF)
            place_rows(a2t_ref, rows, o_ref[rows, :], order_ref)
        dgain_ref[...] = total
        copy(mixed_ref, mixed_out, 2).start()
        copy(acc_ref, dh_out, 3).start()
        copy(do_ref, do_out, 4).start()

    for tile_number in range(2):

        @pl.when(step == tail + tile_number)
        def _():
            half = width // 2
            grads = dyb_ref[:, tile_number * half : (tile_number + 1) * half]
            own_ref[...] = dot(a2t_ref[:side, :], grads, NN).astype(BF)
            send_ref[...] = dot(a2t_ref[side:, :], grads, NN).astype(BF)

    @pl.when(step == steps - 1)
    def _():
        copy(mixed_ref, mixed_out, 2).wait()
        copy(acc_ref, dh_out, 3).wait()
        copy(do_ref, do_out, 4).wait()


def feed_forward(order, inverse, start, count, skip, state, x, o, out_grad, factor, gain, out_pieces, pieces, down_pieces):
    length, width = out_grad.shape
    chunk = CHUNK
    first = state is None
    steps = count if first else count + 2
    last = count - 1
    rows = pl.BlockSpec((chunk, width), lambda i, *_: (start + jnp.minimum(i, last), 0))
    columns = pl.BlockSpec((width // 2, TILE), lambda i, *_: (0, i))
    whole = lambda *s: pl.BlockSpec(s, lambda i, *_: (0,) * len(s), pipeline_mode=pl.Buffered(1))
    anywhere = pl.BlockSpec(memory_space=pl.ANY)
    shape = jax.ShapeDtypeStruct
    (outs, out_places), (tiles, w_places), (downs, d_places) = out_pieces, pieces, down_pieces
    big = whole(length, width)
    full, low = pltpu.VMEM((length, width), F32), pltpu.VMEM((length, width), BF)
    scratch = [
        pltpu.VMEM((width, width), BF),
        pltpu.VMEM((width, TILE), BF),
        pltpu.VMEM((FF, width), BF),
        low,
        pltpu.VMEM((width, length), BF),
        low,
        pltpu.VMEM((length, chunk), BF),
        pltpu.VMEM((length, TILE), BF),
        pltpu.SemaphoreType.DMA((inverse.shape[0], 2)),
        pltpu.SemaphoreType.DMA((5,)),
    ]
    in_specs = [whole(*piece.shape[:2], width) for piece in outs]
    in_specs += [
        pl.BlockSpec((*piece.shape[:2], TILE), lambda i, *_: (0, 0, skip + jnp.minimum(i, last))) for piece in tiles
    ]
    in_specs += [anywhere] * len(downs)
    in_specs += [big, whole(length, 1), whole(1, width), big]
    operands = [*outs, *tiles, *downs, out_grad, factor, gain, o]
    halves_out = [shape((width // 2, steps * TILE), BF)] * 2
    aliases = {}
    if first:
        in_specs += [big]
        operands += [x]
        out_specs = [anywhere, big, big, columns, columns, rows]
        out_shape = [shape((length, width), F32)] * 3 + halves_out + [shape((FF, width), BF)]
        scratch = [full] + scratch
    else:
        in_specs += [big, anywhere, anywhere, anywhere]
        operands += list(state)
        out_specs = [anywhere, anywhere, anywhere, columns, columns, rows, whole(1, width)]
        out_shape = [shape((length, width), BF), shape((length, width), F32), shape((length, width), BF)]
        out_shape += halves_out + [shape((FF, width), BF), shape((1, width), F32)]
        scratch = [full, full, full, full, low, low] + scratch
        aliases = {len(operands) + 1: 5}
    return pl.pallas_call(
        functools.partial(feed_forward_kernel, first, start, count, (out_places, w_places, d_places)),
        grid_spec=pltpu.PrefetchScalarGridSpec(
            num_scalar_prefetch=2, grid=(steps,), in_specs=in_specs, out_specs=out_specs, scratch_shapes=scratch
        ),
        out_shape=out_shape,
        input_output_aliases=aliases,
        compiler_params=pltpu.CompilerParams(vmem_limit_bytes=63 * MIB),
        cost_estimate=cost(40),
        name="feed_forward",
    )(order, inverse, *operands)


def unproject_kernel(devices, order_ref, a1_ref, c_ref, dq_ref, dk_ref, dv_ref, wup_ref, *refs):
    dc_ref, own_ref, send_ref = refs[:3]
    a1t_ref = refs[-1]
    head = pl.program_id(0)
    length, width = a1_ref.shape
    half = width // 2
    tile = min(256, length)

    @pl.when(head == 0)
    def _():
        for m in range(0, length, tile):
            place_rows(a1t_ref, pl.ds(m, tile), a1_ref[m : m + tile, :], order_ref)

    dq, dk, dv = dq_ref[...], dk_ref[...], dv_ref[...]
    dc = (dot(dk, wup_ref[:, :GROUP_WIDTH], NT) + dot(dv, wup_ref[:, GROUP_WIDTH:], NT)).astype(BF)
    dc_ref[...] = dc
    grads = [
        (ref, start, size, dot(a1t_ref[rows, :], grad, NN).astype(BF))
        for ref, rows in ((own_ref, slice(half)), (send_ref, slice(half, width)))
        for start, size, grad in ((0, GROUP_WIDTH, dq), (QUERY_WIDTH, LATENT_WIDTH, dc))
    ]
    for which in range(LATENT_HEADS):

        @pl.when(head == which)
        def _():
            for ref, start, size, grad in grads:
                ref[:, start + which * size : start + (which + 1) * size] = grad

    turned = c_ref[...].T
    sides = [dot(turned, grad, NN).astype(BF) for grad in (dk, dv)]
    if not devices:
        refs[3][:, :GROUP_WIDTH], refs[3][:, GROUP_WIDTH:] = sides
        return
    all_ref = refs[3]
    side = QUERY_WIDTH + LATENT_HEADS * LATENT_WIDTH
    rows, ups = width // devices, wup_ref.shape[0] * LATENT_HEADS // devices
    blocks = order_ref.shape[0] // LATENT_HEADS
    line = devices // order_ref.shape[0]
    for block in range(blocks):
        place = order_ref[head * blocks + block]
        for z in range(line):
            device = block * line + z
            for piece, value in enumerate(sides):
                start = pl.multiple_of(place * (line * rows) + (z * rows + piece * ups), ups)
                all_ref[pl.ds(start, ups), :] = value[device * ups : (device + 1) * ups, :]

    @pl.when(head == LATENT_HEADS - 1)
    def _():
        own_ref[:, side:] = all_ref[:half, :]
        send_ref[:, side:] = all_ref[half:, :]


def unproject(devices, order, a1, c, dq, dk, dv, w_up):
    length, width = a1.shape
    latents = LATENT_HEADS * LATENT_WIDTH
    half = width // 2
    columns = lambda rows, size: pl.BlockSpec((rows, size), lambda g, *_: (0, g))
    up = pl.BlockSpec((LATENT_WIDTH, 2 * GROUP_WIDTH), lambda g, *_: (g, 0))
    group = columns(length, GROUP_WIDTH)
    both = QUERY_WIDTH + latents + (TILE if devices else 0)
    outs = [(length, latents)] + [(half, both)] * 2
    out_specs = [columns(length, LATENT_WIDTH)] + [resident(half, both)] * 2
    scratch = [pltpu.VMEM((width, length), BF)]
    if devices:
        scratch = [pltpu.VMEM((width, TILE), BF)] + scratch
    else:
        outs.append(w_up.shape)
        out_specs.append(up)
    return pl.pallas_call(
        functools.partial(unproject_kernel, devices),
        grid_spec=pltpu.PrefetchScalarGridSpec(
            num_scalar_prefetch=1,
            grid=(LATENT_HEADS,),
            in_specs=[resident(length, width), columns(length, LATENT_WIDTH), group, group, group, up],
            out_specs=out_specs,
            scratch_shapes=scratch,
        ),
        out_shape=[jax.ShapeDtypeStruct(s, BF) for s in outs],
        compiler_params=pltpu.CompilerParams(vmem_limit_bytes=60 * MIB),
        cost_estimate=cost(20),
        name="unproject",
    )(order, a1, c, dq, dk, dv, w_up)


def input_grad_kernel(x_ref, dh_ref, dq_ref, dc_ref, gain_ref, win_ref, out_ref, dgain_ref):
    x = x_ref[...].astype(F32)
    inverse = lax.rsqrt(jnp.mean(x * x, axis=1, keepdims=True) + EPSILON_NORM)
    hat = x * inverse
    da1 = dot(dq_ref[...], win_ref[:, :QUERY_WIDTH], NT) + dot(dc_ref[...], win_ref[:, QUERY_WIDTH:], NT)
    part = jnp.sum(da1 * hat, axis=0, keepdims=True)
    scaled = da1 * gain_ref[...].astype(F32)
    out_ref[...] = (
        dh_ref[...] + inverse * (scaled - hat * jnp.mean(scaled * hat, axis=1, keepdims=True))
    ).astype(BF)

    @pl.when(pl.program_id(0) == 0)
    def _():
        dgain_ref[...] = part

    @pl.when(pl.program_id(0) > 0)
    def _():
        dgain_ref[...] += part


def input_grad(x, dh, dql, gain, w_in):
    dq, dc = dql
    length, width = x.shape
    tile = min(256, length)
    rows = lambda columns: pl.BlockSpec((tile, columns), lambda i: (i, 0))
    return pl.pallas_call(
        input_grad_kernel,
        grid=(length // tile,),
        in_specs=[rows(width), rows(width), rows(dq.shape[1]), rows(dc.shape[1]), resident(1, width), resident(*w_in.shape)],
        out_specs=[rows(width), resident(1, width)],
        out_shape=[jax.ShapeDtypeStruct((length, width), BF), jax.ShapeDtypeStruct((1, width), F32)],
        compiler_params=pltpu.CompilerParams(vmem_limit_bytes=60 * MIB),
        cost_estimate=cost(20),
        name="input_grad",
    )(x, dh, dq, dc, gain, w_in)


class Ring:
    def __init__(self, data, line):
        self.cores = 2 if data % 2 == 0 else 1
        self.plane, self.line = data // self.cores, line
        place = lax.axis_index("dp")
        self.core, self.at, self.z = place % self.cores, place // self.cores, lax.axis_index("fsdp")

    def partner(self, index, shift, count):
        if count & (count - 1) == 0:
            return index ^ shift
        return (index + shift) % count

    def send_core(self, value):
        swap = [(i, i ^ 1) for i in range(self.plane * 2)]
        return lax.ppermute(value, "dp", swap)

    def send_plane(self, value, shift):
        pairs = [
            (p * self.cores + c, self.partner(p, shift, self.plane) * self.cores + c)
            for p in range(self.plane)
            for c in range(self.cores)
        ]
        return lax.ppermute(value, "dp", pairs)

    def send_line(self, value, shift):
        return lax.ppermute(value, "fsdp", [(i, (i + shift) % self.line) for i in range(self.line)])


def take(array, index, axis):
    return lax.dynamic_index_in_dim(array, index, axis, keepdims=False)


def core_blocks(ring, grad, core):
    rows = grad.shape[0] // (ring.plane * ring.cores * ring.line)
    return take(grad.reshape(ring.plane, ring.cores, ring.line, rows, grad.shape[1]), core, 1)


def total(parts):
    return sum(part.astype(F32) for part in parts)


def core_sends(ring, value):
    return [(ring.send_core, value)]


def plane_sends(ring, parts, relative):
    spot = lambda shift: shift if relative else ring.partner(ring.at, shift, ring.plane)
    block = lambda shift: total([take(part, spot(shift), 0) for part in parts]).astype(BF)
    sends = [
        (lambda value, shift=shift: ring.send_plane(value, shift), block(shift)) for shift in range(1, ring.plane)
    ]
    return block(0), sends


def cross_sends(ring, grad, bit, left):
    axis = len(left) - 1 - left.index(bit)
    side = (ring.at >> bit) & 1
    send = lambda value: ring.send_plane(value, 1 << bit)
    return take(grad, side, axis), [(send, take(grad, 1 - side, axis).astype(BF))]


def line_sends(ring, grad, bit, axis=0):
    shape = grad.shape
    pairs = grad.reshape(*shape[:axis], shape[axis] // 2, 2, *shape[axis + 1 :])
    side = (ring.z >> bit) & 1
    swap = [(i, i ^ (1 << bit)) for i in range(ring.line)]
    give = take(pairs, 1 - side, axis + 1).astype(BF)
    return take(pairs, side, axis + 1), [(lambda value: lax.ppermute(value, "fsdp", swap), give)]


def beside(sends, kept, kernel=None, *inputs):
    inputs, gives, kept = together(inputs, [give for _, give in sends], kept)
    received = [send(give) for (send, _), give in zip(sends, gives)]
    return together(kernel(*inputs) if kernel else (), received, kept)


def line_rest(ring, grads, done):
    for bit in range(done, ring.line.bit_length() - 1):
        kept, sends = zip(*(line_sends(ring, grad, bit) for grad in grads))
        _, received, kept = beside([send for one in sends for send in one], kept)
        grads = [total(pair) for pair in zip(kept, received)]
    return [grad[0] for grad in grads]


def halves_order(ring):
    blocks = jnp.arange(ring.plane * ring.cores)
    plane, core = blocks // ring.cores, blocks % ring.cores
    if ring.plane & (ring.plane - 1) == 0:
        shift = plane ^ ring.at
    else:
        shift = (plane - ring.at) % ring.plane
    order = (((core - ring.core) % ring.cores) * ring.plane + shift).astype(jnp.int32)
    shift, core = blocks % ring.plane, blocks // ring.plane
    if ring.plane & (ring.plane - 1) == 0:
        plane = shift ^ ring.at
    else:
        plane = (shift + ring.at) % ring.plane
    inverse = (plane * ring.cores + (core + ring.core) % ring.cores).astype(jnp.int32)
    return order, inverse


class Gather:
    def __init__(self, ring, piece, by_columns=False):
        self.ring, self.by_columns = ring, by_columns
        self.block = piece[None]
        self.bits = list(range(ring.line.bit_length() - 1))[::-1]

    def line_sends(self):
        swap = [(i, i ^ (1 << self.bits[0])) for i in range(self.ring.line)]
        return [(lambda value: lax.ppermute(value, "fsdp", swap), self.block)]

    def line_receive(self, values):
        low = ((self.ring.z >> self.bits.pop(0)) & 1) == 0
        pair = [jnp.where(low, self.block, values[0]), jnp.where(low, values[0], self.block)]
        block = jnp.stack(pair, axis=1)
        self.block = block.reshape(-1, *block.shape[2:])
        if not self.bits:
            self.split()

    def split(self):
        line, rows, columns = self.block.shape
        count = self.ring.plane.bit_length() - 1
        if self.by_columns:
            cut = columns // 2
            halves = [self.block[..., :cut].reshape(1, -1, cut), self.block[..., cut:].reshape(1, -1, cut)]
            self.offsets = [(0, 0), (cut, 0)]
        else:
            whole = self.block.reshape(-1, columns)
            cut = whole.shape[0] // 2
            halves = [whole[None, :cut], whole[None, cut:]]
            self.offsets = [(0, 0), (0, cut)]
        self.halves = [([half], [[0]]) for half in halves]
        self.orders = [list(range(count)), list(range(count))[::-1]]

    def plane_sends(self):
        sends = []
        for (arrays, _), order in zip(self.halves, self.orders):
            value = jnp.concatenate(arrays, axis=0) if len(arrays) > 1 else arrays[0]
            sends.append((lambda value, bit=order[0]: self.ring.send_plane(value, 1 << bit), value))
        return sends

    def plane_receive(self, values):
        for (arrays, shifts), order, value in zip(self.halves, self.orders, values):
            bit = order.pop(0)
            shifts.append([shift ^ (1 << bit) for have in shifts for shift in have])
            arrays.append(value)

    def direct_sends(self):
        self.offsets = [(0, 0)]
        block = self.block.reshape(1, -1, self.block.shape[-1])
        self.halves = [([block], [[0]])]
        return [(lambda value, k=k: self.ring.send_plane(value, k), block) for k in range(1, self.ring.plane)]

    def direct_receive(self, values):
        for shift, value in enumerate(values, 1):
            self.halves[0][0].append(value)
            self.halves[0][1].append([shift])

    def arrays(self):
        return [array for arrays, _ in self.halves for array in arrays]

    def hold(self, arrays):
        arrays = list(arrays)
        for mine, _ in self.halves:
            for number in range(len(mine)):
                mine[number] = arrays.pop(0)

    def places(self, core):
        return [
            (column, [(core * self.ring.plane + shift, row) for shift in have])
            for (_, shifts), (column, row) in zip(self.halves, self.offsets)
            for have in shifts
        ]

    def pieces(self, other):
        if self.ring.cores == 1:
            return self.arrays(), self.places(0)
        return self.arrays() + list(other), self.places(0) + self.places(1)

    def stacked(self):
        blocks = [{}, {}]
        for found, (arrays, shifts) in zip(blocks, self.halves):
            for array, have in zip(arrays, shifts):
                found.update(zip(have, array))
        return jnp.stack([jnp.concatenate([found[k] for found in blocks], axis=0) for k in range(self.ring.plane)])


def natural(ring, mine, other):
    if ring.plane & (ring.plane - 1) == 0:
        shifts = [ring.at ^ at for at in range(ring.plane)]
    else:
        shifts = [(ring.at - at) % ring.plane for at in range(ring.plane)]
    blocks = []
    for shift in shifts:
        pair = [choose(shift, list(part)) for part in (mine, other)][: ring.cores]
        blocks += [choose((core - ring.core) % ring.cores, pair) for core in range(ring.cores)]
    return jnp.stack(blocks)


def choose(index, options):
    result = options[0]
    for number, option in enumerate(options[1:], 1):
        result = jnp.where(index == number, option, result)
    return result


def sum_all(ring, value):
    if ring.cores == 2:
        value = value + ring.send_core(value)
    for count, send in ((ring.plane, ring.send_plane), (ring.line, None)):
        if count & (count - 1):
            return lax.psum(value, AXES)
    shift = 1
    while shift < ring.plane:
        value = value + ring.send_plane(value, shift)
        shift *= 2
    shift = 1
    while shift < ring.line:
        swap = [(i, i ^ shift) for i in range(ring.line)]
        value = value + lax.ppermute(value, "fsdp", swap)
        shift *= 2
    return value


def adamw_kernel(message_ref, dgains_ref, a_ref, b_ref, c_ref, d_ref, *refs):
    masters, firsts, seconds, norm_ref, outs = refs[:6], refs[6:12], refs[12:18], refs[18], refs[19:]
    gains = message_ref[:-8, :]
    norm = jnp.sqrt(message_ref[-1:, :1] + jnp.sum(gains * gains, keepdims=True))
    norm_ref[...] = norm
    clip = jnp.minimum(1.0, MAX_NORM / (norm + 1e-06))

    def update(index, place, grad, rate, decay):
        grad = clip * grad
        master = masters[index][place]
        first_new = BETA_ONE * firsts[index][place] + (1.0 - BETA_ONE) * grad
        second_new = BETA_TWO * seconds[index][place] + (1.0 - BETA_TWO) * grad * grad
        first_hat = first_new / (1.0 - BETA_ONE**STEP)
        second_hat = second_new / (1.0 - BETA_TWO**STEP)
        outs[3 * index][place] = master - rate * (
            first_hat / (jnp.sqrt(second_hat) + EPSILON_ADAM) + decay * master
        )
        outs[3 * index + 1][place] = first_new
        outs[3 * index + 2][place] = second_new

    everything = (slice(None), slice(None))
    side = masters[0].shape[1]
    update(0, everything, c_ref[:, :side], RATE_MATRIX, DECAY_MATRIX)
    rows = masters[1].shape[0]
    for tile in range(masters[1].shape[1] // TILE):
        place = (slice(None), slice(tile * TILE, (tile + 1) * TILE))
        update(1, place, c_ref[tile * rows : (tile + 1) * rows, side:], RATE_MATRIX, DECAY_MATRIX)
    second = FF // CHUNK - FIRST_CHUNKS
    update(2, everything, b_ref[:, second * TILE :], RATE_OUTPUT, DECAY_MATRIX)
    for chunk in range(FF // CHUNK):
        ref, at = (a_ref, chunk) if chunk < FIRST_CHUNKS else (b_ref, chunk - FIRST_CHUNKS)
        for which in range(2):
            place = (slice(None), slice(which * FF + chunk * CHUNK, which * FF + (chunk + 1) * CHUNK))
            start = at * TILE + which * CHUNK
            update(3, place, ref[:, start : start + CHUNK], RATE_MATRIX, DECAY_MATRIX)
    update(4, everything, d_ref[...], RATE_MATRIX, DECAY_MATRIX)
    update(5, everything, dgains_ref[...], RATE_GAIN, 0.0)


def adamw(message, dgains, totals, masters, firsts, seconds):
    shape = jax.ShapeDtypeStruct
    outs = [shape((1, 1), F32)] + [shape(w.shape, F32) for w in masters for _ in range(3)]
    return pl.pallas_call(
        adamw_kernel,
        out_shape=outs,
        compiler_params=pltpu.CompilerParams(vmem_limit_bytes=60 * MIB),
        cost_estimate=cost(5),
        name="adamw",
    )(message, dgains, *totals, *masters, *firsts, *seconds)


def together(*values):
    return lax.optimization_barrier(values)


def shards(data, line, tokens, out_grad, domain_ids, domain_scale, *state):
    masters, moments = state[:6], state[6:]
    firsts, seconds = moments[0::2], moments[1::2]
    ring = Ring(data, line)
    devices = data * line
    length, width = tokens.shape
    p_in, p_up, p_out, p_gate, p_down, p_gains = masters
    latents = LATENT_HEADS * LATENT_WIDTH
    rows = width // devices
    chunks = FF // CHUNK
    columns = lambda a: a.reshape(a.shape[0], -1, TILE).transpose(1, 0, 2).reshape(-1, TILE)

    half = FIRST_CHUNKS
    one = jnp.concatenate([p_in, columns(p_up).reshape(rows, -1), lane_pad(p_gains, rows)], axis=1).astype(BF)
    one = Gather(ring, one)
    order, inverse = halves_order(ring)

    def early(domain_ids, p_out, p_gate, p_down):
        picked = domain_ids[:, None] == jnp.arange(NDOM)[None, :]
        factor = jnp.sum(jnp.where(picked, domain_scale[None, :], 0.0), axis=1, keepdims=True)
        tiles = p_gate.astype(BF).reshape(rows, 2, chunks, CHUNK).transpose(0, 2, 1, 3).reshape(rows, -1)
        two = jnp.concatenate([p_out.astype(BF), tiles[:, : half * TILE]], axis=1)
        return rotation_tables(length), factor, two, p_down.astype(BF), tiles[:, half * TILE :]

    out, received, _ = beside(one.line_sends(), (), early, domain_ids, p_out, p_gate, p_down)
    tables, factor, two, down, three = out
    two, down, three = Gather(ring, two), Gather(ring, down, True), Gather(ring, three)
    one.line_receive(received)
    while len(one.bits) > 0:
        one.line_receive(beside(one.line_sends(), ())[1])
    while len(down.bits) > 0 or len(one.orders[0]) > 0:
        sends = one.plane_sends() if len(one.orders[0]) > 0 else []
        split = len(sends)
        sends += down.line_sends() if len(down.bits) > 0 else []
        _, received, kept = beside(sends, one.arrays())
        one.hold(kept)
        if split:
            one.plane_receive(received[:split])
        if len(received) > split:
            down.line_receive(received[split:])
    one_block = one.stacked()
    sends = core_sends(ring, one_block) + down.plane_sends() + two.line_sends()
    _, received, (one_block, kept, tokens) = beside(sends, (one_block, down.arrays(), tokens))
    down.hold(kept)
    one_other = received[0]
    down.plane_receive(received[1:-1])
    two.line_receive(received[-1:])
    other = {}
    core_of = lambda keys: [send for h, r in keys for send in core_sends(ring, down.halves[h][0][r])]
    while len(down.orders[0]) > 0 or len(two.bits) > 0:
        sends = down.plane_sends() if len(down.orders[0]) > 0 else []
        split = len(sends)
        sends += two.line_sends() if len(two.bits) > 0 else []
        middle = len(sends)
        keys = [(0, 0), (1, 0)] if len(other) == 0 else []
        _, received, kept = beside(sends + core_of(keys), down.arrays())
        down.hold(kept)
        other.update(zip(keys, received[middle:]))
        if split:
            down.plane_receive(received[:split])
        if middle > split:
            two.line_receive(received[split:middle])
    aligned = rows % 32 == 0 and p_up.shape[0] % 16 == 0
    if aligned:
        run = lambda tokens: project(devices, inverse, tokens, tables, one_block, one_other)
    else:
        first = natural(ring, one_block, one_other).reshape(devices, rows, -1)
        w_in = first[:, :, : p_in.shape[1]].reshape(width, -1)
        w_up = first[:, :, p_in.shape[1] : p_in.shape[1] + p_up.size // rows]
        w_up = w_up.reshape(devices, 2 * GROUP_WIDTH // TILE, p_up.shape[0], TILE).transpose(0, 2, 1, 3).reshape(latents, -1)
        gains = first[:, :2, -LANES:][:, :, : p_gains.shape[1]].transpose(1, 0, 2).reshape(2, width).astype(F32)
        run = lambda tokens: (*project(0, inverse, tokens, tables, w_in, w_up, gains), w_in, w_up, gains)
    rounds = len(down.halves[0][0])
    rest = [(h, r) for r in range(1, rounds) for h in range(2)]
    sends = two.plane_sends() + three.line_sends()
    split = len(sends)
    out, received, kept = beside(sends + core_of(rest[:2]), (two.arrays(), down.arrays(), other), run, tokens)
    a1, q, k, v, c, w_in, w_up, gains = out
    two.hold(kept[0])
    down.hold(kept[1])
    other = dict(kept[2])
    two.plane_receive(received[:2])
    three.line_receive(received[2:3])
    other.update(zip(rest[:2], received[split:]))
    sends = two.plane_sends() if len(two.orders[0]) > 0 else []
    split = len(sends)
    sends += three.line_sends() if len(three.bits) > 0 else []
    middle = len(sends)
    sends += core_of(rest[2:4])
    (o, logs), received, kept = beside(sends, (two.arrays(), down.arrays(), other), attention, q, k, v)
    two.hold(kept[0])
    down.hold(kept[1])
    other = dict(kept[2])
    if split:
        two.plane_receive(received[:split])
    if middle > split:
        three.line_receive(received[split:middle])
    other.update(zip(rest[2:4], received[middle:]))
    while len(two.orders[0]) > 0:
        two.plane_receive(beside(two.plane_sends(), ())[1])
    while len(three.bits) > 0:
        three.line_receive(beside(three.line_sends(), ())[1])
    sends = core_of(rest[4:])
    split = len(sends)
    sends += [send for array in two.arrays() for send in core_sends(ring, array)]
    _, received, (o, kept, kept_down, other) = beside(sends, (o, two.arrays(), down.arrays(), other))
    two.hold(kept)
    down.hold(kept_down)
    other = dict(other)
    other.update(zip(rest[4:], received[:split]))
    down_pieces = down.pieces([other[h, r] for h in range(2) for r in range(rounds)])
    two_pieces = two.pieces(received[split:])
    common = (tokens, o, out_grad, factor, gains[1:], two_pieces)
    run = lambda o: feed_forward(
        order, inverse, 0, half, width // TILE, None, tokens, o, out_grad, factor, gains[1:], two_pieces, two_pieces, down_pieces
    )
    (h, acc, da2, own_a, send_a, g_down), received, kept = beside(three.direct_sends(), three.arrays(), run, o)
    three.hold(kept)
    three.direct_receive(received)
    blocks = lambda a: a.reshape(ring.plane, ring.line, rows, -1)
    sends = core_sends(ring, blocks(send_a)) + [send for array in three.arrays() for send in core_sends(ring, array)]
    _, received, (h, own_a, kept) = beside(sends, (h, own_a, three.arrays()))
    three.hold(kept)
    three_pieces = three.pieces(received[1:])
    kept_a, sends = plane_sends(ring, [blocks(own_a), received[0]], True)
    state = (acc, da2, g_down)
    run = lambda h: feed_forward(
        order, inverse, half, chunks - half, 0, (h, *state), *common, three_pieces, down_pieces
    )
    out, received, kept_a = beside(sends, kept_a, run, h)
    mixed, dh, do, own_b, send_b, g_down, dgain_two = out

    def run(g_down, kept_a, *came_a):
        kept_a, send_a = line_sends(ring, total([kept_a, *came_a]), 0)
        return core_blocks(ring, g_down, 1 - ring.core), kept_a, send_a[0][1]

    out, came_b, (do, own_b) = beside(core_sends(ring, blocks(send_b)), (do, own_b), run, g_down, kept_a, *received)
    send_d, kept_a, give_a = out
    kept_b, send_b = plane_sends(ring, [blocks(own_b), *came_b], True)
    sends = send_b + core_sends(ring, send_d) + [(line_sends(ring, give_a, 0)[1][0][0], give_a)]
    run = lambda do: attention_back(40, 0, PAIRS, q, k, v, o, do, logs, tables)
    grads, received, (kept_a, kept_b, g_down) = beside(sends, (kept_a, kept_b, g_down), run, do)
    *came_b, came_d, came_a = received
    bits = list(range(ring.plane.bit_length() - 1))
    orders, left = (bits, bits[::-1]), [bits[:], bits[:]]
    halves_d = zip(*(jnp.split(part, 2, axis=-1) for part in (core_blocks(ring, g_down, ring.core), came_d)))
    halves_d = [total(pair) for pair in halves_d]
    halves_d = [half.reshape(*(2,) * len(bits), *half.shape[1:]) for half in halves_d]

    def step_d(number, halves_d):
        kept, sends = zip(*(cross_sends(ring, half, order[number], have) for half, order, have in zip(halves_d, orders, left)))
        for order, have in zip(orders, left):
            have.remove(order[number])
        return kept, [send for one in sends for send in one]

    kept_d, send_d = step_d(0, halves_d)
    kept_a, send_a = line_sends(ring, total([kept_a, came_a]), 1)

    def run(dq, dk, dv):
        dc, own, send, *ups = unproject(devices if aligned else 0, order, a1, c, dq, dk, dv, w_up)
        if not aligned:
            g_up = ups[0].reshape(devices, -1, 2 * GROUP_WIDTH // TILE, TILE).transpose(0, 2, 1, 3).reshape(width, -1)
            spots = lambda core: [
                take(core_blocks(ring, g_up, core), ring.partner(ring.at, k, ring.plane), 0) for k in range(ring.plane)
            ]
            ups = [jnp.stack(spots(core)).reshape(width // 2, -1) for core in (ring.core, 1 - ring.core)]
            own, send = (jnp.concatenate(parts, axis=1) for parts in zip((own, send), ups))
        dql = (dq, dc)
        return dql, own, send

    kept_b, send_b = line_sends(ring, total([kept_b, *came_b]), 0)
    kept = (kept_a, kept_b, kept_d)
    out, received, (kept_a, kept_b, kept_d) = beside(send_d + send_a + send_b, kept, run, *grads)
    dql, own_c, send_c = out
    *came_d, came_a, came_b = received

    def second(kept_d, came_d):
        kept_d, send_d = step_d(1, [total(pair) for pair in zip(kept_d, came_d)])
        return kept_d, [give for _, give in send_d]

    send_d = [(lambda value, bit=order[1]: ring.send_plane(value, 1 << bit)) for order in orders]
    kept = (dql, own_c, kept_a, came_a, kept_b, came_b)
    (kept_d, give_d), came_c, kept = beside(core_sends(ring, blocks(send_c)), kept, second, kept_d, came_d)
    dql, own_c, kept_a, came_a, kept_b, came_b = kept
    run = lambda own_c, *came_c: plane_sends(ring, [blocks(own_c), *came_c], True)[0:1] + tuple(
        give for _, give in plane_sends(ring, [blocks(own_c), *came_c], True)[1]
    )
    kept = (dql, kept_a, came_a, kept_b, came_b, kept_d)
    (kept_c, *gives_c), came_d, kept = beside(list(zip(send_d, give_d)), kept, run, own_c, *came_c)
    dql, kept_a, came_a, kept_b, came_b, kept_d = kept
    send_c = [(lambda value, k=k: ring.send_plane(value, k), give) for k, give in enumerate(gives_c, 1)]
    for number in range(2, len(bits)):
        kept_d, send_d = step_d(number, [total(pair) for pair in zip(kept_d, came_d)])
        _, came_d, kept_d = beside(send_d, kept_d)
    sum_d = jnp.concatenate([total(pair) for pair in zip(kept_d, came_d)], axis=-1)
    kept_a = total([kept_a, came_a])
    kept_b, send_b = line_sends(ring, total([kept_b, came_b]), 1)
    kept_d, send_d = line_sends(ring, sum_d, 0)
    run = lambda dql: input_grad(tokens, dh, dql, gains[:1], w_in)
    kept = (kept_b, kept_c, kept_d)
    (given, dgain_one), received, (kept_b, kept_c, kept_d) = beside(send_c + send_d + send_b, kept, run, dql)
    *came_c, came_d, came_b = received
    kept_b = total([kept_b, came_b])
    kept_c, send_c = line_sends(ring, total([kept_c, *came_c]), 0)
    kept_d, send_d = line_sends(ring, total([kept_d, came_d]), 1)
    _, received, (kept_c, kept_d) = beside(send_c + send_d, (kept_c, kept_d))
    came_c, came_d = received
    sums = [kept_a, kept_b, total([kept_d, came_d])]
    total_a, total_b, total_d = line_rest(ring, sums, 2)
    (total_c,) = line_rest(ring, [total([kept_c, came_c])], 1)

    squares = sum(jnp.sum(grad * grad) for grad in (total_a, total_b, total_c, total_d))
    dgains = jnp.concatenate([dgain_one, dgain_two], axis=0)
    message = jnp.concatenate(
        [dgains.reshape(-1, LANES), jnp.full((8, LANES), squares, F32)], axis=0
    )
    message = sum_all(ring, message)
    share = masters[5].shape[1]
    place = lax.axis_index("dp") * line + lax.axis_index("fsdp")
    dgains = lax.dynamic_slice_in_dim(message[:-8].reshape(2, width), place * share, share, 1)
    totals = (total_a, total_b, total_c, total_d)
    grad_norm, *results = adamw(message, dgains, totals, masters, firsts, seconds)
    return (mixed, given, grad_norm[0, 0], *results)


def lane_pad(gains, rows):
    return jnp.pad(gains, ((0, rows - gains.shape[0]), (0, LANES - gains.shape[1])))


def solution(mesh):
    data, line = mesh.shape["dp"], mesh.shape["fsdp"]
    rows, flat, columns = P(AXES, None), P(AXES), P(None, AXES)

    def run(*arrays):
        return shards(data, line, *arrays)

    return jax.shard_map(
        run,
        mesh=mesh,
        in_specs=(rows, rows, flat, P()) + (rows,) * 5 + (columns,) + (rows,) * 10 + (columns,) * 2,
        out_specs=(rows, rows, P()) + (rows,) * 15 + (columns,) * 3,
        check_vma=False,
    )
```

```python
import functools
import math

import jax
import jax.numpy as jnp
from jax import lax
from jax.experimental import pallas as pl
from jax.experimental.pallas import tpu as pltpu
from jax.sharding import PartitionSpec as P

HQ = 16
HD = 64
LATENT_HEADS = 2
LATENT_WIDTH = 256
FF = 2816
NDOM = 16
STEP = 10
ROPE = 32
QUERY_WIDTH = HQ * HD
GROUP_WIDTH = QUERY_WIDTH // LATENT_HEADS
LANES = 128
PAIRS = QUERY_WIDTH // LANES
PAIRS_PER_LATENT = PAIRS // LATENT_HEADS

MAX_NORM = 1.0
BETA_ONE = 0.9
BETA_TWO = 0.95
RATE_MATRIX = 0.02
RATE_OUTPUT = 0.2
RATE_GAIN = 1.0
DECAY_MATRIX = 0.1
EPSILON_ADAM = 1e-08
EPSILON_NORM = 1e-06
ROPE_BASE = 10000.0

AXES = ("dp", "fsdp")
BF = jnp.bfloat16
F32 = jnp.float32
LOG2E = 1.4426950408889634
SCALE = HD**-0.5
NN = (((1,), (0,)), ((), ()))
NT = (((1,), (1,)), ((), ()))
TN = (((0,), (0,)), ((), ()))
MIB = 1 << 20
CHUNK = 256
TILE = 2 * CHUNK
FIRST_CHUNKS = 7


def dot(left, right, dims):
    return lax.dot_general(left, right, dims, preferred_element_type=F32)


def cost(microseconds):
    return pl.CostEstimate(flops=int(microseconds * 1e9), bytes_accessed=1 << 20, transcendentals=0)


def resident(*shape):
    return pl.BlockSpec(shape, lambda *step: (0,) * len(shape), pipeline_mode=pl.Buffered(1))


def rotation_tables(length):
    half = ROPE // 2
    lane = jnp.arange(LANES) % HD
    freqs = jnp.where(lane < ROPE, ROPE_BASE ** (-(lane % half).astype(F32) / half), 0.0)
    theta = jnp.arange(length).astype(F32)[:, None] * freqs[None, :]
    sine = jnp.sin(theta)
    ahead = jnp.where(lane < half, -sine, 0.0)
    behind = jnp.where((lane >= half) & (lane < ROPE), sine, 0.0)
    return jnp.cos(theta), ahead, behind


def rotate(values, own, ahead, behind):
    half = ROPE // 2
    return (
        values * own
        + pltpu.roll(values, LANES - half, 1) * ahead
        + pltpu.roll(values, half, 1) * behind
    )


def unrotate(values, own, ahead, behind):
    half = ROPE // 2
    return (
        values * own
        - pltpu.roll(values, LANES - half, 1) * ahead
        - pltpu.roll(values, half, 1) * behind
    )


def lay_out(devices, inverse_ref, mine_ref, other_ref, win_ref, wup_ref, gains_ref):
    plane, size = mine_ref.shape[:2]
    width, side = win_ref.shape
    rows, ups, pieces = width // devices, wup_ref.shape[0] // devices, wup_ref.shape[1] // TILE
    line = size // rows
    gains = [jnp.zeros((1, width), F32)] * 2
    source = lambda rows, columns: lax.broadcasted_iota(jnp.int32, (rows, columns), 0)
    target = lambda rows, columns: lax.broadcasted_iota(jnp.int32, (rows, columns), 1)
    share = width // devices
    spread = (source(LANES, width) == target(LANES, width) % share).astype(BF)
    for place in range(inverse_ref.shape[0]):
        ref = mine_ref if place < plane else other_ref
        block = ref[place % plane]
        index = inverse_ref[place]
        win_ref[pl.ds(pl.multiple_of(index * size, size), size), :] = block[:, :side]
        for z in range(line):
            start = pl.multiple_of((index * line + z) * ups, ups)
            for piece in range(pieces):
                row = z * rows + piece * ups
                columns = slice(piece * TILE, (piece + 1) * TILE)
                wup_ref[pl.ds(start, ups), columns] = block[row : row + ups, side : side + TILE]
        spots = block[:, side + TILE :]
        for which in range(2):
            pick = (target(line, size) == source(line, size) * rows + which).astype(BF)
            found = dot(dot(pick, spots, NN).astype(BF), spread, NN)
            here = target(line, width) // share == source(line, width) + index * line
            gains[which] += jnp.sum(jnp.where(here, found, 0.0), axis=0, keepdims=True)
    gains_ref[...] = jnp.concatenate(gains, axis=0)


def project_kernel(devices, *refs):
    if devices:
        inverse_ref, x_ref, mine_ref, other_ref = refs[:4]
        own_ref, ahead_ref, behind_ref, a1_ref, q_ref, k_ref, v_ref, c_ref, win_ref, wup_ref, gains_ref = refs[4:]

        @pl.when(pl.program_id(0) == 0)
        def _():
            lay_out(devices, inverse_ref, mine_ref, other_ref, win_ref, wup_ref, gains_ref)
    else:
        x_ref, win_ref, wup_ref, gains_ref = refs[1:5]
        own_ref, ahead_ref, behind_ref, a1_ref, q_ref, k_ref, v_ref, c_ref = refs[5:]
    tables = (own_ref[...], ahead_ref[...], behind_ref[...])
    x = x_ref[...].astype(F32)
    inverse = lax.rsqrt(jnp.mean(x * x, axis=1, keepdims=True) + EPSILON_NORM)
    a1 = (x * inverse * gains_ref[:1, :]).astype(BF)
    a1_ref[...] = a1
    joined = dot(a1, win_ref[...], NN)
    for pair in range(PAIRS):
        lanes = slice(pair * LANES, (pair + 1) * LANES)
        q_ref[:, lanes] = rotate(joined[:, lanes], *tables).astype(BF)
    c = joined[:, QUERY_WIDTH:].astype(BF)
    c_ref[...] = c
    for head in range(LATENT_HEADS):
        latent = slice(head * LATENT_WIDTH, (head + 1) * LATENT_WIDTH)
        both = dot(c[:, latent], wup_ref[latent, :], NN)
        for pair in range(PAIRS_PER_LATENT):
            lanes = slice(pair * LANES, (pair + 1) * LANES)
            out = slice(head * GROUP_WIDTH + pair * LANES, head * GROUP_WIDTH + (pair + 1) * LANES)
            k_ref[:, out] = rotate(both[:, lanes], *tables).astype(BF)
        out = slice(head * GROUP_WIDTH, (head + 1) * GROUP_WIDTH)
        v_ref[:, out] = both[:, GROUP_WIDTH:].astype(BF)


def project(devices, inverse, x, tables, *weights):
    length, width = x.shape
    tile = min(256, length)
    latents = LATENT_HEADS * LATENT_WIDTH
    rows = lambda columns: pl.BlockSpec((tile, columns), lambda i, *_: (i, 0))
    shape = lambda columns: jax.ShapeDtypeStruct((length, columns), BF)
    out_specs = [rows(width), rows(QUERY_WIDTH), rows(QUERY_WIDTH), rows(QUERY_WIDTH), rows(latents)]
    out_shape = [shape(width), shape(QUERY_WIDTH), shape(QUERY_WIDTH), shape(QUERY_WIDTH), shape(latents)]
    if devices:
        more = [((width, QUERY_WIDTH + latents), BF), ((latents, 2 * GROUP_WIDTH), BF), ((2, width), F32)]
        out_specs += [resident(*s) for s, _ in more]
        out_shape += [jax.ShapeDtypeStruct(*s) for s in more]
    return pl.pallas_call(
        functools.partial(project_kernel, devices),
        grid_spec=pltpu.PrefetchScalarGridSpec(
            num_scalar_prefetch=1,
            grid=(length // tile,),
            in_specs=[rows(width)] + [resident(*w.shape) for w in weights] + [rows(LANES)] * 3,
            out_specs=out_specs,
        ),
        out_shape=out_shape,
        compiler_params=pltpu.CompilerParams(vmem_limit_bytes=60 * MIB),
        cost_estimate=cost(20),
        name="project",
    )(inverse, x, *weights, *tables)


def halves(pair, axis):
    first = lax.broadcasted_iota(jnp.int32, pair.shape, axis) < HD
    zero = jnp.zeros_like(pair)
    return (jnp.where(first, pair, zero), jnp.where(first, zero, pair))


def not_after(block):
    keys = lax.broadcasted_iota(jnp.int32, (block, block), 0)
    queries = lax.broadcasted_iota(jnp.int32, (block, block), 1)
    return keys <= queries


def attention_kernel(q_ref, k_ref, v_ref, o_ref, log_ref):
    length = q_ref.shape[0]
    block = min(512, length)
    values = halves(v_ref[...].T, 0)
    for start in range(0, length, block):
        stop = start + block
        queries = halves(q_ref[start:stop, :], 1)
        probs = []
        for head in range(2):
            scores = dot(k_ref[:stop, :], queries[head], NT) * (SCALE * LOG2E)
            last = jnp.where(not_after(block), scores[start:, :], -1e30)
            scores = jnp.concatenate([scores[:start, :], last], axis=0) if start else last
            peak = jnp.max(scores, axis=0, keepdims=True)
            expo = jnp.exp2(scores - peak)
            total = jnp.sum(expo, axis=0, keepdims=True)
            log_ref[0, head : head + 1, start:stop] = peak + jnp.log2(total)
            probs.append((expo * (1.0 / total)).astype(BF))
        mixed = dot(values[0][:, :stop], probs[0], NN) + dot(values[1][:, :stop], probs[1], NN)
        o_ref[start:stop, :] = mixed.T.astype(BF)


def attention(q, k, v):
    length, width = q.shape
    spec = pl.BlockSpec((length, LANES), lambda i: (0, i))
    logs = pl.BlockSpec((1, 2, length), lambda i: (i, 0, 0))
    return pl.pallas_call(
        attention_kernel,
        grid=(PAIRS,),
        in_specs=[spec] * 3,
        out_specs=[spec, logs],
        out_shape=[
            jax.ShapeDtypeStruct((length, width), BF),
            jax.ShapeDtypeStruct((PAIRS, 2, length), F32),
        ],
        compiler_params=pltpu.CompilerParams(vmem_limit_bytes=60 * MIB),
        cost_estimate=cost(1),
        name="attention",
    )(q, k, v)


def attention_back_kernel(q_ref, k_ref, v_ref, o_ref, do_ref, log_ref, own_ref, ahead_ref, behind_ref,
                          dq_ref, dk_ref, dv_ref, total_ref):
    length = q_ref.shape[0]
    block = min(256, length)
    tables = lambda rows: (own_ref[rows, :], ahead_ref[rows, :], behind_ref[rows, :])
    product = (do_ref[...].astype(F32) * o_ref[...].astype(F32)).T
    deltas = (
        jnp.sum(product[:HD], axis=0, keepdims=True),
        jnp.sum(product[HD:], axis=0, keepdims=True),
    )
    keys = halves(k_ref[...].T, 0)
    for start in range(0, length, block):
        stop = start + block
        queries = halves(q_ref[start:, :], 1)
        grads = halves(do_ref[start:, :], 1)
        dk = dv = dq = None
        for head in range(2):
            scores = dot(k_ref[start:stop, :], queries[head], NT) * (SCALE * LOG2E)
            probs = jnp.exp2(scores - log_ref[0, head : head + 1, start:])
            first = jnp.where(not_after(block), probs[:, :block], 0.0)
            probs = jnp.concatenate([first, probs[:, block:]], axis=1) if stop < length else first
            dprobs = dot(v_ref[start:stop, :], grads[head], NT)
            dscores = (probs * (dprobs - deltas[head][:, start:])).astype(BF)
            parts = (
                dot(probs.astype(BF), grads[head], NN),
                dot(dscores, queries[head], NN),
                dot(keys[head][:, start:stop], dscores, NN),
            )
            dv = parts[0] if dv is None else dv + parts[0]
            dk = parts[1] if dk is None else dk + parts[1]
            dq = parts[2] if dq is None else dq + parts[2]
        dv_ref[start:stop, :] = dv.astype(BF)
        dk_ref[start:stop, :] = unrotate(dk * SCALE, *tables(slice(start, stop))).astype(BF)
        if start == 0:
            total_ref[...] = dq
        else:
            total_ref[:, start:] += dq
    dq_ref[...] = unrotate(total_ref[...].T * SCALE, *tables(slice(None))).astype(BF)


def attention_back(weight, start, count, q, k, v, o, do, logs, tables):
    length = q.shape[0]
    spec = pl.BlockSpec((length, LANES), lambda i: (0, i + start))
    out = pl.BlockSpec((length, LANES), lambda i: (0, i))
    log = pl.BlockSpec((1, 2, length), lambda i: (i + start, 0, 0))
    return pl.pallas_call(
        attention_back_kernel,
        grid=(count,),
        in_specs=[spec] * 5 + [log] + [resident(length, LANES)] * 3,
        out_specs=[out] * 3,
        out_shape=[jax.ShapeDtypeStruct((length, count * LANES), BF)] * 3,
        scratch_shapes=[pltpu.VMEM((LANES, length), F32)],
        compiler_params=pltpu.CompilerParams(vmem_limit_bytes=60 * MIB),
        cost_estimate=cost(weight),
        name="attention_back",
    )(q, k, v, o, do, logs, *tables)


def place_rows(target_ref, columns, values, order_ref):
    blocks = order_ref.shape[0]
    size = values.shape[1] // blocks
    for block in range(blocks):
        start = pl.multiple_of(order_ref[block] * size, size)
        target_ref[pl.ds(start, size), columns] = values[:, block * size : (block + 1) * size].T


def natural_rows(target_ref, piece_refs, places, inverse_ref):
    size = target_ref.shape[0] // inverse_ref.shape[0]
    for ref, (_, entries) in zip(piece_refs, places):
        for number, (place, row) in enumerate(entries):
            start = pl.multiple_of(inverse_ref[place] * size + row, math.gcd(size, row or size))
            target_ref[pl.ds(start, ref.shape[1]), :] = ref[number]


def natural_copies(target_ref, piece_refs, places, inverse_ref, sems, first, last):
    size = target_ref.shape[0] // inverse_ref.shape[0]
    starts = sorted({column for column, _ in places})
    copy = lambda ref, number, column, block: pltpu.make_async_copy(
        ref.at[number],
        target_ref.at[pl.ds(block * size, size), pl.ds(column, ref.shape[2])],
        sems.at[block, starts.index(column)],
    )

    def start():
        for ref, (column, entries) in zip(piece_refs, places):
            for number, (place, _) in enumerate(entries):
                block = inverse_ref[place]

                @pl.when((block >= first) & (block <= last))
                def _():
                    copy(ref, number, column, block).start()

    def wait(block):
        for column in starts:
            ref = next(ref for ref, (at, _) in zip(piece_refs, places) if at == column)
            copy(ref, 0, column, block).wait()

    return start, wait


def feed_forward_kernel(first, start, count, places, order_ref, inverse_ref, *refs):
    out_places, w_places, d_places = places
    out_refs, refs = refs[: len(out_places)], refs[len(out_places) :]
    w_refs, refs = refs[: len(w_places)], refs[len(w_places) :]
    d_refs, refs = refs[: len(d_places)], refs[len(d_places) :]
    og_ref, factor_ref, gain_ref, o_ref = refs[:4]
    if first:
        x_ref, h_out, acc_out, da2_out, own_ref, send_ref, gd_ref, h_ref, acc_ref, da2_ref = refs[4:14]
        refs = refs[14:]
    else:
        h_ref, acc_in, da2_in = refs[4:7]
        mixed_out, dh_out, do_out, own_ref, send_ref, gd_ref, dgain_ref = refs[8:15]
        acc_ref, da2_ref, acc_old_ref, da2_old_ref, mixed_ref, do_ref = refs[15:21]
        refs = refs[21:]
    wout_ref, w_ref, wd_ref, a2_ref, a2t_ref, dyb_ref, hid_ref, dgu_ref, sems, more_sems = refs
    step = pl.program_id(0)
    steps = pl.num_programs(0)
    length, width = og_ref.shape
    chunk = gd_ref.shape[0]
    side = width // 2
    tile, big = min(256, length), min(1024, length)
    gain = gain_ref[...]
    copy = lambda source, target, number: pltpu.make_async_copy(source, target, more_sems.at[number])
    block_size = wd_ref.shape[0] // inverse_ref.shape[0]
    block_first, block_last = start * chunk // block_size, ((start + count) * chunk - 1) // block_size
    fetch, arrived = natural_copies(wd_ref, d_refs, d_places, inverse_ref, sems, block_first, block_last)

    @pl.when(step == 0)
    def _():
        fetch()
        if not first:
            copy(acc_in, acc_old_ref, 0).start()
            copy(da2_in, da2_old_ref, 1).start()
        natural_rows(wout_ref, out_refs, out_places, inverse_ref)
        for m in range(0, length, tile):
            rows = pl.ds(m, tile)
            if first:
                h = x_ref[rows, :].astype(F32) + dot(o_ref[rows, :], wout_ref[...], NN)
                h_ref[rows, :] = h
                acc_ref[rows, :] = h
            else:
                h = h_ref[rows, :]
                acc_ref[rows, :] = jnp.zeros((tile, width), F32)
            da2_ref[rows, :] = jnp.zeros((tile, width), F32)
            inverse = lax.rsqrt(jnp.mean(h * h, axis=1, keepdims=True) + EPSILON_NORM)
            a2 = (h * inverse * gain).astype(BF)
            a2_ref[rows, :] = a2
            place_rows(a2t_ref, rows, a2, order_ref)
            dyb_ref[rows, :] = (og_ref[rows, :].astype(F32) * factor_ref[rows, :1]).astype(BF)
        if first:
            copy(h_ref, h_out, 0).start()

    for block in range(block_first, block_last + 1):

        @pl.when(step == max(0, block * block_size // chunk - start))
        def _():
            arrived(block)

    def one_chunk():
        natural_rows(w_ref, w_refs, w_places, inverse_ref)
        down = wd_ref[pl.ds(pl.multiple_of((start + step) * chunk, chunk), chunk), :]
        for m in range(0, length, big):
            rows = pl.ds(m, big)
            gate = dot(a2_ref[rows, :], w_ref[:, :chunk], NN)
            up = dot(a2_ref[rows, :], w_ref[:, chunk:], NN)
            dhid = dot(dyb_ref[rows, :], down, NT)
            sig = 1.0 / (1.0 + jnp.exp2(gate * -LOG2E))
            act = gate * sig
            hid_ref[rows, :] = (act * up).astype(BF)
            dgu_ref[rows, :chunk] = (dhid * up * (sig + act * (1.0 - sig))).astype(BF)
            dgu_ref[rows, chunk:] = (dhid * act).astype(BF)
        for m in range(0, length, big):
            rows = pl.ds(m, big)
            acc_ref[rows, :] += dot(hid_ref[rows, :], down, NN)
            da2_ref[rows, :] += dot(dgu_ref[rows, :], w_ref[...], NT)
        if first:

            @pl.when(step == steps - 1)
            def _():
                copy(acc_ref, acc_out, 1).start()
                copy(da2_ref, da2_out, 2).start()

        gd_ref[...] = dot(hid_ref[...], dyb_ref[...], TN).astype(BF)
        own_ref[...] = dot(a2t_ref[:side, :], dgu_ref[...], NN).astype(BF)
        send_ref[...] = dot(a2t_ref[side:, :], dgu_ref[...], NN).astype(BF)

    if first:
        one_chunk()

        @pl.when(step == steps - 1)
        def _():
            copy(h_ref, h_out, 0).wait()
            copy(acc_ref, acc_out, 1).wait()
            copy(da2_ref, da2_out, 2).wait()

        return
    tail = steps - 2
    pl.when(step < tail)(one_chunk)

    @pl.when(step == tail)
    def _():
        copy(acc_in, acc_old_ref, 0).wait()
        copy(da2_in, da2_old_ref, 1).wait()
        total = jnp.zeros((1, width), F32)
        for m in range(0, length, tile):
            rows = pl.ds(m, tile)
            mixed_ref[rows, :] = (acc_old_ref[rows, :] + acc_ref[rows, :]).astype(BF)
            h = h_ref[rows, :]
            inverse = lax.rsqrt(jnp.mean(h * h, axis=1, keepdims=True) + EPSILON_NORM)
            hat = h * inverse
            da2 = da2_old_ref[rows, :] + da2_ref[rows, :]
            total = total + jnp.sum(da2 * hat, axis=0, keepdims=True)
            scaled = da2 * gain
            dy = og_ref[rows, :].astype(F32) * factor_ref[rows, :1]
            dh = dy + inverse * (scaled - hat * jnp.mean(scaled * hat, axis=1, keepdims=True))
            acc_ref[rows, :] = dh
            low = dh.astype(BF)
            dyb_ref[rows, :] = low
            do_ref[rows, :] = dot(low, wout_ref[...], NT).astype(BF)
            place_rows(a2t_ref, rows, o_ref[rows, :], order_ref)
        dgain_ref[...] = total
        copy(mixed_ref, mixed_out, 2).start()
        copy(acc_ref, dh_out, 3).start()
        copy(do_ref, do_out, 4).start()

    for tile_number in range(2):

        @pl.when(step == tail + tile_number)
        def _():
            half = width // 2
            grads = dyb_ref[:, tile_number * half : (tile_number + 1) * half]
            own_ref[...] = dot(a2t_ref[:side, :], grads, NN).astype(BF)
            send_ref[...] = dot(a2t_ref[side:, :], grads, NN).astype(BF)

    @pl.when(step == steps - 1)
    def _():
        copy(mixed_ref, mixed_out, 2).wait()
        copy(acc_ref, dh_out, 3).wait()
        copy(do_ref, do_out, 4).wait()


def feed_forward(order, inverse, start, count, skip, state, x, o, out_grad, factor, gain, out_pieces, pieces, down_pieces):
    length, width = out_grad.shape
    chunk = CHUNK
    first = state is None
    steps = count if first else count + 2
    last = count - 1
    rows = pl.BlockSpec((chunk, width), lambda i, *_: (start + jnp.minimum(i, last), 0))
    columns = pl.BlockSpec((width // 2, TILE), lambda i, *_: (0, i))
    whole = lambda *s: pl.BlockSpec(s, lambda i, *_: (0,) * len(s), pipeline_mode=pl.Buffered(1))
    anywhere = pl.BlockSpec(memory_space=pl.ANY)
    shape = jax.ShapeDtypeStruct
    (outs, out_places), (tiles, w_places), (downs, d_places) = out_pieces, pieces, down_pieces
    big = whole(length, width)
    full, low = pltpu.VMEM((length, width), F32), pltpu.VMEM((length, width), BF)
    scratch = [
        pltpu.VMEM((width, width), BF),
        pltpu.VMEM((width, TILE), BF),
        pltpu.VMEM((FF, width), BF),
        low,
        pltpu.VMEM((width, length), BF),
        low,
        pltpu.VMEM((length, chunk), BF),
        pltpu.VMEM((length, TILE), BF),
        pltpu.SemaphoreType.DMA((inverse.shape[0], 2)),
        pltpu.SemaphoreType.DMA((5,)),
    ]
    in_specs = [whole(*piece.shape[:2], width) for piece in outs]
    in_specs += [
        pl.BlockSpec((*piece.shape[:2], TILE), lambda i, *_: (0, 0, skip + jnp.minimum(i, last))) for piece in tiles
    ]
    in_specs += [anywhere] * len(downs)
    in_specs += [big, whole(length, LANES), whole(1, width), big]
    operands = [*outs, *tiles, *downs, out_grad, factor, gain, o]
    halves_out = [shape((width // 2, steps * TILE), BF)] * 2
    aliases = {}
    if first:
        in_specs += [big]
        operands += [x]
        out_specs = [anywhere, anywhere, anywhere, columns, columns, rows]
        out_shape = [shape((length, width), F32)] * 3 + halves_out + [shape((FF, width), BF)]
        scratch = [full, full, full] + scratch
    else:
        in_specs += [big, anywhere, anywhere, anywhere]
        operands += list(state)
        out_specs = [anywhere, anywhere, anywhere, columns, columns, rows, whole(1, width)]
        out_shape = [shape((length, width), BF), shape((length, width), F32), shape((length, width), BF)]
        out_shape += halves_out + [shape((FF, width), BF), shape((1, width), F32)]
        scratch = [full, full, full, full, low, low] + scratch
        aliases = {len(operands) + 1: 5}
    return pl.pallas_call(
        functools.partial(feed_forward_kernel, first, start, count, (out_places, w_places, d_places)),
        grid_spec=pltpu.PrefetchScalarGridSpec(
            num_scalar_prefetch=2, grid=(steps,), in_specs=in_specs, out_specs=out_specs, scratch_shapes=scratch
        ),
        out_shape=out_shape,
        input_output_aliases=aliases,
        compiler_params=pltpu.CompilerParams(vmem_limit_bytes=63 * MIB),
        cost_estimate=cost(40),
        name="feed_forward",
    )(order, inverse, *operands)


def unproject_kernel(devices, order_ref, a1_ref, c_ref, dq_ref, dk_ref, dv_ref, wup_ref, *refs):
    dc_ref, own_ref, send_ref = refs[:3]
    a1t_ref = refs[-1]
    head = pl.program_id(0)
    length, width = a1_ref.shape
    half = width // 2
    tile = min(256, length)

    @pl.when(head == 0)
    def _():
        for m in range(0, length, tile):
            place_rows(a1t_ref, pl.ds(m, tile), a1_ref[m : m + tile, :], order_ref)

    dq, dk, dv = dq_ref[...], dk_ref[...], dv_ref[...]
    dc = (dot(dk, wup_ref[:, :GROUP_WIDTH], NT) + dot(dv, wup_ref[:, GROUP_WIDTH:], NT)).astype(BF)
    dc_ref[...] = dc
    grads = [
        (ref, start, size, dot(a1t_ref[rows, :], grad, NN).astype(BF))
        for ref, rows in ((own_ref, slice(half)), (send_ref, slice(half, width)))
        for start, size, grad in ((0, GROUP_WIDTH, dq), (QUERY_WIDTH, LATENT_WIDTH, dc))
    ]
    for which in range(LATENT_HEADS):

        @pl.when(head == which)
        def _():
            for ref, start, size, grad in grads:
                ref[:, start + which * size : start + (which + 1) * size] = grad

    turned = c_ref[...].T
    sides = [dot(turned, grad, NN).astype(BF) for grad in (dk, dv)]
    if not devices:
        refs[3][:, :GROUP_WIDTH], refs[3][:, GROUP_WIDTH:] = sides
        return
    all_ref = refs[3]
    side = QUERY_WIDTH + LATENT_HEADS * LATENT_WIDTH
    rows, ups = width // devices, wup_ref.shape[0] * LATENT_HEADS // devices
    blocks = order_ref.shape[0] // LATENT_HEADS
    line = devices // order_ref.shape[0]
    for block in range(blocks):
        place = order_ref[head * blocks + block]
        for z in range(line):
            device = block * line + z
            for piece, value in enumerate(sides):
                start = pl.multiple_of(place * (line * rows) + (z * rows + piece * ups), ups)
                all_ref[pl.ds(start, ups), :] = value[device * ups : (device + 1) * ups, :]

    @pl.when(head == LATENT_HEADS - 1)
    def _():
        own_ref[:, side:] = all_ref[:half, :]
        send_ref[:, side:] = all_ref[half:, :]


def unproject(devices, order, a1, c, dq, dk, dv, w_up):
    length, width = a1.shape
    latents = LATENT_HEADS * LATENT_WIDTH
    half = width // 2
    columns = lambda rows, size: pl.BlockSpec((rows, size), lambda g, *_: (0, g))
    up = pl.BlockSpec((LATENT_WIDTH, 2 * GROUP_WIDTH), lambda g, *_: (g, 0))
    group = columns(length, GROUP_WIDTH)
    both = QUERY_WIDTH + latents + (TILE if devices else 0)
    outs = [(length, latents)] + [(half, both)] * 2
    out_specs = [columns(length, LATENT_WIDTH)] + [resident(half, both)] * 2
    scratch = [pltpu.VMEM((width, length), BF)]
    if devices:
        scratch = [pltpu.VMEM((width, TILE), BF)] + scratch
    else:
        outs.append(w_up.shape)
        out_specs.append(up)
    return pl.pallas_call(
        functools.partial(unproject_kernel, devices),
        grid_spec=pltpu.PrefetchScalarGridSpec(
            num_scalar_prefetch=1,
            grid=(LATENT_HEADS,),
            in_specs=[resident(length, width), columns(length, LATENT_WIDTH), group, group, group, up],
            out_specs=out_specs,
            scratch_shapes=scratch,
        ),
        out_shape=[jax.ShapeDtypeStruct(s, BF) for s in outs],
        compiler_params=pltpu.CompilerParams(vmem_limit_bytes=60 * MIB),
        cost_estimate=cost(20),
        name="unproject",
    )(order, a1, c, dq, dk, dv, w_up)


def input_grad_kernel(x_ref, dh_ref, dq_ref, dc_ref, gain_ref, win_ref, out_ref, dgain_ref):
    x = x_ref[...].astype(F32)
    inverse = lax.rsqrt(jnp.mean(x * x, axis=1, keepdims=True) + EPSILON_NORM)
    hat = x * inverse
    da1 = dot(dq_ref[...], win_ref[:, :QUERY_WIDTH], NT) + dot(dc_ref[...], win_ref[:, QUERY_WIDTH:], NT)
    part = jnp.sum(da1 * hat, axis=0, keepdims=True)
    scaled = da1 * gain_ref[...].astype(F32)
    out_ref[...] = (
        dh_ref[...] + inverse * (scaled - hat * jnp.mean(scaled * hat, axis=1, keepdims=True))
    ).astype(BF)

    @pl.when(pl.program_id(0) == 0)
    def _():
        dgain_ref[...] = part

    @pl.when(pl.program_id(0) > 0)
    def _():
        dgain_ref[...] += part


def input_grad(x, dh, dql, gain, w_in):
    dq, dc = dql
    length, width = x.shape
    tile = min(256, length)
    rows = lambda columns: pl.BlockSpec((tile, columns), lambda i: (i, 0))
    return pl.pallas_call(
        input_grad_kernel,
        grid=(length // tile,),
        in_specs=[rows(width), rows(width), rows(dq.shape[1]), rows(dc.shape[1]), resident(1, width), resident(*w_in.shape)],
        out_specs=[rows(width), resident(1, width)],
        out_shape=[jax.ShapeDtypeStruct((length, width), BF), jax.ShapeDtypeStruct((1, width), F32)],
        compiler_params=pltpu.CompilerParams(vmem_limit_bytes=60 * MIB),
        cost_estimate=cost(20),
        name="input_grad",
    )(x, dh, dq, dc, gain, w_in)


class Ring:
    def __init__(self, data, line):
        self.cores = 2 if data % 2 == 0 else 1
        self.plane, self.line = data // self.cores, line
        place = lax.axis_index("dp")
        self.core, self.at, self.z = place % self.cores, place // self.cores, lax.axis_index("fsdp")

    def partner(self, index, shift, count):
        if count & (count - 1) == 0:
            return index ^ shift
        return (index + shift) % count

    def send_core(self, value):
        swap = [(i, i ^ 1) for i in range(self.plane * 2)]
        return lax.ppermute(value, "dp", swap)

    def send_plane(self, value, shift):
        pairs = [
            (p * self.cores + c, self.partner(p, shift, self.plane) * self.cores + c)
            for p in range(self.plane)
            for c in range(self.cores)
        ]
        return lax.ppermute(value, "dp", pairs)

    def send_line(self, value, shift):
        return lax.ppermute(value, "fsdp", [(i, (i + shift) % self.line) for i in range(self.line)])


def take(array, index, axis):
    return lax.dynamic_index_in_dim(array, index, axis, keepdims=False)


def core_blocks(ring, grad, core):
    rows = grad.shape[0] // (ring.plane * ring.cores * ring.line)
    return take(grad.reshape(ring.plane, ring.cores, ring.line, rows, grad.shape[1]), core, 1)


def total(parts):
    return sum(part.astype(F32) for part in parts)


def core_sends(ring, value):
    return [(ring.send_core, value)]


def plane_sends(ring, parts, relative):
    spot = lambda shift: shift if relative else ring.partner(ring.at, shift, ring.plane)
    block = lambda shift: total([take(part, spot(shift), 0) for part in parts]).astype(BF)
    sends = [
        (lambda value, shift=shift: ring.send_plane(value, shift), block(shift)) for shift in range(1, ring.plane)
    ]
    return block(0), sends


def cross_sends(ring, parts, bit, left):
    axis = len(left) - 1 - left.index(bit)
    side = (ring.at >> bit) & 1
    kept, give = (total([take(part, which, axis) for part in parts]) for which in (side, 1 - side))
    return kept, [(lambda value: ring.send_plane(value, 1 << bit), give.astype(BF))]


def line_sends(ring, parts, bit, axis=0):
    shape = parts[0].shape
    pairs = [part.reshape(*shape[:axis], shape[axis] // 2, 2, *shape[axis + 1 :]) for part in parts]
    side = (ring.z >> bit) & 1
    swap = [(i, i ^ (1 << bit)) for i in range(ring.line)]
    kept, give = (total([take(pair, which, axis + 1) for pair in pairs]) for which in (side, 1 - side))
    return kept, [(lambda value: lax.ppermute(value, "fsdp", swap), give.astype(BF))]


def beside(sends, kept, kernel=None, *inputs):
    inputs, gives, kept = together(inputs, [give for _, give in sends], kept)
    received = [send(give) for (send, _), give in zip(sends, gives)]
    return together(kernel(*inputs) if kernel else (), received, kept)


def line_rest(ring, grads, done):
    for bit in range(done, ring.line.bit_length() - 1):
        kept, sends = zip(*(line_sends(ring, [grad], bit) for grad in grads))
        _, received, kept = beside([send for one in sends for send in one], kept)
        grads = [total(pair) for pair in zip(kept, received)]
    return [grad[0] for grad in grads]


def halves_order(ring):
    blocks = jnp.arange(ring.plane * ring.cores)
    plane, core = blocks // ring.cores, blocks % ring.cores
    if ring.plane & (ring.plane - 1) == 0:
        shift = plane ^ ring.at
    else:
        shift = (plane - ring.at) % ring.plane
    order = (((core - ring.core) % ring.cores) * ring.plane + shift).astype(jnp.int32)
    shift, core = blocks % ring.plane, blocks // ring.plane
    if ring.plane & (ring.plane - 1) == 0:
        plane = shift ^ ring.at
    else:
        plane = (shift + ring.at) % ring.plane
    inverse = (plane * ring.cores + (core + ring.core) % ring.cores).astype(jnp.int32)
    return order, inverse


class Gather:
    def __init__(self, ring, piece, by_columns=False):
        self.ring, self.by_columns = ring, by_columns
        self.block = piece[None]
        self.bits = list(range(ring.line.bit_length() - 1))[::-1]

    def line_sends(self):
        swap = [(i, i ^ (1 << self.bits[0])) for i in range(self.ring.line)]
        return [(lambda value: lax.ppermute(value, "fsdp", swap), self.block)]

    def line_receive(self, values):
        low = ((self.ring.z >> self.bits.pop(0)) & 1) == 0
        pair = [jnp.where(low, self.block, values[0]), jnp.where(low, values[0], self.block)]
        block = jnp.stack(pair, axis=1)
        self.block = block.reshape(-1, *block.shape[2:])
        if not self.bits:
            self.split()

    def split(self):
        line, rows, columns = self.block.shape
        count = self.ring.plane.bit_length() - 1
        if self.by_columns:
            cut = columns // 2
            halves = [self.block[..., :cut].reshape(1, -1, cut), self.block[..., cut:].reshape(1, -1, cut)]
            self.offsets = [(0, 0), (cut, 0)]
        else:
            whole = self.block.reshape(-1, columns)
            cut = whole.shape[0] // 2
            halves = [whole[None, :cut], whole[None, cut:]]
            self.offsets = [(0, 0), (0, cut)]
        self.halves = [([half], [[0]]) for half in halves]
        self.orders = [list(range(count)), list(range(count))[::-1]]

    def plane_sends(self):
        sends = []
        for (arrays, _), order in zip(self.halves, self.orders):
            value = jnp.concatenate(arrays, axis=0) if len(arrays) > 1 else arrays[0]
            sends.append((lambda value, bit=order[0]: self.ring.send_plane(value, 1 << bit), value))
        return sends

    def plane_receive(self, values):
        for (arrays, shifts), order, value in zip(self.halves, self.orders, values):
            bit = order.pop(0)
            shifts.append([shift ^ (1 << bit) for have in shifts for shift in have])
            arrays.append(value)

    def direct_sends(self):
        self.offsets = [(0, 0)]
        block = self.block.reshape(1, -1, self.block.shape[-1])
        self.halves = [([block], [[0]])]
        return [(lambda value, k=k: self.ring.send_plane(value, k), block) for k in range(1, self.ring.plane)]

    def direct_receive(self, values):
        for shift, value in enumerate(values, 1):
            self.halves[0][0].append(value)
            self.halves[0][1].append([shift])

    def arrays(self):
        return [array for arrays, _ in self.halves for array in arrays]

    def hold(self, arrays):
        arrays = list(arrays)
        for mine, _ in self.halves:
            for number in range(len(mine)):
                mine[number] = arrays.pop(0)

    def places(self, core):
        return [
            (column, [(core * self.ring.plane + shift, row) for shift in have])
            for (_, shifts), (column, row) in zip(self.halves, self.offsets)
            for have in shifts
        ]

    def pieces(self, other):
        if self.ring.cores == 1:
            return self.arrays(), self.places(0)
        return self.arrays() + list(other), self.places(0) + self.places(1)

    def stacked(self):
        blocks = [{}, {}]
        for found, (arrays, shifts) in zip(blocks, self.halves):
            for array, have in zip(arrays, shifts):
                found.update(zip(have, array))
        return jnp.stack([jnp.concatenate([found[k] for found in blocks], axis=0) for k in range(self.ring.plane)])


def natural(ring, mine, other):
    if ring.plane & (ring.plane - 1) == 0:
        shifts = [ring.at ^ at for at in range(ring.plane)]
    else:
        shifts = [(ring.at - at) % ring.plane for at in range(ring.plane)]
    blocks = []
    for shift in shifts:
        pair = [choose(shift, list(part)) for part in (mine, other)][: ring.cores]
        blocks += [choose((core - ring.core) % ring.cores, pair) for core in range(ring.cores)]
    return jnp.stack(blocks)


def choose(index, options):
    result = options[0]
    for number, option in enumerate(options[1:], 1):
        result = jnp.where(index == number, option, result)
    return result


def sum_all(ring, value):
    if ring.cores == 2:
        value = value + ring.send_core(value)
    for count, send in ((ring.plane, ring.send_plane), (ring.line, None)):
        if count & (count - 1):
            return lax.psum(value, AXES)
    shift = 1
    while shift < ring.plane:
        value = value + ring.send_plane(value, shift)
        shift *= 2
    shift = 1
    while shift < ring.line:
        swap = [(i, i ^ shift) for i in range(ring.line)]
        value = value + lax.ppermute(value, "fsdp", swap)
        shift *= 2
    return value


def adamw_kernel(message_ref, dgains_ref, a_ref, b_ref, c_ref, d_ref, *refs):
    masters, firsts, seconds, norm_ref, outs = refs[:6], refs[6:12], refs[12:18], refs[18], refs[19:]
    gains = message_ref[:-8, :]
    norm = jnp.sqrt(message_ref[-1:, :1] + jnp.sum(gains * gains, keepdims=True))
    norm_ref[...] = norm
    clip = jnp.minimum(1.0, MAX_NORM / (norm + 1e-06))

    def update(index, place, grad, rate, decay):
        grad = clip * grad
        master = masters[index][place]
        first_new = BETA_ONE * firsts[index][place] + (1.0 - BETA_ONE) * grad
        second_new = BETA_TWO * seconds[index][place] + (1.0 - BETA_TWO) * grad * grad
        first_hat = first_new / (1.0 - BETA_ONE**STEP)
        second_hat = second_new / (1.0 - BETA_TWO**STEP)
        outs[3 * index][place] = master - rate * (
            first_hat / (jnp.sqrt(second_hat) + EPSILON_ADAM) + decay * master
        )
        outs[3 * index + 1][place] = first_new
        outs[3 * index + 2][place] = second_new

    everything = (slice(None), slice(None))
    side = masters[0].shape[1]
    update(0, everything, c_ref[:, :side], RATE_MATRIX, DECAY_MATRIX)
    rows = masters[1].shape[0]
    for tile in range(masters[1].shape[1] // TILE):
        place = (slice(None), slice(tile * TILE, (tile + 1) * TILE))
        update(1, place, c_ref[tile * rows : (tile + 1) * rows, side:], RATE_MATRIX, DECAY_MATRIX)
    second = FF // CHUNK - FIRST_CHUNKS
    update(2, everything, b_ref[:, second * TILE :], RATE_OUTPUT, DECAY_MATRIX)
    for chunk in range(FF // CHUNK):
        ref, at = (a_ref, chunk) if chunk < FIRST_CHUNKS else (b_ref, chunk - FIRST_CHUNKS)
        for which in range(2):
            place = (slice(None), slice(which * FF + chunk * CHUNK, which * FF + (chunk + 1) * CHUNK))
            start = at * TILE + which * CHUNK
            update(3, place, ref[:, start : start + CHUNK], RATE_MATRIX, DECAY_MATRIX)
    update(4, everything, d_ref[...], RATE_MATRIX, DECAY_MATRIX)
    update(5, everything, dgains_ref[...], RATE_GAIN, 0.0)


def adamw(message, dgains, totals, masters, firsts, seconds):
    shape = jax.ShapeDtypeStruct
    outs = [shape((1, 1), F32)] + [shape(w.shape, F32) for w in masters for _ in range(3)]
    return pl.pallas_call(
        adamw_kernel,
        out_shape=outs,
        compiler_params=pltpu.CompilerParams(vmem_limit_bytes=60 * MIB),
        cost_estimate=cost(5),
        name="adamw",
    )(message, dgains, *totals, *masters, *firsts, *seconds)


def together(*values):
    return lax.optimization_barrier(values)


def shards(data, line, tokens, out_grad, domain_ids, domain_scale, *state):
    masters, moments = state[:6], state[6:]
    firsts, seconds = moments[0::2], moments[1::2]
    ring = Ring(data, line)
    devices = data * line
    length, width = tokens.shape
    p_in, p_up, p_out, p_gate, p_down, p_gains = masters
    latents = LATENT_HEADS * LATENT_WIDTH
    rows = width // devices
    chunks = FF // CHUNK
    columns = lambda a: a.reshape(a.shape[0], -1, TILE).transpose(1, 0, 2).reshape(-1, TILE)

    half = FIRST_CHUNKS
    one = jnp.concatenate([p_in, columns(p_up).reshape(rows, -1), lane_pad(p_gains, rows)], axis=1).astype(BF)
    one = Gather(ring, one)
    order, inverse = halves_order(ring)

    def early(domain_ids, p_out, p_gate, p_down):
        picked = domain_ids[:, None] == jnp.arange(NDOM)[None, :]
        factor = jnp.sum(jnp.where(picked, domain_scale[None, :], 0.0), axis=1, keepdims=True)
        factor = jnp.broadcast_to(factor, (length, LANES))
        tiles = p_gate.astype(BF).reshape(rows, 2, chunks, CHUNK).transpose(0, 2, 1, 3).reshape(rows, -1)
        two = jnp.concatenate([p_out.astype(BF), tiles[:, : half * TILE]], axis=1)
        return rotation_tables(length), factor, two, p_down.astype(BF), tiles[:, half * TILE :]

    out, received, _ = beside(one.line_sends(), (), early, domain_ids, p_out, p_gate, p_down)
    tables, factor, two, down, three = out
    two, down, three = Gather(ring, two), Gather(ring, down, True), Gather(ring, three)
    one.line_receive(received)
    while len(one.bits) > 0:
        one.line_receive(beside(one.line_sends(), ())[1])
    while len(down.bits) > 0 or len(one.orders[0]) > 0:
        sends = one.plane_sends() if len(one.orders[0]) > 0 else []
        split = len(sends)
        sends += down.line_sends() if len(down.bits) > 0 else []
        _, received, kept = beside(sends, one.arrays())
        one.hold(kept)
        if split:
            one.plane_receive(received[:split])
        if len(received) > split:
            down.line_receive(received[split:])
    one_block = one.stacked()
    sends = core_sends(ring, one_block) + down.plane_sends() + two.line_sends()
    _, received, (one_block, kept, tokens) = beside(sends, (one_block, down.arrays(), tokens))
    down.hold(kept)
    one_other = received[0]
    down.plane_receive(received[1:-1])
    two.line_receive(received[-1:])
    other = {}
    core_of = lambda keys: [send for h, r in keys for send in core_sends(ring, down.halves[h][0][r])]
    while len(down.orders[0]) > 0 or len(two.bits) > 0:
        sends = down.plane_sends() if len(down.orders[0]) > 0 else []
        split = len(sends)
        sends += two.line_sends() if len(two.bits) > 0 else []
        middle = len(sends)
        keys = [(0, 0), (1, 0)] if len(other) == 0 else []
        _, received, kept = beside(sends + core_of(keys), down.arrays())
        down.hold(kept)
        other.update(zip(keys, received[middle:]))
        if split:
            down.plane_receive(received[:split])
        if middle > split:
            two.line_receive(received[split:middle])
    aligned = rows % 32 == 0 and p_up.shape[0] % 16 == 0
    if aligned:
        run = lambda tokens: project(devices, inverse, tokens, tables, one_block, one_other)
    else:
        first = natural(ring, one_block, one_other).reshape(devices, rows, -1)
        w_in = first[:, :, : p_in.shape[1]].reshape(width, -1)
        w_up = first[:, :, p_in.shape[1] : p_in.shape[1] + p_up.size // rows]
        w_up = w_up.reshape(devices, 2 * GROUP_WIDTH // TILE, p_up.shape[0], TILE).transpose(0, 2, 1, 3).reshape(latents, -1)
        gains = first[:, :2, -LANES:][:, :, : p_gains.shape[1]].transpose(1, 0, 2).reshape(2, width).astype(F32)
        run = lambda tokens: (*project(0, inverse, tokens, tables, w_in, w_up, gains), w_in, w_up, gains)
    rounds = len(down.halves[0][0])
    rest = [(h, r) for r in range(1, rounds) for h in range(2)]
    sends = two.plane_sends() + three.line_sends()
    split = len(sends)
    out, received, kept = beside(sends + core_of(rest[:2]), (two.arrays(), down.arrays(), other), run, tokens)
    a1, q, k, v, c, w_in, w_up, gains = out
    two.hold(kept[0])
    down.hold(kept[1])
    other = dict(kept[2])
    two.plane_receive(received[:2])
    three.line_receive(received[2:3])
    other.update(zip(rest[:2], received[split:]))
    sends = two.plane_sends() if len(two.orders[0]) > 0 else []
    split = len(sends)
    sends += three.line_sends() if len(three.bits) > 0 else []
    middle = len(sends)
    sends += core_of(rest[2:4])
    (o, logs), received, kept = beside(sends, (two.arrays(), down.arrays(), other), attention, q, k, v)
    two.hold(kept[0])
    down.hold(kept[1])
    other = dict(kept[2])
    if split:
        two.plane_receive(received[:split])
    if middle > split:
        three.line_receive(received[split:middle])
    other.update(zip(rest[2:4], received[middle:]))
    while len(two.orders[0]) > 0:
        two.plane_receive(beside(two.plane_sends(), ())[1])
    while len(three.bits) > 0:
        three.line_receive(beside(three.line_sends(), ())[1])
    sends = core_of(rest[4:])
    split = len(sends)
    sends += [send for array in two.arrays() for send in core_sends(ring, array)]
    _, received, (o, kept, kept_down, other) = beside(sends, (o, two.arrays(), down.arrays(), other))
    two.hold(kept)
    down.hold(kept_down)
    other = dict(other)
    other.update(zip(rest[4:], received[:split]))
    down_pieces = down.pieces([other[h, r] for h in range(2) for r in range(rounds)])
    two_pieces = two.pieces(received[split:])
    common = (tokens, o, out_grad, factor, gains[1:], two_pieces)
    run = lambda o: feed_forward(
        order, inverse, 0, half, width // TILE, None, tokens, o, out_grad, factor, gains[1:], two_pieces, two_pieces, down_pieces
    )
    sends = three.direct_sends()
    split = len(sends)
    sends += core_sends(ring, three.arrays()[0])
    (h, acc, da2, own_a, send_a, g_down), received, kept = beside(sends, three.arrays(), run, o)
    three.hold(kept)
    three.direct_receive(received[:split])
    other = list(received[split:])
    blocks = lambda a: a.reshape(ring.plane, ring.line, rows, -1)
    sends = core_sends(ring, blocks(send_a)) + [send for array in three.arrays()[1:] for send in core_sends(ring, array)]
    _, received, (h, own_a, kept, other) = beside(sends, (h, own_a, three.arrays(), other))
    three.hold(kept)
    three_pieces = three.pieces(list(other) + list(received[1:]))
    kept_a, sends = plane_sends(ring, [blocks(own_a), received[0]], True)
    state = (acc, da2, g_down)
    run = lambda h: feed_forward(
        order, inverse, half, chunks - half, 0, (h, *state), *common, three_pieces, down_pieces
    )
    out, received, kept_a = beside(sends, kept_a, run, h)
    mixed, dh, do, own_b, send_b, g_down, dgain_two = out

    def run(g_down, kept_a, *came_a):
        kept_a, send_a = line_sends(ring, [kept_a, *came_a], 0)
        return core_blocks(ring, g_down, 1 - ring.core), kept_a, send_a[0][1]

    out, came_b, (do, own_b) = beside(core_sends(ring, blocks(send_b)), (do, own_b), run, g_down, kept_a, *received)
    send_d, kept_a, give_a = out
    kept_b, send_b = plane_sends(ring, [blocks(own_b), *came_b], True)
    sends = send_b + core_sends(ring, send_d) + [(line_sends(ring, [give_a], 0)[1][0][0], give_a)]
    run = lambda do: attention_back(40, 0, PAIRS, q, k, v, o, do, logs, tables)
    grads, received, (kept_a, kept_b, g_down) = beside(sends, (kept_a, kept_b, g_down), run, do)
    *came_b, came_d, came_a = received
    bits = list(range(ring.plane.bit_length() - 1))
    orders, left = (bits, bits[::-1]), [bits[:], bits[:]]
    halves_d = zip(*(jnp.split(part, 2, axis=-1) for part in (core_blocks(ring, g_down, ring.core), came_d)))
    halves_d = [[part.reshape(*(2,) * len(bits), *part.shape[1:]) for part in pair] for pair in halves_d]

    def step_d(number, halves_d):
        kept, sends = zip(*(cross_sends(ring, half, order[number], have) for half, order, have in zip(halves_d, orders, left)))
        for order, have in zip(orders, left):
            have.remove(order[number])
        return kept, [send for one in sends for send in one]

    kept_d, send_d = step_d(0, halves_d)
    kept_a, send_a = line_sends(ring, [kept_a, came_a], 1)

    def run(dq, dk, dv):
        dc, own, send, *ups = unproject(devices if aligned else 0, order, a1, c, dq, dk, dv, w_up)
        if not aligned:
            g_up = ups[0].reshape(devices, -1, 2 * GROUP_WIDTH // TILE, TILE).transpose(0, 2, 1, 3).reshape(width, -1)
            spots = lambda core: [
                take(core_blocks(ring, g_up, core), ring.partner(ring.at, k, ring.plane), 0) for k in range(ring.plane)
            ]
            ups = [jnp.stack(spots(core)).reshape(width // 2, -1) for core in (ring.core, 1 - ring.core)]
            own, send = (jnp.concatenate(parts, axis=1) for parts in zip((own, send), ups))
        dql = (dq, dc)
        return dql, own, send

    kept_b, send_b = line_sends(ring, [kept_b, *came_b], 0)
    kept = (kept_a, kept_b, kept_d)
    out, received, (kept_a, kept_b, kept_d) = beside(send_d + send_a + send_b, kept, run, *grads)
    dql, own_c, send_c = out
    *came_d, came_a, came_b = received

    def second(kept_d, came_d):
        kept_d, send_d = step_d(1, list(zip(kept_d, came_d)))
        return kept_d, [give for _, give in send_d]

    send_d = [(lambda value, bit=order[1]: ring.send_plane(value, 1 << bit)) for order in orders]
    kept = (dql, own_c, kept_a, came_a, kept_b, came_b)
    (kept_d, give_d), came_c, kept = beside(core_sends(ring, blocks(send_c)), kept, second, kept_d, came_d)
    dql, own_c, kept_a, came_a, kept_b, came_b = kept
    run = lambda own_c, *came_c: plane_sends(ring, [blocks(own_c), *came_c], True)[0:1] + tuple(
        give for _, give in plane_sends(ring, [blocks(own_c), *came_c], True)[1]
    )
    kept = (dql, kept_a, came_a, kept_b, came_b, kept_d)
    (kept_c, *gives_c), came_d, kept = beside(list(zip(send_d, give_d)), kept, run, own_c, *came_c)
    dql, kept_a, came_a, kept_b, came_b, kept_d = kept
    send_c = [(lambda value, k=k: ring.send_plane(value, k), give) for k, give in enumerate(gives_c, 1)]
    for number in range(2, len(bits)):
        kept_d, send_d = step_d(number, list(zip(kept_d, came_d)))
        _, came_d, kept_d = beside(send_d, kept_d)
    sum_d = jnp.concatenate([total(pair) for pair in zip(kept_d, came_d)], axis=-1)
    kept_a = total([kept_a, came_a])
    kept_b, send_b = line_sends(ring, [kept_b, came_b], 1)
    kept_d, send_d = line_sends(ring, [sum_d], 0)
    run = lambda dql: input_grad(tokens, dh, dql, gains[:1], w_in)
    kept = (kept_b, kept_c, kept_d)
    (given, dgain_one), received, (kept_b, kept_c, kept_d) = beside(send_c + send_d + send_b, kept, run, dql)
    *came_c, came_d, came_b = received
    kept_b = total([kept_b, came_b])
    kept_c, send_c = line_sends(ring, [kept_c, *came_c], 0)
    kept_d, send_d = line_sends(ring, [kept_d, came_d], 1)
    _, received, (kept_c, kept_d) = beside(send_c + send_d, (kept_c, kept_d))
    came_c, came_d = received
    sums = [kept_a, kept_b, total([kept_d, came_d])]
    total_a, total_b, total_d = line_rest(ring, sums, 2)
    (total_c,) = line_rest(ring, [total([kept_c, came_c])], 1)

    squares = sum(jnp.sum(grad * grad) for grad in (total_a, total_b, total_c, total_d))
    dgains = jnp.concatenate([dgain_one, dgain_two], axis=0)
    message = jnp.concatenate(
        [dgains.reshape(-1, LANES), jnp.full((8, LANES), squares, F32)], axis=0
    )
    message = sum_all(ring, message)
    share = masters[5].shape[1]
    place = lax.axis_index("dp") * line + lax.axis_index("fsdp")
    dgains = lax.dynamic_slice_in_dim(message[:-8].reshape(2, width), place * share, share, 1)
    totals = (total_a, total_b, total_c, total_d)
    grad_norm, *results = adamw(message, dgains, totals, masters, firsts, seconds)
    return (mixed, given, grad_norm[0, 0], *results)


def lane_pad(gains, rows):
    return jnp.pad(gains, ((0, rows - gains.shape[0]), (0, LANES - gains.shape[1])))


def solution(mesh):
    data, line = mesh.shape["dp"], mesh.shape["fsdp"]
    rows, flat, columns = P(AXES, None), P(AXES), P(None, AXES)

    def run(*arrays):
        return shards(data, line, *arrays)

    return jax.shard_map(
        run,
        mesh=mesh,
        in_specs=(rows, rows, flat, P()) + (rows,) * 5 + (columns,) + (rows,) * 10 + (columns,) * 2,
        out_specs=(rows, rows, P()) + (rows,) * 15 + (columns,) * 3,
        check_vma=False,
    )
```

```python
import functools
import math

import jax
import jax.numpy as jnp
from jax import lax
from jax.experimental import pallas as pl
from jax.experimental.pallas import tpu as pltpu
from jax.sharding import PartitionSpec as P

HQ = 16
HD = 64
LATENT_HEADS = 2
LATENT_WIDTH = 256
FF = 2816
NDOM = 16
STEP = 10
ROPE = 32
QUERY_WIDTH = HQ * HD
GROUP_WIDTH = QUERY_WIDTH // LATENT_HEADS
LANES = 128
PAIRS = QUERY_WIDTH // LANES
PAIRS_PER_LATENT = PAIRS // LATENT_HEADS

MAX_NORM = 1.0
BETA_ONE = 0.9
BETA_TWO = 0.95
RATE_MATRIX = 0.02
RATE_OUTPUT = 0.2
RATE_GAIN = 1.0
DECAY_MATRIX = 0.1
EPSILON_ADAM = 1e-08
EPSILON_NORM = 1e-06
ROPE_BASE = 10000.0

AXES = ("dp", "fsdp")
BF = jnp.bfloat16
F32 = jnp.float32
LOG2E = 1.4426950408889634
SCALE = HD**-0.5
NN = (((1,), (0,)), ((), ()))
NT = (((1,), (1,)), ((), ()))
TN = (((0,), (0,)), ((), ()))
MIB = 1 << 20
CHUNK = 256
TILE = 2 * CHUNK
FIRST_CHUNKS = 7


def dot(left, right, dims):
    return lax.dot_general(left, right, dims, preferred_element_type=F32)


def cost(microseconds):
    return pl.CostEstimate(flops=int(microseconds * 1e9), bytes_accessed=1 << 20, transcendentals=0)


def resident(*shape):
    return pl.BlockSpec(shape, lambda *step: (0,) * len(shape), pipeline_mode=pl.Buffered(1))


def rotation_tables(length):
    half = ROPE // 2
    lane = jnp.arange(LANES) % HD
    freqs = jnp.where(lane < ROPE, ROPE_BASE ** (-(lane % half).astype(F32) / half), 0.0)
    theta = jnp.arange(length).astype(F32)[:, None] * freqs[None, :]
    sine = jnp.sin(theta)
    ahead = jnp.where(lane < half, -sine, 0.0)
    behind = jnp.where((lane >= half) & (lane < ROPE), sine, 0.0)
    return jnp.cos(theta), ahead, behind


def rotate(values, own, ahead, behind):
    half = ROPE // 2
    return (
        values * own
        + pltpu.roll(values, LANES - half, 1) * ahead
        + pltpu.roll(values, half, 1) * behind
    )


def unrotate(values, own, ahead, behind):
    half = ROPE // 2
    return (
        values * own
        - pltpu.roll(values, LANES - half, 1) * ahead
        - pltpu.roll(values, half, 1) * behind
    )


def lay_out(devices, inverse_ref, mine_ref, other_ref, win_ref, wup_ref, gains_ref):
    plane, size = mine_ref.shape[:2]
    width, side = win_ref.shape
    rows, ups, pieces = width // devices, wup_ref.shape[0] // devices, wup_ref.shape[1] // TILE
    line = size // rows
    gains = [jnp.zeros((1, width), F32)] * 2
    source = lambda rows, columns: lax.broadcasted_iota(jnp.int32, (rows, columns), 0)
    target = lambda rows, columns: lax.broadcasted_iota(jnp.int32, (rows, columns), 1)
    share = width // devices
    spread = (source(LANES, width) == target(LANES, width) % share).astype(BF)
    for place in range(inverse_ref.shape[0]):
        ref = mine_ref if place < plane else other_ref
        block = ref[place % plane]
        index = inverse_ref[place]
        win_ref[pl.ds(pl.multiple_of(index * size, size), size), :] = block[:, :side]
        for z in range(line):
            start = pl.multiple_of((index * line + z) * ups, ups)
            for piece in range(pieces):
                row = z * rows + piece * ups
                columns = slice(piece * TILE, (piece + 1) * TILE)
                wup_ref[pl.ds(start, ups), columns] = block[row : row + ups, side : side + TILE]
        spots = block[:, side + TILE :]
        for which in range(2):
            pick = (target(line, size) == source(line, size) * rows + which).astype(BF)
            found = dot(dot(pick, spots, NN).astype(BF), spread, NN)
            here = target(line, width) // share == source(line, width) + index * line
            gains[which] += jnp.sum(jnp.where(here, found, 0.0), axis=0, keepdims=True)
    gains_ref[...] = jnp.concatenate(gains, axis=0)


def project_kernel(devices, *refs):
    if devices:
        inverse_ref, x_ref, mine_ref, other_ref = refs[:4]
        own_ref, ahead_ref, behind_ref, a1_ref, q_ref, k_ref, v_ref, c_ref, win_ref, wup_ref, gains_ref = refs[4:]

        @pl.when(pl.program_id(0) == 0)
        def _():
            lay_out(devices, inverse_ref, mine_ref, other_ref, win_ref, wup_ref, gains_ref)
    else:
        x_ref, win_ref, wup_ref, gains_ref = refs[1:5]
        own_ref, ahead_ref, behind_ref, a1_ref, q_ref, k_ref, v_ref, c_ref = refs[5:]
    tables = (own_ref[...], ahead_ref[...], behind_ref[...])
    x = x_ref[...].astype(F32)
    inverse = lax.rsqrt(jnp.mean(x * x, axis=1, keepdims=True) + EPSILON_NORM)
    a1 = (x * inverse * gains_ref[:1, :]).astype(BF)
    a1_ref[...] = a1
    joined = dot(a1, win_ref[...], NN)
    for pair in range(PAIRS):
        lanes = slice(pair * LANES, (pair + 1) * LANES)
        q_ref[:, lanes] = rotate(joined[:, lanes], *tables).astype(BF)
    c = joined[:, QUERY_WIDTH:].astype(BF)
    c_ref[...] = c
    for head in range(LATENT_HEADS):
        latent = slice(head * LATENT_WIDTH, (head + 1) * LATENT_WIDTH)
        both = dot(c[:, latent], wup_ref[latent, :], NN)
        for pair in range(PAIRS_PER_LATENT):
            lanes = slice(pair * LANES, (pair + 1) * LANES)
            out = slice(head * GROUP_WIDTH + pair * LANES, head * GROUP_WIDTH + (pair + 1) * LANES)
            k_ref[:, out] = rotate(both[:, lanes], *tables).astype(BF)
        out = slice(head * GROUP_WIDTH, (head + 1) * GROUP_WIDTH)
        v_ref[:, out] = both[:, GROUP_WIDTH:].astype(BF)


def project(devices, inverse, x, tables, *weights):
    length, width = x.shape
    tile = min(256, length)
    latents = LATENT_HEADS * LATENT_WIDTH
    rows = lambda columns: pl.BlockSpec((tile, columns), lambda i, *_: (i, 0))
    shape = lambda columns: jax.ShapeDtypeStruct((length, columns), BF)
    out_specs = [rows(width), rows(QUERY_WIDTH), rows(QUERY_WIDTH), rows(QUERY_WIDTH), rows(latents)]
    out_shape = [shape(width), shape(QUERY_WIDTH), shape(QUERY_WIDTH), shape(QUERY_WIDTH), shape(latents)]
    if devices:
        more = [((width, QUERY_WIDTH + latents), BF), ((latents, 2 * GROUP_WIDTH), BF), ((2, width), F32)]
        out_specs += [resident(*s) for s, _ in more]
        out_shape += [jax.ShapeDtypeStruct(*s) for s in more]
    return pl.pallas_call(
        functools.partial(project_kernel, devices),
        grid_spec=pltpu.PrefetchScalarGridSpec(
            num_scalar_prefetch=1,
            grid=(length // tile,),
            in_specs=[rows(width)] + [resident(*w.shape) for w in weights] + [rows(LANES)] * 3,
            out_specs=out_specs,
        ),
        out_shape=out_shape,
        compiler_params=pltpu.CompilerParams(vmem_limit_bytes=60 * MIB),
        cost_estimate=cost(20),
        name="project",
    )(inverse, x, *weights, *tables)


def halves(pair, axis):
    first = lax.broadcasted_iota(jnp.int32, pair.shape, axis) < HD
    zero = jnp.zeros_like(pair)
    return (jnp.where(first, pair, zero), jnp.where(first, zero, pair))


def not_after(block):
    keys = lax.broadcasted_iota(jnp.int32, (block, block), 0)
    queries = lax.broadcasted_iota(jnp.int32, (block, block), 1)
    return keys <= queries


def attention_kernel(q_ref, k_ref, v_ref, o_ref, log_ref):
    length = q_ref.shape[0]
    block = min(512, length)
    values = halves(v_ref[...].T, 0)
    for start in range(0, length, block):
        stop = start + block
        queries = halves(q_ref[start:stop, :], 1)
        probs = []
        for head in range(2):
            scores = dot(k_ref[:stop, :], queries[head], NT) * (SCALE * LOG2E)
            last = jnp.where(not_after(block), scores[start:, :], -1e30)
            scores = jnp.concatenate([scores[:start, :], last], axis=0) if start else last
            peak = jnp.max(scores, axis=0, keepdims=True)
            expo = jnp.exp2(scores - peak)
            total = jnp.sum(expo, axis=0, keepdims=True)
            log_ref[0, head : head + 1, start:stop] = peak + jnp.log2(total)
            probs.append((expo * (1.0 / total)).astype(BF))
        mixed = dot(values[0][:, :stop], probs[0], NN) + dot(values[1][:, :stop], probs[1], NN)
        o_ref[start:stop, :] = mixed.T.astype(BF)


def attention(q, k, v):
    length, width = q.shape
    spec = pl.BlockSpec((length, LANES), lambda i: (0, i))
    logs = pl.BlockSpec((1, 2, length), lambda i: (i, 0, 0))
    return pl.pallas_call(
        attention_kernel,
        grid=(PAIRS,),
        in_specs=[spec] * 3,
        out_specs=[spec, logs],
        out_shape=[
            jax.ShapeDtypeStruct((length, width), BF),
            jax.ShapeDtypeStruct((PAIRS, 2, length), F32),
        ],
        compiler_params=pltpu.CompilerParams(vmem_limit_bytes=60 * MIB),
        cost_estimate=cost(1),
        name="attention",
    )(q, k, v)


def attention_back_kernel(q_ref, k_ref, v_ref, o_ref, do_ref, log_ref, own_ref, ahead_ref, behind_ref,
                          dq_ref, dk_ref, dv_ref, total_ref):
    length = q_ref.shape[0]
    block = min(256, length)
    tables = lambda rows: (own_ref[rows, :], ahead_ref[rows, :], behind_ref[rows, :])
    product = (do_ref[...].astype(F32) * o_ref[...].astype(F32)).T
    deltas = (
        jnp.sum(product[:HD], axis=0, keepdims=True),
        jnp.sum(product[HD:], axis=0, keepdims=True),
    )
    keys = halves(k_ref[...].T, 0)
    for start in range(0, length, block):
        stop = start + block
        queries = halves(q_ref[start:, :], 1)
        grads = halves(do_ref[start:, :], 1)
        dk = dv = dq = None
        for head in range(2):
            scores = dot(k_ref[start:stop, :], queries[head], NT) * (SCALE * LOG2E)
            probs = jnp.exp2(scores - log_ref[0, head : head + 1, start:])
            first = jnp.where(not_after(block), probs[:, :block], 0.0)
            probs = jnp.concatenate([first, probs[:, block:]], axis=1) if stop < length else first
            dprobs = dot(v_ref[start:stop, :], grads[head], NT)
            dscores = (probs * (dprobs - deltas[head][:, start:])).astype(BF)
            parts = (
                dot(probs.astype(BF), grads[head], NN),
                dot(dscores, queries[head], NN),
                dot(keys[head][:, start:stop], dscores, NN),
            )
            dv = parts[0] if dv is None else dv + parts[0]
            dk = parts[1] if dk is None else dk + parts[1]
            dq = parts[2] if dq is None else dq + parts[2]
        dv_ref[start:stop, :] = dv.astype(BF)
        dk_ref[start:stop, :] = unrotate(dk * SCALE, *tables(slice(start, stop))).astype(BF)
        if start == 0:
            total_ref[...] = dq
        else:
            total_ref[:, start:] += dq
    dq_ref[...] = unrotate(total_ref[...].T * SCALE, *tables(slice(None))).astype(BF)


def attention_back(weight, start, count, q, k, v, o, do, logs, tables):
    length = q.shape[0]
    spec = pl.BlockSpec((length, LANES), lambda i: (0, i + start))
    out = pl.BlockSpec((length, LANES), lambda i: (0, i))
    log = pl.BlockSpec((1, 2, length), lambda i: (i + start, 0, 0))
    return pl.pallas_call(
        attention_back_kernel,
        grid=(count,),
        in_specs=[spec] * 5 + [log] + [resident(length, LANES)] * 3,
        out_specs=[out] * 3,
        out_shape=[jax.ShapeDtypeStruct((length, count * LANES), BF)] * 3,
        scratch_shapes=[pltpu.VMEM((LANES, length), F32)],
        compiler_params=pltpu.CompilerParams(vmem_limit_bytes=60 * MIB),
        cost_estimate=cost(weight),
        name="attention_back",
    )(q, k, v, o, do, logs, *tables)


def place_rows(target_ref, columns, values, order_ref):
    blocks = order_ref.shape[0]
    size = values.shape[1] // blocks
    for block in range(blocks):
        start = pl.multiple_of(order_ref[block] * size, size)
        target_ref[pl.ds(start, size), columns] = values[:, block * size : (block + 1) * size].T


def natural_rows(target_ref, piece_refs, places, inverse_ref):
    size = target_ref.shape[0] // inverse_ref.shape[0]
    for ref, (_, entries) in zip(piece_refs, places):
        for number, (place, row) in enumerate(entries):
            start = pl.multiple_of(inverse_ref[place] * size + row, math.gcd(size, row or size))
            target_ref[pl.ds(start, ref.shape[1]), :] = ref[number]


def natural_copies(target_ref, piece_refs, places, inverse_ref, sems, first, last):
    size = target_ref.shape[0] // inverse_ref.shape[0]
    starts = sorted({column for column, _ in places})
    copy = lambda ref, number, column, block: pltpu.make_async_copy(
        ref.at[number],
        target_ref.at[pl.ds(block * size, size), pl.ds(column, ref.shape[2])],
        sems.at[block, starts.index(column)],
    )

    def start():
        for ref, (column, entries) in zip(piece_refs, places):
            for number, (place, _) in enumerate(entries):
                block = inverse_ref[place]

                @pl.when((block >= first) & (block <= last))
                def _():
                    copy(ref, number, column, block).start()

    def wait(block):
        for column in starts:
            ref = next(ref for ref, (at, _) in zip(piece_refs, places) if at == column)
            copy(ref, 0, column, block).wait()

    return start, wait


def feed_forward_kernel(first, start, count, places, order_ref, inverse_ref, *refs):
    out_places, w_places, d_places = places
    out_refs, refs = refs[: len(out_places)], refs[len(out_places) :]
    w_refs, refs = refs[: len(w_places)], refs[len(w_places) :]
    d_refs, refs = refs[: len(d_places)], refs[len(d_places) :]
    og_ref, factor_ref, gain_ref, o_ref = refs[:4]
    if first:
        x_ref, h_out, acc_out, da2_out, own_ref, send_ref, gd_ref, h_ref, acc_ref, da2_ref = refs[4:14]
        refs = refs[14:]
    else:
        h_ref, acc_in, da2_in = refs[4:7]
        mixed_out, dh_out, do_out, own_ref, send_ref, gd_ref, dgain_ref = refs[8:15]
        acc_ref, da2_ref, acc_old_ref, da2_old_ref, mixed_ref, do_ref = refs[15:21]
        refs = refs[21:]
    wout_ref, w_ref, wd_ref, a2_ref, a2t_ref, dyb_ref, hid_ref, dgu_ref, sems, more_sems = refs
    step = pl.program_id(0)
    steps = pl.num_programs(0)
    length, width = og_ref.shape
    chunk = gd_ref.shape[0]
    side = width // 2
    tile, big = min(256, length), min(1024, length)
    gain = gain_ref[...]
    copy = lambda source, target, number: pltpu.make_async_copy(source, target, more_sems.at[number])
    block_size = wd_ref.shape[0] // inverse_ref.shape[0]
    block_first, block_last = start * chunk // block_size, ((start + count) * chunk - 1) // block_size
    fetch, arrived = natural_copies(wd_ref, d_refs, d_places, inverse_ref, sems, block_first, block_last)

    @pl.when(step == 0)
    def _():
        fetch()
        if not first:
            copy(acc_in, acc_old_ref, 0).start()
            copy(da2_in, da2_old_ref, 1).start()
        natural_rows(wout_ref, out_refs, out_places, inverse_ref)
        for m in range(0, length, tile):
            rows = pl.ds(m, tile)
            if first:
                h = x_ref[rows, :].astype(F32) + dot(o_ref[rows, :], wout_ref[...], NN)
                h_ref[rows, :] = h
                acc_ref[rows, :] = h
            else:
                h = h_ref[rows, :]
                acc_ref[rows, :] = jnp.zeros((tile, width), F32)
            da2_ref[rows, :] = jnp.zeros((tile, width), F32)
            inverse = lax.rsqrt(jnp.mean(h * h, axis=1, keepdims=True) + EPSILON_NORM)
            a2 = (h * inverse * gain).astype(BF)
            a2_ref[rows, :] = a2
            place_rows(a2t_ref, rows, a2, order_ref)
            dyb_ref[rows, :] = (og_ref[rows, :].astype(F32) * factor_ref[rows, :1]).astype(BF)
        if first:
            copy(h_ref, h_out, 0).start()

    for block in range(block_first, block_last + 1):

        @pl.when(step == max(0, block * block_size // chunk - start))
        def _():
            arrived(block)

    def one_chunk():
        natural_rows(w_ref, w_refs, w_places, inverse_ref)
        down = wd_ref[pl.ds(pl.multiple_of((start + step) * chunk, chunk), chunk), :]
        for m in range(0, length, big):
            rows = pl.ds(m, big)
            gate = dot(a2_ref[rows, :], w_ref[:, :chunk], NN)
            up = dot(a2_ref[rows, :], w_ref[:, chunk:], NN)
            dhid = dot(dyb_ref[rows, :], down, NT)
            sig = 1.0 / (1.0 + jnp.exp2(gate * -LOG2E))
            act = gate * sig
            hid_ref[rows, :] = (act * up).astype(BF)
            dgu_ref[rows, :chunk] = (dhid * up * (sig + act * (1.0 - sig))).astype(BF)
            dgu_ref[rows, chunk:] = (dhid * act).astype(BF)
        for m in range(0, length, big):
            rows = pl.ds(m, big)
            acc_ref[rows, :] += dot(hid_ref[rows, :], down, NN)
            da2_ref[rows, :] += dot(dgu_ref[rows, :], w_ref[...], NT)
        if first:

            @pl.when(step == steps - 1)
            def _():
                copy(acc_ref, acc_out, 1).start()
                copy(da2_ref, da2_out, 2).start()

        gd_ref[...] = dot(hid_ref[...], dyb_ref[...], TN).astype(BF)
        own_ref[...] = dot(a2t_ref[:side, :], dgu_ref[...], NN).astype(BF)
        send_ref[...] = dot(a2t_ref[side:, :], dgu_ref[...], NN).astype(BF)

    if first:
        one_chunk()

        @pl.when(step == steps - 1)
        def _():
            copy(h_ref, h_out, 0).wait()
            copy(acc_ref, acc_out, 1).wait()
            copy(da2_ref, da2_out, 2).wait()

        return
    tail = steps - 2
    pl.when(step < tail)(one_chunk)

    @pl.when(step == tail)
    def _():
        copy(acc_in, acc_old_ref, 0).wait()
        copy(da2_in, da2_old_ref, 1).wait()
        total = jnp.zeros((1, width), F32)
        for m in range(0, length, tile):
            rows = pl.ds(m, tile)
            mixed_ref[rows, :] = (acc_old_ref[rows, :] + acc_ref[rows, :]).astype(BF)
            h = h_ref[rows, :]
            inverse = lax.rsqrt(jnp.mean(h * h, axis=1, keepdims=True) + EPSILON_NORM)
            hat = h * inverse
            da2 = da2_old_ref[rows, :] + da2_ref[rows, :]
            total = total + jnp.sum(da2 * hat, axis=0, keepdims=True)
            scaled = da2 * gain
            dy = og_ref[rows, :].astype(F32) * factor_ref[rows, :1]
            dh = dy + inverse * (scaled - hat * jnp.mean(scaled * hat, axis=1, keepdims=True))
            acc_ref[rows, :] = dh
            low = dh.astype(BF)
            dyb_ref[rows, :] = low
            do_ref[rows, :] = dot(low, wout_ref[...], NT).astype(BF)
            place_rows(a2t_ref, rows, o_ref[rows, :], order_ref)
        dgain_ref[...] = total
        copy(mixed_ref, mixed_out, 2).start()
        copy(acc_ref, dh_out, 3).start()
        copy(do_ref, do_out, 4).start()

    for tile_number in range(2):

        @pl.when(step == tail + tile_number)
        def _():
            half = width // 2
            grads = dyb_ref[:, tile_number * half : (tile_number + 1) * half]
            own_ref[...] = dot(a2t_ref[:side, :], grads, NN).astype(BF)
            send_ref[...] = dot(a2t_ref[side:, :], grads, NN).astype(BF)

    @pl.when(step == steps - 1)
    def _():
        copy(mixed_ref, mixed_out, 2).wait()
        copy(acc_ref, dh_out, 3).wait()
        copy(do_ref, do_out, 4).wait()


def feed_forward(order, inverse, start, count, skip, state, x, o, out_grad, factor, gain, out_pieces, pieces, down_pieces):
    length, width = out_grad.shape
    chunk = CHUNK
    first = state is None
    steps = count if first else count + 2
    last = count - 1
    rows = pl.BlockSpec((chunk, width), lambda i, *_: (start + jnp.minimum(i, last), 0))
    columns = pl.BlockSpec((width // 2, TILE), lambda i, *_: (0, i))
    whole = lambda *s: pl.BlockSpec(s, lambda i, *_: (0,) * len(s), pipeline_mode=pl.Buffered(1))
    anywhere = pl.BlockSpec(memory_space=pl.ANY)
    shape = jax.ShapeDtypeStruct
    (outs, out_places), (tiles, w_places), (downs, d_places) = out_pieces, pieces, down_pieces
    big = whole(length, width)
    full, low = pltpu.VMEM((length, width), F32), pltpu.VMEM((length, width), BF)
    scratch = [
        pltpu.VMEM((width, width), BF),
        pltpu.VMEM((width, TILE), BF),
        pltpu.VMEM((FF, width), BF),
        low,
        pltpu.VMEM((width, length), BF),
        low,
        pltpu.VMEM((length, chunk), BF),
        pltpu.VMEM((length, TILE), BF),
        pltpu.SemaphoreType.DMA((inverse.shape[0], 2)),
        pltpu.SemaphoreType.DMA((5,)),
    ]
    in_specs = [whole(*piece.shape[:2], width) for piece in outs]
    in_specs += [
        pl.BlockSpec((*piece.shape[:2], TILE), lambda i, *_: (0, 0, skip + jnp.minimum(i, last))) for piece in tiles
    ]
    in_specs += [anywhere] * len(downs)
    in_specs += [big, whole(length, LANES), whole(1, width), big]
    operands = [*outs, *tiles, *downs, out_grad, factor, gain, o]
    halves_out = [shape((width // 2, steps * TILE), BF)] * 2
    aliases = {}
    if first:
        in_specs += [big]
        operands += [x]
        out_specs = [anywhere, anywhere, anywhere, columns, columns, rows]
        out_shape = [shape((length, width), F32)] * 3 + halves_out + [shape((FF, width), BF)]
        scratch = [full, full, full] + scratch
    else:
        in_specs += [big, anywhere, anywhere, anywhere]
        operands += list(state)
        out_specs = [anywhere, anywhere, anywhere, columns, columns, rows, whole(1, width)]
        out_shape = [shape((length, width), BF), shape((length, width), F32), shape((length, width), BF)]
        out_shape += halves_out + [shape((FF, width), BF), shape((1, width), F32)]
        scratch = [full, full, full, full, low, low] + scratch
        aliases = {len(operands) + 1: 5}
    return pl.pallas_call(
        functools.partial(feed_forward_kernel, first, start, count, (out_places, w_places, d_places)),
        grid_spec=pltpu.PrefetchScalarGridSpec(
            num_scalar_prefetch=2, grid=(steps,), in_specs=in_specs, out_specs=out_specs, scratch_shapes=scratch
        ),
        out_shape=out_shape,
        input_output_aliases=aliases,
        compiler_params=pltpu.CompilerParams(vmem_limit_bytes=63 * MIB),
        cost_estimate=cost(40),
        name="feed_forward",
    )(order, inverse, *operands)


def unproject_kernel(devices, order_ref, a1_ref, c_ref, dq_ref, dk_ref, dv_ref, wup_ref, *refs):
    dc_ref, own_ref, send_ref = refs[:3]
    a1t_ref = refs[-1]
    head = pl.program_id(0)
    length, width = a1_ref.shape
    half = width // 2
    tile = min(256, length)

    @pl.when(head == 0)
    def _():
        for m in range(0, length, tile):
            place_rows(a1t_ref, pl.ds(m, tile), a1_ref[m : m + tile, :], order_ref)

    dq, dk, dv = dq_ref[...], dk_ref[...], dv_ref[...]
    dc = (dot(dk, wup_ref[:, :GROUP_WIDTH], NT) + dot(dv, wup_ref[:, GROUP_WIDTH:], NT)).astype(BF)
    dc_ref[...] = dc
    grads = [
        (ref, start, size, dot(a1t_ref[rows, :], grad, NN).astype(BF))
        for ref, rows in ((own_ref, slice(half)), (send_ref, slice(half, width)))
        for start, size, grad in ((0, GROUP_WIDTH, dq), (QUERY_WIDTH, LATENT_WIDTH, dc))
    ]
    for which in range(LATENT_HEADS):

        @pl.when(head == which)
        def _():
            for ref, start, size, grad in grads:
                ref[:, start + which * size : start + (which + 1) * size] = grad

    turned = c_ref[...].T
    sides = [dot(turned, grad, NN).astype(BF) for grad in (dk, dv)]
    if not devices:
        refs[3][:, :GROUP_WIDTH], refs[3][:, GROUP_WIDTH:] = sides
        return
    all_ref = refs[3]
    side = QUERY_WIDTH + LATENT_HEADS * LATENT_WIDTH
    rows, ups = width // devices, wup_ref.shape[0] * LATENT_HEADS // devices
    blocks = order_ref.shape[0] // LATENT_HEADS
    line = devices // order_ref.shape[0]
    for block in range(blocks):
        place = order_ref[head * blocks + block]
        for z in range(line):
            device = block * line + z
            for piece, value in enumerate(sides):
                start = pl.multiple_of(place * (line * rows) + (z * rows + piece * ups), ups)
                all_ref[pl.ds(start, ups), :] = value[device * ups : (device + 1) * ups, :]

    @pl.when(head == LATENT_HEADS - 1)
    def _():
        own_ref[:, side:] = all_ref[:half, :]
        send_ref[:, side:] = all_ref[half:, :]


def unproject(devices, order, a1, c, dq, dk, dv, w_up):
    length, width = a1.shape
    latents = LATENT_HEADS * LATENT_WIDTH
    half = width // 2
    columns = lambda rows, size: pl.BlockSpec((rows, size), lambda g, *_: (0, g))
    up = pl.BlockSpec((LATENT_WIDTH, 2 * GROUP_WIDTH), lambda g, *_: (g, 0))
    group = columns(length, GROUP_WIDTH)
    both = QUERY_WIDTH + latents + (TILE if devices else 0)
    outs = [(length, latents)] + [(half, both)] * 2
    out_specs = [columns(length, LATENT_WIDTH)] + [resident(half, both)] * 2
    scratch = [pltpu.VMEM((width, length), BF)]
    if devices:
        scratch = [pltpu.VMEM((width, TILE), BF)] + scratch
    else:
        outs.append(w_up.shape)
        out_specs.append(up)
    return pl.pallas_call(
        functools.partial(unproject_kernel, devices),
        grid_spec=pltpu.PrefetchScalarGridSpec(
            num_scalar_prefetch=1,
            grid=(LATENT_HEADS,),
            in_specs=[resident(length, width), columns(length, LATENT_WIDTH), group, group, group, up],
            out_specs=out_specs,
            scratch_shapes=scratch,
        ),
        out_shape=[jax.ShapeDtypeStruct(s, BF) for s in outs],
        compiler_params=pltpu.CompilerParams(vmem_limit_bytes=60 * MIB),
        cost_estimate=cost(20),
        name="unproject",
    )(order, a1, c, dq, dk, dv, w_up)


def input_grad_kernel(x_ref, dh_ref, dq_ref, dc_ref, gain_ref, win_ref, out_ref, dgain_ref):
    x = x_ref[...].astype(F32)
    inverse = lax.rsqrt(jnp.mean(x * x, axis=1, keepdims=True) + EPSILON_NORM)
    hat = x * inverse
    da1 = dot(dq_ref[...], win_ref[:, :QUERY_WIDTH], NT) + dot(dc_ref[...], win_ref[:, QUERY_WIDTH:], NT)
    part = jnp.sum(da1 * hat, axis=0, keepdims=True)
    scaled = da1 * gain_ref[...].astype(F32)
    out_ref[...] = (
        dh_ref[...] + inverse * (scaled - hat * jnp.mean(scaled * hat, axis=1, keepdims=True))
    ).astype(BF)

    @pl.when(pl.program_id(0) == 0)
    def _():
        dgain_ref[...] = part

    @pl.when(pl.program_id(0) > 0)
    def _():
        dgain_ref[...] += part


def input_grad(x, dh, dql, gain, w_in):
    dq, dc = dql
    length, width = x.shape
    tile = min(256, length)
    rows = lambda columns: pl.BlockSpec((tile, columns), lambda i: (i, 0))
    return pl.pallas_call(
        input_grad_kernel,
        grid=(length // tile,),
        in_specs=[rows(width), rows(width), rows(dq.shape[1]), rows(dc.shape[1]), resident(1, width), resident(*w_in.shape)],
        out_specs=[rows(width), resident(1, width)],
        out_shape=[jax.ShapeDtypeStruct((length, width), BF), jax.ShapeDtypeStruct((1, width), F32)],
        compiler_params=pltpu.CompilerParams(vmem_limit_bytes=60 * MIB),
        cost_estimate=cost(20),
        name="input_grad",
    )(x, dh, dq, dc, gain, w_in)


class Ring:
    def __init__(self, data, line):
        self.cores = 2 if data % 2 == 0 else 1
        self.plane, self.line = data // self.cores, line
        place = lax.axis_index("dp")
        self.core, self.at, self.z = place % self.cores, place // self.cores, lax.axis_index("fsdp")

    def partner(self, index, shift, count):
        if count & (count - 1) == 0:
            return index ^ shift
        return (index + shift) % count

    def send_core(self, value):
        swap = [(i, i ^ 1) for i in range(self.plane * 2)]
        return lax.ppermute(value, "dp", swap)

    def send_plane(self, value, shift):
        pairs = [
            (p * self.cores + c, self.partner(p, shift, self.plane) * self.cores + c)
            for p in range(self.plane)
            for c in range(self.cores)
        ]
        return lax.ppermute(value, "dp", pairs)

    def send_line(self, value, shift):
        return lax.ppermute(value, "fsdp", [(i, (i + shift) % self.line) for i in range(self.line)])


def take(array, index, axis):
    return lax.dynamic_index_in_dim(array, index, axis, keepdims=False)


def core_blocks(ring, grad, core):
    rows = grad.shape[0] // (ring.plane * ring.cores * ring.line)
    return take(grad.reshape(ring.plane, ring.cores, ring.line, rows, grad.shape[1]), core, 1)


def total(parts):
    return sum(part.astype(F32) for part in parts)


def core_sends(ring, value):
    return [(ring.send_core, value)]


def plane_sends(ring, parts, relative):
    spot = lambda shift: shift if relative else ring.partner(ring.at, shift, ring.plane)
    block = lambda shift: total([take(part, spot(shift), 0) for part in parts]).astype(BF)
    sends = [
        (lambda value, shift=shift: ring.send_plane(value, shift), block(shift)) for shift in range(1, ring.plane)
    ]
    return block(0), sends


def cross_sends(ring, parts, bit, left):
    axis = len(left) - 1 - left.index(bit)
    side = (ring.at >> bit) & 1
    kept, give = (total([take(part, which, axis) for part in parts]) for which in (side, 1 - side))
    return kept, [(lambda value: ring.send_plane(value, 1 << bit), give.astype(BF))]


def line_sends(ring, parts, bit, axis=0):
    shape = parts[0].shape
    pairs = [part.reshape(*shape[:axis], shape[axis] // 2, 2, *shape[axis + 1 :]) for part in parts]
    side = (ring.z >> bit) & 1
    swap = [(i, i ^ (1 << bit)) for i in range(ring.line)]
    kept, give = (total([take(pair, which, axis + 1) for pair in pairs]) for which in (side, 1 - side))
    return kept, [(lambda value: lax.ppermute(value, "fsdp", swap), give.astype(BF))]


def beside(sends, kept, kernel=None, *inputs):
    inputs, gives, kept = together(inputs, [give for _, give in sends], kept)
    received = [send(give) for (send, _), give in zip(sends, gives)]
    return together(kernel(*inputs) if kernel else (), received, kept)


def line_rest(ring, grads, done):
    for bit in range(done, ring.line.bit_length() - 1):
        kept, sends = zip(*(line_sends(ring, [grad], bit) for grad in grads))
        _, received, kept = beside([send for one in sends for send in one], kept)
        grads = [total(pair) for pair in zip(kept, received)]
    return [grad[0] for grad in grads]


def halves_order(ring):
    blocks = jnp.arange(ring.plane * ring.cores)
    plane, core = blocks // ring.cores, blocks % ring.cores
    if ring.plane & (ring.plane - 1) == 0:
        shift = plane ^ ring.at
    else:
        shift = (plane - ring.at) % ring.plane
    order = (((core - ring.core) % ring.cores) * ring.plane + shift).astype(jnp.int32)
    shift, core = blocks % ring.plane, blocks // ring.plane
    if ring.plane & (ring.plane - 1) == 0:
        plane = shift ^ ring.at
    else:
        plane = (shift + ring.at) % ring.plane
    inverse = (plane * ring.cores + (core + ring.core) % ring.cores).astype(jnp.int32)
    return order, inverse


class Gather:
    def __init__(self, ring, piece, by_columns=False):
        self.ring, self.by_columns = ring, by_columns
        self.block = piece[None]
        self.bits = list(range(ring.line.bit_length() - 1))[::-1]

    def line_sends(self):
        swap = [(i, i ^ (1 << self.bits[0])) for i in range(self.ring.line)]
        return [(lambda value: lax.ppermute(value, "fsdp", swap), self.block)]

    def line_receive(self, values):
        low = ((self.ring.z >> self.bits.pop(0)) & 1) == 0
        pair = [jnp.where(low, self.block, values[0]), jnp.where(low, values[0], self.block)]
        block = jnp.stack(pair, axis=1)
        self.block = block.reshape(-1, *block.shape[2:])
        if not self.bits:
            self.split()

    def split(self):
        line, rows, columns = self.block.shape
        count = self.ring.plane.bit_length() - 1
        if self.by_columns:
            cut = columns // 2
            halves = [self.block[..., :cut].reshape(1, -1, cut), self.block[..., cut:].reshape(1, -1, cut)]
            self.offsets = [(0, 0), (cut, 0)]
        else:
            whole = self.block.reshape(-1, columns)
            cut = whole.shape[0] // 2
            halves = [whole[None, :cut], whole[None, cut:]]
            self.offsets = [(0, 0), (0, cut)]
        self.halves = [([half], [[0]]) for half in halves]
        self.orders = [list(range(count)), list(range(count))[::-1]]

    def plane_sends(self):
        sends = []
        for (arrays, _), order in zip(self.halves, self.orders):
            value = jnp.concatenate(arrays, axis=0) if len(arrays) > 1 else arrays[0]
            sends.append((lambda value, bit=order[0]: self.ring.send_plane(value, 1 << bit), value))
        return sends

    def plane_receive(self, values):
        for (arrays, shifts), order, value in zip(self.halves, self.orders, values):
            bit = order.pop(0)
            shifts.append([shift ^ (1 << bit) for have in shifts for shift in have])
            arrays.append(value)

    def direct_sends(self):
        self.offsets = [(0, 0)]
        block = self.block.reshape(1, -1, self.block.shape[-1])
        self.halves = [([block], [[0]])]
        return [(lambda value, k=k: self.ring.send_plane(value, k), block) for k in range(1, self.ring.plane)]

    def direct_receive(self, values):
        for shift, value in enumerate(values, 1):
            self.halves[0][0].append(value)
            self.halves[0][1].append([shift])

    def arrays(self):
        return [array for arrays, _ in self.halves for array in arrays]

    def hold(self, arrays):
        arrays = list(arrays)
        for mine, _ in self.halves:
            for number in range(len(mine)):
                mine[number] = arrays.pop(0)

    def places(self, core):
        return [
            (column, [(core * self.ring.plane + shift, row) for shift in have])
            for (_, shifts), (column, row) in zip(self.halves, self.offsets)
            for have in shifts
        ]

    def pieces(self, other):
        if self.ring.cores == 1:
            return self.arrays(), self.places(0)
        return self.arrays() + list(other), self.places(0) + self.places(1)

    def stacked(self):
        blocks = [{}, {}]
        for found, (arrays, shifts) in zip(blocks, self.halves):
            for array, have in zip(arrays, shifts):
                found.update(zip(have, array))
        return jnp.stack([jnp.concatenate([found[k] for found in blocks], axis=0) for k in range(self.ring.plane)])


def natural(ring, mine, other):
    if ring.plane & (ring.plane - 1) == 0:
        shifts = [ring.at ^ at for at in range(ring.plane)]
    else:
        shifts = [(ring.at - at) % ring.plane for at in range(ring.plane)]
    blocks = []
    for shift in shifts:
        pair = [choose(shift, list(part)) for part in (mine, other)][: ring.cores]
        blocks += [choose((core - ring.core) % ring.cores, pair) for core in range(ring.cores)]
    return jnp.stack(blocks)


def choose(index, options):
    result = options[0]
    for number, option in enumerate(options[1:], 1):
        result = jnp.where(index == number, option, result)
    return result


def sum_all(ring, value):
    if ring.cores == 2:
        value = value + ring.send_core(value)
    for count, send in ((ring.plane, ring.send_plane), (ring.line, None)):
        if count & (count - 1):
            return lax.psum(value, AXES)
    shift = 1
    while shift < ring.plane:
        value = value + ring.send_plane(value, shift)
        shift *= 2
    shift = 1
    while shift < ring.line:
        swap = [(i, i ^ shift) for i in range(ring.line)]
        value = value + lax.ppermute(value, "fsdp", swap)
        shift *= 2
    return value


def adamw_kernel(message_ref, dgains_ref, a_ref, b_ref, c_ref, d_ref, *refs):
    masters, firsts, seconds, norm_ref, outs = refs[:6], refs[6:12], refs[12:18], refs[18], refs[19:]
    gains = message_ref[:-8, :]
    norm = jnp.sqrt(message_ref[-1:, :1] + jnp.sum(gains * gains, keepdims=True))
    norm_ref[...] = norm
    clip = jnp.minimum(1.0, MAX_NORM / (norm + 1e-06))

    def update(index, place, grad, rate, decay):
        grad = clip * grad
        master = masters[index][place]
        first_new = BETA_ONE * firsts[index][place] + (1.0 - BETA_ONE) * grad
        second_new = BETA_TWO * seconds[index][place] + (1.0 - BETA_TWO) * grad * grad
        first_hat = first_new / (1.0 - BETA_ONE**STEP)
        second_hat = second_new / (1.0 - BETA_TWO**STEP)
        outs[3 * index][place] = master - rate * (
            first_hat / (jnp.sqrt(second_hat) + EPSILON_ADAM) + decay * master
        )
        outs[3 * index + 1][place] = first_new
        outs[3 * index + 2][place] = second_new

    everything = (slice(None), slice(None))
    side = masters[0].shape[1]
    update(0, everything, c_ref[:, :side], RATE_MATRIX, DECAY_MATRIX)
    rows = masters[1].shape[0]
    for tile in range(masters[1].shape[1] // TILE):
        place = (slice(None), slice(tile * TILE, (tile + 1) * TILE))
        update(1, place, c_ref[tile * rows : (tile + 1) * rows, side:], RATE_MATRIX, DECAY_MATRIX)
    second = FF // CHUNK - FIRST_CHUNKS
    update(2, everything, b_ref[:, second * TILE :], RATE_OUTPUT, DECAY_MATRIX)
    for chunk in range(FF // CHUNK):
        ref, at = (a_ref, chunk) if chunk < FIRST_CHUNKS else (b_ref, chunk - FIRST_CHUNKS)
        for which in range(2):
            place = (slice(None), slice(which * FF + chunk * CHUNK, which * FF + (chunk + 1) * CHUNK))
            start = at * TILE + which * CHUNK
            update(3, place, ref[:, start : start + CHUNK], RATE_MATRIX, DECAY_MATRIX)
    update(4, everything, d_ref[...], RATE_MATRIX, DECAY_MATRIX)
    update(5, everything, dgains_ref[...], RATE_GAIN, 0.0)


def adamw(message, dgains, totals, masters, firsts, seconds):
    shape = jax.ShapeDtypeStruct
    outs = [shape((1, 1), F32)] + [shape(w.shape, F32) for w in masters for _ in range(3)]
    return pl.pallas_call(
        adamw_kernel,
        out_shape=outs,
        compiler_params=pltpu.CompilerParams(vmem_limit_bytes=60 * MIB),
        cost_estimate=cost(5),
        name="adamw",
    )(message, dgains, *totals, *masters, *firsts, *seconds)


def together(*values):
    return lax.optimization_barrier(values)


def shards(data, line, tokens, out_grad, domain_ids, domain_scale, *state):
    masters, moments = state[:6], state[6:]
    firsts, seconds = moments[0::2], moments[1::2]
    ring = Ring(data, line)
    devices = data * line
    length, width = tokens.shape
    p_in, p_up, p_out, p_gate, p_down, p_gains = masters
    latents = LATENT_HEADS * LATENT_WIDTH
    rows = width // devices
    chunks = FF // CHUNK
    columns = lambda a: a.reshape(a.shape[0], -1, TILE).transpose(1, 0, 2).reshape(-1, TILE)

    half = FIRST_CHUNKS
    one = jnp.concatenate([p_in, columns(p_up).reshape(rows, -1), lane_pad(p_gains, rows)], axis=1).astype(BF)
    one = Gather(ring, one)
    order, inverse = halves_order(ring)

    def early(domain_ids, p_out, p_gate, p_down):
        picked = domain_ids[:, None] == jnp.arange(NDOM)[None, :]
        factor = jnp.sum(jnp.where(picked, domain_scale[None, :], 0.0), axis=1, keepdims=True)
        factor = jnp.broadcast_to(factor, (length, LANES))
        tiles = p_gate.astype(BF).reshape(rows, 2, chunks, CHUNK).transpose(0, 2, 1, 3).reshape(rows, -1)
        two = jnp.concatenate([p_out.astype(BF), tiles[:, : half * TILE]], axis=1)
        return rotation_tables(length), factor, two, p_down.astype(BF), tiles[:, half * TILE :]

    out, received, _ = beside(one.line_sends(), (), early, domain_ids, p_out, p_gate, p_down)
    tables, factor, two, down, three = out
    two, down, three = Gather(ring, two), Gather(ring, down, True), Gather(ring, three)
    one.line_receive(received)
    while len(one.bits) > 0:
        one.line_receive(beside(one.line_sends(), ())[1])
    while len(down.bits) > 0 or len(one.orders[0]) > 0:
        sends = one.plane_sends() if len(one.orders[0]) > 0 else []
        split = len(sends)
        sends += down.line_sends() if len(down.bits) > 0 else []
        _, received, kept = beside(sends, one.arrays())
        one.hold(kept)
        if split:
            one.plane_receive(received[:split])
        if len(received) > split:
            down.line_receive(received[split:])
    one_block = one.stacked()
    core_of = lambda keys: [send for h, r in keys for send in core_sends(ring, down.halves[h][0][r])]
    sends = core_sends(ring, one_block) + down.plane_sends() + two.line_sends() + core_of([(0, 0)])
    _, received, (one_block, kept, tokens) = beside(sends, (one_block, down.arrays(), tokens))
    down.hold(kept)
    one_other = received[0]
    down.plane_receive(received[1:-2])
    two.line_receive(received[-2:-1])
    other = {(0, 0): received[-1]}
    while len(down.orders[0]) > 0 or len(two.bits) > 0:
        sends = down.plane_sends() if len(down.orders[0]) > 0 else []
        split = len(sends)
        sends += two.line_sends() if len(two.bits) > 0 else []
        middle = len(sends)
        keys = [(1, 0), (0, 1)] if len(other) == 1 else []
        _, received, kept = beside(sends + core_of(keys), down.arrays())
        down.hold(kept)
        other.update(zip(keys, received[middle:]))
        if split:
            down.plane_receive(received[:split])
        if middle > split:
            two.line_receive(received[split:middle])
    aligned = rows % 32 == 0 and p_up.shape[0] % 16 == 0
    if aligned:
        run = lambda tokens: project(devices, inverse, tokens, tables, one_block, one_other)
    else:
        first = natural(ring, one_block, one_other).reshape(devices, rows, -1)
        w_in = first[:, :, : p_in.shape[1]].reshape(width, -1)
        w_up = first[:, :, p_in.shape[1] : p_in.shape[1] + p_up.size // rows]
        w_up = w_up.reshape(devices, 2 * GROUP_WIDTH // TILE, p_up.shape[0], TILE).transpose(0, 2, 1, 3).reshape(latents, -1)
        gains = first[:, :2, -LANES:][:, :, : p_gains.shape[1]].transpose(1, 0, 2).reshape(2, width).astype(F32)
        run = lambda tokens: (*project(0, inverse, tokens, tables, w_in, w_up, gains), w_in, w_up, gains)
    rounds = len(down.halves[0][0])
    rest = [(h, r) for r in range(rounds) for h in range(2) if (h, r) not in other]
    sends = two.plane_sends() + three.line_sends()
    split = len(sends)
    out, received, kept = beside(sends + core_of(rest[:2]), (two.arrays(), down.arrays(), other), run, tokens)
    a1, q, k, v, c, w_in, w_up, gains = out
    two.hold(kept[0])
    down.hold(kept[1])
    other = dict(kept[2])
    two.plane_receive(received[:2])
    three.line_receive(received[2:3])
    other.update(zip(rest[:2], received[split:]))
    sends = two.plane_sends() if len(two.orders[0]) > 0 else []
    split = len(sends)
    sends += three.line_sends() if len(three.bits) > 0 else []
    middle = len(sends)
    sends += core_of(rest[2:3]) + core_sends(ring, two.halves[0][0][0])
    (o, logs), received, kept = beside(sends, (two.arrays(), down.arrays(), other), attention, q, k, v)
    two.hold(kept[0])
    down.hold(kept[1])
    other = dict(kept[2])
    if split:
        two.plane_receive(received[:split])
    if middle > split:
        three.line_receive(received[split:middle])
    other.update(zip(rest[2:3], received[middle:-1]))
    two_other = [received[-1]]
    while len(two.orders[0]) > 0:
        two.plane_receive(beside(two.plane_sends(), ())[1])
    while len(three.bits) > 0:
        three.line_receive(beside(three.line_sends(), ())[1])
    sends = core_of(rest[3:])
    split = len(sends)
    sends += [send for array in two.arrays()[1:] for send in core_sends(ring, array)]
    kept = (o, two.arrays(), down.arrays(), other, two_other)
    _, received, (o, kept, kept_down, other, two_other) = beside(sends, kept)
    two.hold(kept)
    down.hold(kept_down)
    other = dict(other)
    other.update(zip(rest[3:], received[:split]))
    down_pieces = down.pieces([other[h, r] for h in range(2) for r in range(rounds)])
    two_pieces = two.pieces(list(two_other) + list(received[split:]))
    common = (tokens, o, out_grad, factor, gains[1:], two_pieces)
    run = lambda o: feed_forward(
        order, inverse, 0, half, width // TILE, None, tokens, o, out_grad, factor, gains[1:], two_pieces, two_pieces, down_pieces
    )
    sends = three.direct_sends()
    split = len(sends)
    sends += core_sends(ring, three.arrays()[0])
    (h, acc, da2, own_a, send_a, g_down), received, kept = beside(sends, three.arrays(), run, o)
    three.hold(kept)
    three.direct_receive(received[:split])
    other = list(received[split:])
    blocks = lambda a: a.reshape(ring.plane, ring.line, rows, -1)
    sends = core_sends(ring, blocks(send_a)) + [send for array in three.arrays()[1:] for send in core_sends(ring, array)]
    _, received, (h, own_a, kept, other) = beside(sends, (h, own_a, three.arrays(), other))
    three.hold(kept)
    three_pieces = three.pieces(list(other) + list(received[1:]))
    kept_a, sends = plane_sends(ring, [blocks(own_a), received[0]], True)
    state = (acc, da2, g_down)
    run = lambda h: feed_forward(
        order, inverse, half, chunks - half, 0, (h, *state), *common, three_pieces, down_pieces
    )
    out, received, kept_a = beside(sends, kept_a, run, h)
    mixed, dh, do, own_b, send_b, g_down, dgain_two = out

    def run(g_down, kept_a, *came_a):
        kept_a, send_a = line_sends(ring, [kept_a, *came_a], 0)
        return core_blocks(ring, g_down, 1 - ring.core), kept_a, send_a[0][1]

    out, came_b, (do, own_b) = beside(core_sends(ring, blocks(send_b)), (do, own_b), run, g_down, kept_a, *received)
    send_d, kept_a, give_a = out
    kept_b, send_b = plane_sends(ring, [blocks(own_b), *came_b], True)
    sends = send_b + core_sends(ring, send_d) + [(line_sends(ring, [give_a], 0)[1][0][0], give_a)]
    run = lambda do: attention_back(40, 0, PAIRS, q, k, v, o, do, logs, tables)
    grads, received, (kept_a, kept_b, g_down) = beside(sends, (kept_a, kept_b, g_down), run, do)
    *came_b, came_d, came_a = received
    bits = list(range(ring.plane.bit_length() - 1))
    orders, left = (bits, bits[::-1]), [bits[:], bits[:]]
    halves_d = zip(*(jnp.split(part, 2, axis=-1) for part in (core_blocks(ring, g_down, ring.core), came_d)))
    halves_d = [[part.reshape(*(2,) * len(bits), *part.shape[1:]) for part in pair] for pair in halves_d]

    def step_d(number, halves_d):
        kept, sends = zip(*(cross_sends(ring, half, order[number], have) for half, order, have in zip(halves_d, orders, left)))
        for order, have in zip(orders, left):
            have.remove(order[number])
        return kept, [send for one in sends for send in one]

    kept_d, send_d = step_d(0, halves_d)
    kept_a, send_a = line_sends(ring, [kept_a, came_a], 1)

    def run(dq, dk, dv):
        dc, own, send, *ups = unproject(devices if aligned else 0, order, a1, c, dq, dk, dv, w_up)
        if not aligned:
            g_up = ups[0].reshape(devices, -1, 2 * GROUP_WIDTH // TILE, TILE).transpose(0, 2, 1, 3).reshape(width, -1)
            spots = lambda core: [
                take(core_blocks(ring, g_up, core), ring.partner(ring.at, k, ring.plane), 0) for k in range(ring.plane)
            ]
            ups = [jnp.stack(spots(core)).reshape(width // 2, -1) for core in (ring.core, 1 - ring.core)]
            own, send = (jnp.concatenate(parts, axis=1) for parts in zip((own, send), ups))
        dql = (dq, dc)
        return dql, own, send

    kept_b, send_b = line_sends(ring, [kept_b, *came_b], 0)
    kept = (kept_a, kept_b, kept_d)
    out, received, (kept_a, kept_b, kept_d) = beside(send_d + send_a + send_b, kept, run, *grads)
    dql, own_c, send_c = out
    *came_d, came_a, came_b = received

    def second(kept_d, came_d):
        kept_d, send_d = step_d(1, list(zip(kept_d, came_d)))
        return kept_d, [give for _, give in send_d]

    send_d = [(lambda value, bit=order[1]: ring.send_plane(value, 1 << bit)) for order in orders]
    kept = (dql, own_c, kept_a, came_a, kept_b, came_b)
    (kept_d, give_d), came_c, kept = beside(core_sends(ring, blocks(send_c)), kept, second, kept_d, came_d)
    dql, own_c, kept_a, came_a, kept_b, came_b = kept
    run = lambda own_c, *came_c: plane_sends(ring, [blocks(own_c), *came_c], True)[0:1] + tuple(
        give for _, give in plane_sends(ring, [blocks(own_c), *came_c], True)[1]
    )
    kept = (dql, kept_a, came_a, kept_b, came_b, kept_d)
    (kept_c, *gives_c), came_d, kept = beside(list(zip(send_d, give_d)), kept, run, own_c, *came_c)
    dql, kept_a, came_a, kept_b, came_b, kept_d = kept
    send_c = [(lambda value, k=k: ring.send_plane(value, k), give) for k, give in enumerate(gives_c, 1)]
    for number in range(2, len(bits)):
        kept_d, send_d = step_d(number, list(zip(kept_d, came_d)))
        _, came_d, kept_d = beside(send_d, kept_d)
    sum_d = jnp.concatenate([total(pair) for pair in zip(kept_d, came_d)], axis=-1)
    kept_a = total([kept_a, came_a])
    kept_b, send_b = line_sends(ring, [kept_b, came_b], 1)
    kept_d, send_d = line_sends(ring, [sum_d], 0)
    run = lambda dql: input_grad(tokens, dh, dql, gains[:1], w_in)
    kept = (kept_b, kept_c, kept_d)
    (given, dgain_one), received, (kept_b, kept_c, kept_d) = beside(send_c + send_d + send_b, kept, run, dql)
    *came_c, came_d, came_b = received
    kept_b = total([kept_b, came_b])
    kept_c, send_c = line_sends(ring, [kept_c, *came_c], 0)
    kept_d, send_d = line_sends(ring, [kept_d, came_d], 1)
    _, received, (kept_c, kept_d) = beside(send_c + send_d, (kept_c, kept_d))
    came_c, came_d = received
    sums = [kept_a, kept_b, total([kept_d, came_d])]
    total_a, total_b, total_d = line_rest(ring, sums, 2)
    (total_c,) = line_rest(ring, [total([kept_c, came_c])], 1)

    squares = sum(jnp.sum(grad * grad) for grad in (total_a, total_b, total_c, total_d))
    dgains = jnp.concatenate([dgain_one, dgain_two], axis=0)
    message = jnp.concatenate(
        [dgains.reshape(-1, LANES), jnp.full((8, LANES), squares, F32)], axis=0
    )
    message = sum_all(ring, message)
    share = masters[5].shape[1]
    place = lax.axis_index("dp") * line + lax.axis_index("fsdp")
    dgains = lax.dynamic_slice_in_dim(message[:-8].reshape(2, width), place * share, share, 1)
    totals = (total_a, total_b, total_c, total_d)
    grad_norm, *results = adamw(message, dgains, totals, masters, firsts, seconds)
    return (mixed, given, grad_norm[0, 0], *results)


def lane_pad(gains, rows):
    return jnp.pad(gains, ((0, rows - gains.shape[0]), (0, LANES - gains.shape[1])))


def solution(mesh):
    data, line = mesh.shape["dp"], mesh.shape["fsdp"]
    rows, flat, columns = P(AXES, None), P(AXES), P(None, AXES)

    def run(*arrays):
        return shards(data, line, *arrays)

    return jax.shard_map(
        run,
        mesh=mesh,
        in_specs=(rows, rows, flat, P()) + (rows,) * 5 + (columns,) + (rows,) * 10 + (columns,) * 2,
        out_specs=(rows, rows, P()) + (rows,) * 15 + (columns,) * 3,
        check_vma=False,
    )
```
